32 devices in a mesh: dp: 16 (over z, y, core), seg: 2 (over x).
Axes of the slice: x: 2, y: 2, z: 4, core: 2. Of those that a mesh axis runs over, the one named last changes fastest.
Arguments:
- activations: bfloat16 [32, 1044, 768], P('dp', 'seg'), may hold values from -6 to 6
- tok_count: int32 [32, 2], P('dp', 'seg'), may hold values from 0 to 502, as said below
- w_query: bfloat16 [768, 768], replicated, may hold values from -0.21875 to 0.21875
- w_key: bfloat16 [768, 768], replicated, may hold values from -0.21875 to 0.21875
- w_value: bfloat16 [768, 768], replicated, may hold values from -0.21875 to 0.21875
- w_proj: bfloat16 [768, 768], replicated, may hold values from -1.75 to 1.75
- b_query: float32 [768], replicated, may hold values from -3 to 3
- b_value: float32 [768], replicated, may hold values from -3 to 3
- b_proj: float32 [768], replicated, may hold values from -3 to 3
- gain_attn: float32 [768], replicated, may hold values from 0.5 to 1.5
- shift_attn: float32 [768], replicated, may hold values from -2 to 2
- w_up: bfloat16 [768, 3072], P(None, 'seg'), may hold values from -0.21875 to 0.21875
- b_up: float32 [3072], P('seg'), may hold values from -3 to 3
- w_down: bfloat16 [3072, 768], P('seg'), may hold values from -0.21875 to 0.21875
- b_down: float32 [768], replicated, may hold values from -3 to 3
- gain_ffn: float32 [768], replicated, may hold values from 0.5 to 1.5
- shift_ffn: float32 [768], replicated, may hold values from -2 to 2
- cotangent: bfloat16 [32, 1044, 768], P('dp', 'seg'), may hold values from -6 to 6
Outputs:
- layer_out: bfloat16 [32, 1044, 768], P('dp', 'seg')
- grad_input: float32 [32, 1044, 768], P('dp', 'seg')
- grad_w_query: float32 [768, 768], replicated
- grad_w_key: float32 [768, 768], replicated
- grad_w_value: float32 [768, 768], replicated
- grad_w_proj: float32 [768, 768], replicated
- grad_b_query: float32 [768], replicated
- grad_b_value: float32 [768], replicated
- grad_b_proj: float32 [768], replicated
- grad_gain_attn: float32 [768], replicated
- grad_shift_attn: float32 [768], replicated
- grad_w_up: float32 [768, 3072], P(None, 'seg')
- grad_b_up: float32 [3072], P('seg')
- grad_w_down: float32 [3072, 768], P('seg')
- grad_b_down: float32 [768], replicated
- grad_gain_ffn: float32 [768], replicated
- grad_shift_ffn: float32 [768], replicated
The draws below stay inside these ranges and needn't reach their ends.
Inputs may be any that keep to these rules, and one draw needn't show every extreme that they name: tok_count of an empty item slot is 0 in all its segments; item slot i belongs to group i // 2, whose live slots come first and number at least one; some group has all 2 slots live and some other group has one; a live segment holds 251 to 502 tokens, and some segment holds exactly 502.
All inputs are finite; a program needn't handle non-finite values.
Results may differ from the reference program's by a relative error of at most 0.019.
Values may be sent and summed in bfloat16 or wider, within the bound.
No kernel may reach another device: no remote copies, remote signals or barrier semaphores. Data moves between devices by JAX's collectives and lax.ppermute only.
A program may use at most 256 MiB of HBM per device.

```python
import math
import jax
import jax.numpy as jnp
from jax import lax

D = 768
FF = 3072
HEADS = 12
HEAD = 64
MEM = 10
SEG_TOK = 502
SLOTS = 2
ROWS = 522
SEGS = 2
SLOTS_ALL = 32


def draw_tok_count(key, part):
    key = jax.random.fold_in(key, 7)
    groups = SLOTS_ALL // SLOTS
    keys = jax.random.split(key, 5)
    live_count = jax.random.randint(keys[0], (groups,), 1, SLOTS + 1)
    full_group = jax.random.randint(keys[1], (), 0, groups)
    single_group = (full_group + jax.random.randint(keys[2], (), 1, groups)) % groups
    group_ids = jnp.arange(groups)
    live_count = jnp.where(group_ids == full_group, SLOTS, jnp.where(group_ids == single_group, 1, live_count))
    slot_live = (jnp.arange(SLOTS)[None, :] < live_count[:, None]).reshape(SLOTS_ALL, 1)
    lengths = jax.random.randint(keys[3], (SLOTS_ALL, SEGS), SEG_TOK // 2, SEG_TOK + 1)
    seg_pick = jax.random.randint(keys[4], (), 0, SEGS)
    lengths = lengths.at[full_group * SLOTS, seg_pick].set(SEG_TOK)
    return jnp.where(slot_live, lengths, 0).astype(jnp.int32)


def steps_of(own_key, dims, pieces, smallest, top_value):
    gain = 1.0
    for axis_at, blocks in pieces:
        steps = jax.random.uniform(jax.random.fold_in(jax.random.fold_in(own_key, 6), axis_at), (blocks,), jnp.float32, smallest / len(pieces), top_value / len(pieces))
        gain = gain * jnp.repeat(jnp.exp(steps), dims[axis_at] // blocks).reshape((-1,) + (1,) * (len(dims) - 1 - axis_at))
    return gain


def normal_values(rng, extent, scale, bound, cuts=(), held_as=jnp.bfloat16):
    array = jax.random.normal(rng, extent, jnp.float32) * scale
    if len(cuts) > 0:
        array = steps_of(rng, extent, cuts, -0.22, 0.18) * array
    return jnp.clip(array, min=-bound, max=bound).astype(held_as)


def setup_inputs(seed: int = 0) -> dict:
    splits = jax.random.split(jax.random.key(seed), 19)
    activations = normal_values(splits[0], (SLOTS_ALL, SEGS * ROWS, D), 1.0, 6.0, ((0, 16), (1, 2)))
    tok_count = draw_tok_count(jax.random.fold_in(splits[18], 71), 0)
    w_query = normal_values(splits[2], (D, D), D ** -0.5, 0.21875)
    w_key = normal_values(splits[3], (D, D), D ** -0.5, 0.21875)
    w_value = normal_values(splits[4], (D, D), D ** -0.5, 0.21875)
    w_proj = normal_values(splits[5], (D, D), (D // 64) ** -0.5, 1.75)
    b_query = normal_values(splits[6], (D,), 0.5, 3.0, (), jnp.float32)
    b_value = normal_values(splits[7], (D,), 0.5, 3.0, (), jnp.float32)
    b_proj = normal_values(splits[8], (D,), 0.5, 3.0, (), jnp.float32)
    gain_attn = jnp.clip(1.0 + 0.1 * jax.random.normal(splits[9], (D,), jnp.float32), 0.5, 1.5)
    shift_attn = normal_values(splits[10], (D,), 0.3, 2.0, (), jnp.float32)
    w_up = normal_values(splits[11], (D, FF), D ** -0.5, 0.21875, ((1, 2),))
    b_up = normal_values(splits[12], (FF,), 0.5, 3.0, ((0, 2),), jnp.float32)
    w_down = normal_values(splits[13], (FF, D), (FF // 4) ** -0.5, 0.21875, ((0, 2),))
    b_down = normal_values(splits[14], (D,), 0.5, 3.0, (), jnp.float32)
    gain_ffn = jnp.clip(1.0 + 0.1 * jax.random.normal(splits[15], (D,), jnp.float32), 0.5, 1.5)
    shift_ffn = normal_values(splits[16], (D,), 0.3, 2.0, (), jnp.float32)
    cotangent = normal_values(splits[17], (SLOTS_ALL, SEGS * ROWS, D), 1.0, 6.0, ((0, 16), (1, 2)))
    return dict(activations=activations, tok_count=tok_count, w_query=w_query, w_key=w_key, w_value=w_value, w_proj=w_proj, b_query=b_query, b_value=b_value, b_proj=b_proj, gain_attn=gain_attn, shift_attn=shift_attn, w_up=w_up, b_up=b_up, w_down=w_down, b_down=b_down, gain_ffn=gain_ffn, shift_ffn=shift_ffn, cotangent=cotangent)


@jax.custom_vjp
def low(v):
    return lax.optimization_barrier(v.astype(jnp.bfloat16)).astype(jnp.float32)

@jax.custom_vjp
def low_back(v):
    return v

def low_keep(v):
    return (low(v), None)

def low_pass(kept, grad):
    return (grad,)

def back_keep(v):
    return (v, None)

def back_low(kept, grad):
    return (low(grad),)
low.defvjp(low_keep, low_pass)
low_back.defvjp(back_keep, back_low)
EPSILON = 1e-05
NEG_BIG = -1e+30

def highest(left_mat, right_mat):
    return jnp.dot(left_mat, right_mat, precision=lax.Precision.HIGHEST)

def layer_norm(values, norm_gain, norm_shift):
    center = values - lax.optimization_barrier(jnp.mean(values, -1, keepdims=True))
    spread = lax.optimization_barrier(jnp.mean(center * center, -1, keepdims=True))
    return center * lax.rsqrt(spread + EPSILON) * norm_gain + norm_shift

def attend(segment, key_keep, attn_weights):
    w_query, w_key, w_value, w_proj, b_query, b_value = attn_weights
    head_scale = 1.0 / math.sqrt(HEAD)
    query_rows = low(low_back((highest(segment, w_query) + b_query) * head_scale)).reshape(ROWS, HEADS, HEAD)
    key_rows = low(low_back(highest(segment, w_key))).reshape(ROWS, HEADS, HEAD)
    value_rows = low(low_back(highest(segment, w_value) + b_value)).reshape(ROWS, HEADS, HEAD)
    scores = low_back(jnp.einsum('qhd,khd->hqk', query_rows, key_rows, precision=lax.Precision.HIGHEST))
    scores = jnp.where(key_keep[None, None, :], scores, NEG_BIG)
    row_max = lax.optimization_barrier(jnp.max(scores, -1, keepdims=True))
    exp_scores = jnp.exp(scores - row_max)
    attn_probs = low(exp_scores / lax.optimization_barrier(jnp.sum(exp_scores, -1, keepdims=True)))
    context = jnp.einsum('hqk,khd->qhd', attn_probs, value_rows, precision=lax.Precision.HIGHEST).reshape(ROWS, D)
    context = low(low_back(context))
    return low_back(highest(context, w_proj))

def forward(activations, weights, key_keep, row_keep):
    w_query, w_key, w_value, w_proj, b_query, b_value, b_proj, gain_attn, shift_attn, w_up, b_up, w_down, b_down, gain_ffn, shift_ffn = weights
    attn_weights = (w_query, w_key, w_value, w_proj, b_query, b_value)

    def one_item(inputs):
        item_rows, item_keep, item_mask = inputs
        segments = item_rows.reshape(SEGS, ROWS, D)
        branch = lax.map(lambda pair_in: attend(pair_in[0], pair_in[1], attn_weights), (segments, item_keep))
        pre_norm = segments + branch + b_proj
        normed = low(layer_norm(pre_norm, gain_attn, shift_attn)).reshape(SEGS * ROWS, D)
        hidden_pre = low_back(highest(normed, w_up) + b_up)
        hidden_act = low(jax.nn.gelu(hidden_pre, approximate=False))
        summed = normed + low_back(highest(hidden_act, w_down)) + b_down
        return layer_norm(summed, gain_ffn, shift_ffn) * item_mask
    return lax.map(jax.checkpoint(one_item), (activations, key_keep, row_keep))

def reference(activations, tok_count, w_query, w_key, w_value, w_proj, b_query, b_value, b_proj, gain_attn, shift_attn, w_up, b_up, w_down, b_down, gain_ffn, shift_ffn, cotangent):
    position = jnp.arange(ROWS).astype(jnp.int32)
    counts = tok_count.astype(jnp.int32)
    key_keep = (position[None, None, :] < MEM + counts[:, :, None]) | (position[None, None, :] >= MEM + SEG_TOK)
    live_rows = counts[:, :, None] > 0
    row_keep = (key_keep & live_rows).astype(jnp.float32).reshape(SLOTS_ALL, SEGS * ROWS, 1)
    weights = tuple((weight.astype(jnp.float32) for weight in (w_query, w_key, w_value, w_proj, b_query, b_value, b_proj, gain_attn, shift_attn, w_up, b_up, w_down, b_down, gain_ffn, shift_ffn)))

    def run(rows_in, *weight_list):
        return forward(rows_in, weight_list, key_keep, row_keep)
    layer_out, pull = jax.vjp(run, activations.astype(jnp.float32), *weights)
    grads = pull(cotangent.astype(jnp.float32))
    return (layer_out.astype(jnp.bfloat16), grads[0], grads[1], grads[2], grads[3], grads[4], grads[5], grads[6], grads[7], grads[8], grads[9], grads[10], grads[11], grads[12], grads[13], grads[14], grads[15])
```

```python
import functools
import math

import jax
import jax.numpy as jnp
from jax import lax
from jax.experimental import pallas as pl
from jax.experimental.pallas import tpu as pltpu
from jax.sharding import PartitionSpec as P

HEAD = 64
MEM = 10
EPSILON = 1e-05
NEG_BIG = -1e30
PAIR = 2 * HEAD
BF = jnp.bfloat16
F32 = jnp.float32
VMEM_MIB = 28
JOINT = ("dp", "seg")


def nn(left, right):
    return jnp.dot(left, right, preferred_element_type=F32)


def tn(left, right):
    return lax.dot_general(left, right, (((0,), (0,)), ((), ())), preferred_element_type=F32)


def nt(left, right):
    return lax.dot_general(left, right, (((1,), (1,)), ((), ())), preferred_element_type=F32)


def colsum(values):
    return jnp.sum(values, 0, keepdims=True)


def rowmean(values):
    return jnp.mean(values, -1, keepdims=True)


def kernel_call(kernel, micros, operands, grid, in_specs, out_specs, out_shape, after=(), pick=None, scratch_shapes=(), aliases=None, vmem=VMEM_MIB):
    chosen = 0 if pick is None else 1
    many = chosen + len(operands)

    def run(*refs):
        kernel(*refs[:many], *refs[many + len(after) :])

    in_specs = list(in_specs) + [pl.BlockSpec(memory_space=pl.ANY)] * len(after)
    return pl.pallas_call(
        run,
        grid_spec=pltpu.PrefetchScalarGridSpec(
            num_scalar_prefetch=chosen,
            grid=grid,
            in_specs=in_specs,
            out_specs=out_specs,
            scratch_shapes=scratch_shapes,
        ),
        out_shape=out_shape,
        input_output_aliases=aliases or {},
        compiler_params=pltpu.CompilerParams(vmem_limit_bytes=vmem * 2**20),
        cost_estimate=pl.CostEstimate(
            flops=int(micros * 1.0e9), bytes_accessed=1 << 20, transcendentals=0
        ),
    )(*([pick] if chosen else []), *operands, *after)


def whole(shape):
    return pl.BlockSpec(shape, lambda *_: (0,) * len(shape))


def smem():
    return pl.BlockSpec(memory_space=pltpu.SMEM)


def shape_of(shape, dtype):
    return jax.ShapeDtypeStruct(shape, dtype)


def key_bias(count, rows, padded):
    row = lax.broadcasted_iota(jnp.int32, (padded, PAIR), 0)
    valid = ((row < MEM + count) | (row >= rows - MEM)) & (row < rows)
    return jnp.where(valid, 0.0, NEG_BIG).astype(BF)


def attend_kernel(
    rows,
    slot,
    count_ref,
    x_ref,
    wq_ref,
    wk_ref,
    wv_ref,
    wp_ref,
    bq_ref,
    bv_ref,
    bp_ref,
    gain_ref,
    shift_ref,
    q_ref,
    aux_ref,
    k_ref,
    v_ref,
    ctx_ref,
    normed_ref,
    xhat_ref,
    rstd_ref,
):
    padded, width = x_ref.shape[1:]
    row = lax.broadcasted_iota(jnp.int32, (padded, width), 0)
    x = jnp.where(row < rows, x_ref[0], jnp.zeros((), BF))
    q_ref[0] = ((nn(x, wq_ref[...]) + bq_ref[...]) * (1.0 / math.sqrt(HEAD))).astype(BF)
    k_ref[0] = nn(x, wk_ref[...]).astype(BF)
    v_ref[0] = (nn(x, wv_ref[...]) + bv_ref[...]).astype(BF)
    lane = lax.broadcasted_iota(jnp.int32, (padded, PAIR), 1)
    bias = key_bias(count_ref[slot], rows, padded)
    one = jnp.ones((), BF)
    zero = jnp.zeros((), BF)
    for pair in range(width // PAIR):
        lanes = slice(pair * PAIR, (pair + 1) * PAIR)
        q, k, v = q_ref[0, :, lanes], k_ref[0, :, lanes], v_ref[0, :, lanes]
        contexts, extras = [], []
        for head in range(2):
            own = (lane < HEAD) if head == 0 else (lane >= HEAD)
            aux = HEAD if head == 0 else 0
            at_aux = jnp.where(lane == aux, one, zero)
            scores = nt(
                jnp.where(own, q, at_aux),
                jnp.where(own, k, jnp.where(lane == aux, bias, zero)),
            )
            top = jnp.max(scores, -1, keepdims=True)
            exps = jnp.exp(scores - top).astype(BF)
            weighted = nn(exps, jnp.where(own, v, at_aux))
            total = weighted[:, aux : aux + 1]
            contexts.append(weighted * (1.0 / total))
            rest = -(top + jnp.log(total))
            high = rest.astype(BF)
            rest = rest - high.astype(F32)
            middle = rest.astype(BF)
            low = (rest - middle.astype(F32)).astype(BF)
            extras.append(
                jnp.where(
                    lane == aux + 1,
                    high,
                    jnp.where(lane == aux + 2, middle, jnp.where(lane == aux + 3, low, at_aux)),
                )
            )
        ctx_ref[0, :, lanes] = jnp.where(lane < HEAD, contexts[0], contexts[1]).astype(BF)
        aux_ref[0, :, lanes] = jnp.where(lane < HEAD, extras[1], extras[0])
    pre_norm = x.astype(F32) + nn(ctx_ref[0], wp_ref[...]) + bp_ref[...]
    center = pre_norm - rowmean(pre_norm)
    rstd = lax.rsqrt(rowmean(center * center) + EPSILON)
    xhat = center * rstd
    normed_ref[0] = (xhat * gain_ref[...] + shift_ref[...]).astype(BF)
    xhat_ref[0] = xhat.astype(BF)
    rstd_ref[0] = rstd


def attend(rows, padded, slot, count, x, weights, vectors, before, after):
    slots, _, width = x.shape
    block = pl.BlockSpec((1, padded, width), lambda _: (slot, 0, 0))
    one_col = pl.BlockSpec((1, padded, 1), lambda _: (slot, 0, 0))
    square, vector = whole((width, width)), whole((1, width))
    array = shape_of((slots, padded, width), BF)
    given = len(weights) + len(vectors) + 2

    def kernel(*refs):
        attend_kernel(rows, slot, *refs[:given], *refs[given + len(before) :])

    return kernel_call(
        kernel,
        12,
        [count, x, *weights, *vectors, *before],
        (1,),
        [smem(), block] + [square] * 4 + [vector] * 5 + [pl.BlockSpec(memory_space=pl.ANY)] * len(before),
        [block] * 7 + [one_col],
        [array] * 7 + [shape_of((slots, padded, 1), F32)],
        after=after,
        aliases={given + i: i for i in range(len(before))},
    )


def hidden_block(n_ref, up_ref, ub_ref, down_ref, act_ref, slope_ref):
    size = act_ref.shape[1]
    cut = math.gcd(256, size)
    for at in range(0, size, cut):
        part = slice(at, at + cut)
        pre = nn(n_ref[...], up_ref[:, part]) + ub_ref[:, part]
        cdf = 0.5 + 0.5 * lax.erf(pre * math.sqrt(0.5))
        act_ref[:, part] = (pre * cdf).astype(BF)
        slope = cdf + pre * (jnp.exp(-0.5 * (pre * pre)) * (1.0 / math.sqrt(2.0 * math.pi)))
        slope_ref[:, part] = slope.astype(BF)
    return nn(act_ref[...], down_ref[...])


def add_to(ref, share, first):
    @pl.when(first)
    def _():
        ref[...] = share

    @pl.when(jnp.logical_not(first))
    def _():
        ref[...] += share


def ffn_first_kernel(n_ref, up_ref, ub_ref, down_ref, act_ref, slope_ref, sum_ref):
    share = hidden_block(n_ref, up_ref, ub_ref, down_ref, act_ref, slope_ref)
    add_to(sum_ref, share, pl.program_id(0) == 0)


def ffn_last_kernel(
    rows,
    count_ref,
    n_ref,
    up_ref,
    ub_ref,
    down_ref,
    first_ref,
    cot_ref,
    bd_ref,
    gain_ref,
    shift_ref,
    _act,
    _slope,
    act_ref,
    slope_ref,
    out_ref,
    gsum_ref,
    gbranch_ref,
    vec_ref,
    sum_ref,
):
    step = pl.program_id(0)
    share = hidden_block(n_ref, up_ref, ub_ref, down_ref, act_ref, slope_ref)

    @pl.when(step == 0)
    def _():
        sum_ref[...] = first_ref[...] + share

    @pl.when(step > 0)
    def _():
        sum_ref[...] += share

    @pl.when(step == pl.num_programs(0) - 1)
    def _():
        slots, padded, width = cot_ref.shape
        row = lax.broadcasted_iota(jnp.int32, (padded, width), 0)
        gain = gain_ref[...]
        sums = [jnp.zeros((1, width), F32)] * 3
        for slot in range(slots):
            part = pl.ds(slot * padded, padded)
            count = count_ref[slot]
            keep = ((row < MEM + count) | (row >= rows - MEM)) & (row < rows) & (count > 0)
            summed = n_ref[part, :].astype(F32) + sum_ref[part, :] + bd_ref[...]
            center = summed - rowmean(summed)
            rstd = lax.rsqrt(rowmean(center * center) + EPSILON)
            xhat = center * rstd
            out_ref[slot] = jnp.where(keep, xhat * gain + shift_ref[...], 0.0).astype(BF)
            g_out = jnp.where(keep, cot_ref[slot].astype(F32), 0.0)
            g_xhat = g_out * gain
            g_sum = rstd * (g_xhat - rowmean(g_xhat) - xhat * rowmean(g_xhat * xhat))
            gsum_ref[part, :] = g_sum
            gbranch_ref[part, :] = g_sum.astype(BF)
            new = (colsum(g_out * xhat), colsum(g_out), colsum(g_sum))
            sums = [a + b for a, b in zip(sums, new)]
        for i in range(3):
            vec_ref[pl.ds(i, 1), :] = sums[i]


def ffn_first(normed, own, every, after):
    total, width = normed.shape
    up, up_bias, down = own
    hidden = up.shape[1]
    size = math.gcd(768, hidden)
    acts = shape_of((total, every), BF)
    block = pl.BlockSpec((total, size), lambda j: (0, j))
    return kernel_call(
        ffn_first_kernel,
        9,
        [normed, up, up_bias, down],
        (hidden // size,),
        [
            whole((total, width)),
            pl.BlockSpec((width, size), lambda j: (0, j)),
            pl.BlockSpec((1, size), lambda j: (0, j)),
            pl.BlockSpec((size, width), lambda j: (j, 0)),
        ],
        [block, block, whole((total, width))],
        [acts, acts, shape_of((total, width), F32)],
        after=after,
    )


def ffn_last(rows, padded, count, normed, others, first, cot, vectors, act, slope):
    total, width = normed.shape
    up, up_bias, down = others
    every = act.shape[1]
    hidden = every - up.shape[1]
    size = math.gcd(768, hidden)
    skip = hidden // size
    slots = total // padded
    later = pl.BlockSpec((total, size), lambda j: (0, j + skip))
    cot_block, tall = whole((slots, padded, width)), whole((total, width))
    return kernel_call(
        functools.partial(ffn_last_kernel, rows),
        13,
        [count, normed, up, up_bias, down, first, cot, *vectors, act, slope],
        ((every - hidden) // size,),
        [
            smem(),
            tall,
            pl.BlockSpec((width, size), lambda j: (0, j)),
            pl.BlockSpec((1, size), lambda j: (0, j)),
            pl.BlockSpec((size, width), lambda j: (j, 0)),
            tall,
            cot_block,
        ]
        + [whole((1, width))] * 3
        + [pl.BlockSpec(memory_space=pl.ANY)] * 2,
        [later, later, cot_block, tall, tall, whole((8, width))],
        [
            shape_of(act.shape, BF),
            shape_of(act.shape, BF),
            shape_of(cot.shape, BF),
            shape_of((total, width), F32),
            shape_of((total, width), BF),
            shape_of((8, width), F32),
        ],
        scratch_shapes=[pltpu.VMEM((total, width), F32)],
        aliases={10: 0, 11: 1},
    )


def store_half(piece_ref, values, step, half, unit, shards):
    per = values.shape[0] // unit
    for i in range(per):
        block = step * per + i
        shard, y = block // 2, block % 2
        low, high = shard % 2, shard // 2
        place = jnp.where(half == 0, low * 2 + y, y * 2 + low) * (shards // 2) + high
        at = pl.multiple_of(place * unit, 16)
        piece_ref[pl.ds(at, unit), :] = values[i * unit : (i + 1) * unit].astype(BF)


def half_block(shards, every, size):
    count = every // 2 // size
    if shards == 2:
        return lambda j, half: j * count + half
    return lambda j, half: half * count + j


def down_grad_kernel(unit, shards, half_ref, act_ref, g_ref, piece_ref):
    store_half(piece_ref, tn(act_ref[...], g_ref[...]), pl.program_id(0), half_ref[0], unit, shards)


def down_grad(half, act, g_branch, shards, after):
    total, every = act.shape
    width = g_branch.shape[1]
    size = every // 4
    at = half_block(shards, every, size)
    return kernel_call(
        functools.partial(down_grad_kernel, every // shards // 4, shards),
        4.5,
        [act, g_branch],
        (2,),
        [pl.BlockSpec((total, size), lambda j, h: (0, at(j, h[0]))), whole((total, width))],
        whole((every // 2, width)),
        shape_of((every // 2, width), BF),
        after=after,
        pick=half,
    )


def up_grad_kernel(unit, shards, half_ref, g_ref, n_ref, slope_ref, down0_ref, up0_ref, down1_ref, up1_ref, *rest):
    *so_far, piece_ref, gb_ref, gn_ref, pre_ref = rest
    step = pl.program_id(0)
    size = slope_ref.shape[1]
    cut = math.gcd(256, size)

    def work(down_ref, up_ref, first):
        for at in range(0, size, cut):
            part = slice(at, at + cut)
            g_pre = nt(g_ref[...], down_ref[part, :]) * slope_ref[:, part].astype(F32)
            pre_ref[:, part] = g_pre.astype(BF)
        store_half(piece_ref, tn(pre_ref[...], n_ref[...]), step, half_ref[0], unit, shards)
        gb_ref[...] = colsum(pre_ref[...].astype(F32))
        share = nt(pre_ref[...], up_ref[...])
        if not first:
            gn_ref[...] += share
        elif so_far:
            gn_ref[...] = so_far[0][...] + share
        else:
            gn_ref[...] = share

    @pl.when(step == 0)
    def _():
        work(down0_ref, up0_ref, True)

    @pl.when(step == 1)
    def _():
        work(down1_ref, up1_ref, False)


def up_grad(half, g_branch, normed, slope, weights, shards, so_far, after):
    total, every = slope.shape
    width = normed.shape[1]
    size = every // 4
    at = half_block(shards, every, size)
    tall = whole((total, width))
    specs = []
    for j in range(2):
        place = (lambda h: h) if shards == 2 else (lambda h, j=j: 2 * h + j)
        specs.append(pl.BlockSpec((size, width), lambda _, h, place=place: (place(h[0]), 0)))
        specs.append(pl.BlockSpec((width, size), lambda _, h, place=place: (0, place(h[0]))))
    return kernel_call(
        functools.partial(up_grad_kernel, every // shards // 4, shards),
        12,
        [g_branch, normed, slope, *weights, *so_far],
        (2,),
        [tall, tall, pl.BlockSpec((total, size), lambda j, h: (0, at(j, h[0])))] + specs + [tall] * len(so_far),
        [whole((every // 2, width)), pl.BlockSpec((1, size), lambda j, h: (0, j)), tall],
        [
            shape_of((every // 2, width), BF),
            shape_of((1, every // 2), F32),
            shape_of((total, width), F32),
        ],
        after=after,
        pick=half,
        scratch_shapes=[pltpu.VMEM((total, size), BF)],
    )


def proj_grad_kernel(gsum_ref, gn_ref, xhat_ref, rstd_ref, ctx_ref, wp_ref, gain_ref, gpre_ref, gctx_ref, gw_ref, vec_ref, attn_ref):
    step = pl.program_id(0)
    padded = gsum_ref.shape[0]
    g_normed = gsum_ref[...] + gn_ref[...]
    xhat = xhat_ref[...].astype(F32)
    g_xhat = g_normed * gain_ref[...]
    g_pre = rstd_ref[...] * (g_xhat - rowmean(g_xhat) - xhat * rowmean(g_xhat * xhat))
    gpre_ref[...] = g_pre
    g_attn = g_pre.astype(BF)
    attn_ref[pl.ds(pl.multiple_of(step * padded, 16), padded), :] = g_attn
    gctx_ref[...] = nt(g_attn, wp_ref[...]).astype(BF)
    new = jnp.concatenate([colsum(g_normed * xhat), colsum(g_normed), colsum(g_pre)] + [jnp.zeros_like(gain_ref)] * 5)
    add_to(vec_ref, new, step == 0)

    @pl.when(step == pl.num_programs(0) - 1)
    def _():
        gw_ref[...] = tn(ctx_ref[...], attn_ref[...]).astype(BF)


def proj_grad(padded, g_sum, g_norm, xhat, rstd, ctx, wp, gain, after):
    total, width = g_sum.shape
    block = pl.BlockSpec((padded, width), lambda s: (s, 0))
    return kernel_call(
        proj_grad_kernel,
        6,
        [g_sum, g_norm, xhat, rstd, ctx, wp, gain],
        (total // padded,),
        [block] * 3
        + [pl.BlockSpec((padded, 1), lambda s: (s, 0)), whole((total, width)), whole((width, width)), whole((1, width))],
        [block, block, whole((width, width)), whole((8, width))],
        [
            shape_of((total, width), F32),
            shape_of((total, width), BF),
            shape_of((width, width), BF),
            shape_of((8, width), F32),
        ],
        after=after,
        scratch_shapes=[pltpu.VMEM((total, width), BF)],
    )


def attend_back_kernel(rows, count_ref, q_ref, aux_ref, k_ref, v_ref, ctx_ref, g_ref, *rest):
    slot = pl.program_id(0)
    x_ref, before_ref, d_ref, gw_ref, vec_ref = rest if len(rest) > 1 else (None, None, *rest, None, None)
    slots, padded, _ = d_ref.shape
    lane = lax.broadcasted_iota(jnp.int32, (padded, PAIR), 1)
    bias = key_bias(count_ref[slot], rows, padded)
    one = jnp.ones((), BF)
    zero = jnp.zeros((), BF)
    q, extra, k, v, g = q_ref[0], aux_ref[0], k_ref[0], v_ref[0], g_ref[0]
    products = g.astype(F32) * ctx_ref[0].astype(F32)
    parts = []
    for head in range(2):
        own = (lane < HEAD) if head == 0 else (lane >= HEAD)
        aux = HEAD if head == 0 else 0
        delta = -jnp.sum(jnp.where(own, products, 0.0), -1, keepdims=True)
        high = delta.astype(BF)
        low = (delta - high.astype(F32)).astype(BF)
        after = (lane > aux) & (lane < aux + 4)
        k_more = jnp.where(own, k, jnp.where(lane == aux, bias, jnp.where(after, one, zero)))
        v_more = jnp.where(own, v, jnp.where((lane >= aux) & (lane < aux + 2), one, zero))
        q_more = jnp.where(own, q, extra)
        g_more = jnp.where(own, g, jnp.where(lane == aux, high, jnp.where(lane == aux + 1, low, zero)))
        probs = jnp.exp(nt(k_more, q_more))
        g_scores = (probs * nt(v_more, g_more)).astype(BF)
        parts.append((tn(g_scores, k_more), nn(g_scores, q_more), nn(probs.astype(BF), g_more)))
    g_q, g_k, g_v = (jnp.where(lane < HEAD, a, b) for a, b in zip(*parts))
    g_q = (g_q.astype(BF).astype(F32) * (1.0 / math.sqrt(HEAD))).astype(BF)
    for i, part in enumerate((g_q, g_k.astype(BF), g_v.astype(BF))):
        d_ref[slot, :, i * PAIR : (i + 1) * PAIR] = part

    if x_ref is None:
        return

    @pl.when(slot == slots - 1)
    def _():
        width = x_ref.shape[2]
        row = lax.broadcasted_iota(jnp.int32, (padded, width), 0)
        x = jnp.concatenate([jnp.where(row < rows, x_ref[s], zero) for s in range(slots)])
        d = jnp.concatenate(
            [jnp.concatenate([before_ref[s], d_ref[s]], axis=1) for s in range(slots)]
        )
        gw_ref[...] = tn(x, d).astype(BF)
        vec_ref[...] = colsum(d.astype(F32))


def attend_back(rows, pair, count, x, arrays, before, after):
    slots, padded, width = arrays[0].shape
    block = pl.BlockSpec((1, padded, PAIR), lambda s: (s, 0, pair))
    wide = whole((slots, padded, 3 * PAIR))
    operands, specs = [count, *arrays], [smem()] + [block] * 6
    outs, out_specs = [shape_of((slots, padded, 3 * PAIR), BF)], [wide]
    if before is not None:
        operands += [x, before]
        specs += [whole((slots, padded, width)), wide]
        outs += [shape_of((width, 6 * PAIR), BF), shape_of((1, 6 * PAIR), F32)]
        out_specs += [whole((width, 6 * PAIR)), whole((1, 6 * PAIR))]
    return kernel_call(
        functools.partial(attend_back_kernel, rows),
        6 if before is None else 8,
        operands,
        (slots,),
        specs,
        out_specs,
        outs,
        after=after,
    )


def in_lanes(pairs, i):
    return jnp.concatenate([p[..., i * PAIR : (i + 1) * PAIR] for p in pairs], axis=-1)


def input_grad_kernel(many, gpre_ref, *refs):
    d_refs, w_refs, out_ref = refs[:many], refs[many : many + 3], refs[-1]
    total = gpre_ref[0]
    for i, w_ref in enumerate(w_refs):
        total = total + nt(in_lanes([d[0] for d in d_refs], i), w_ref[...])
    out_ref[0] = total


def input_grad(shape, g_pre, parts, weights, after):
    slots, padded, width = g_pre.shape
    block = pl.BlockSpec((1, padded, width), lambda s: (s, 0, 0))
    narrow = pl.BlockSpec((1, padded, 3 * PAIR), lambda s: (s, 0, 0))
    return kernel_call(
        functools.partial(input_grad_kernel, len(parts)),
        8,
        [g_pre, *parts, *weights],
        (slots,),
        [block] + [narrow] * len(parts) + [whole((width, width))] * 3,
        block,
        shape_of(shape, F32),
        after=after,
    )


class Links:
    def __init__(self, items, shards):
        self.items, self.shards = items, shards
        self.joint = lax.axis_index("dp") * shards + lax.axis_index("seg")
        self.core = shards
        self.y = 2 * shards
        self.seg = [1 << i for i in range(shards.bit_length() - 1)]
        self.z = [shards << i for i in range(2, items.bit_length() - 1)]

    def swap(self, value, mask0, mask1):
        count = self.items * self.shards
        pairs = [(i, i ^ (mask1 if i & self.core else mask0)) for i in range(count)]
        return lax.ppermute(value, JOINT, pairs)

    def bit(self, mask0, mask1):
        on_core1 = (self.joint & self.core) != 0
        return jnp.where(on_core1, (self.joint & mask1) != 0, (self.joint & mask0) != 0).astype(jnp.int32)

    def steps(self):
        first = self.seg[0] if self.seg else self.y
        return (
            [(self.core, self.core), (first, self.y), (self.y, first)]
            + [(m, m) for m in reversed(self.seg[1:])]
            + [(m, m) for m in self.z]
        )

    def keep_index(self, step, relative):
        if not relative:
            return self.bit(*step)
        own = [mask in self.seg for mask in step]
        here = self.bit(*step)
        on_core1 = (self.joint & self.core) != 0
        return jnp.where(jnp.where(on_core1, own[1], own[0]), 0, here)


def tiled(rows):
    return rows % 16 == 0


def ordered(late, a, b, axis=0):
    return jnp.concatenate([jnp.where(late, b, a), jnp.where(late, a, b)], axis=axis)


def add_halves(held, got, keep, small, after):
    rows, width = held.shape
    half = rows // 2
    extra = 0 if small is None else small.shape[0]
    if not tiled(half):
        total = held + got[:rows]
        send = lax.dynamic_slice_in_dim(total, (1 - keep[0]) * half, half)
        held = lax.dynamic_slice_in_dim(total, keep[0] * half, half)
        if extra:
            small = small + got[rows:]
            send = jnp.concatenate([send, small])
        return send, held, small

    def kernel(_, held0, held1, got0, got1, *rest):
        if extra:
            small_in, got_small, send_ref, held_ref, small_ref = rest
            small_ref[...] = small_in[...] + got_small[...]
            send_ref[half:, :] = small_ref[...]
        else:
            send_ref, held_ref = rest
        send_ref[:half, :] = held0[...] + got0[...]
        held_ref[...] = held1[...] + got1[...]

    other = pl.BlockSpec((half, width), lambda _, k: (1 - k[0], 0))
    mine = pl.BlockSpec((half, width), lambda _, k: (k[0], 0))
    operands, specs = [held, held, got, got], [other, mine, other, mine]
    out_shape = [shape_of((half + extra, width), BF), shape_of((half, width), BF)]
    if extra:
        operands += [small, got]
        specs += [whole((extra, width)), pl.BlockSpec((extra, width), lambda *_: (rows // extra, 0))]
        out_shape.append(shape_of((extra, width), BF))
    out = kernel_call(
        kernel, 1, operands, (1,), specs, [whole(t.shape) for t in out_shape], out_shape, after=after, pick=keep, vmem=16
    )
    return (*out, None)[:3]


def add_whole(held, got, small, after, joined=None):
    rows, width = held.shape
    extra = 0 if small is None else small.shape[0]
    if not tiled(rows):
        piece = held + got[:rows]
        small = small + got[rows:] if extra else None
        return piece, small

    def kernel(held_ref, got_ref, *rest):
        if extra:
            small_in, got_small, piece_ref, small_ref = rest
            small_ref[...] = small_in[...] + got_small[...]
        else:
            (piece_ref,) = rest
        piece_ref[...] = held_ref[...] + got_ref[...]

    part = whole((rows, width))
    operands, specs, out_shape = [held, got], [part, part], [shape_of((rows, width), BF)]
    if extra:
        operands += [small, got]
        specs += [whole((extra, width)), pl.BlockSpec((extra, width), lambda *_: (rows // extra, 0))]
        out_shape.append(shape_of((extra, width), BF))
    out = kernel_call(
        kernel, 1, operands, (1,), specs, [whole(t.shape) for t in out_shape], out_shape, after=after, vmem=16
    )
    return (*out, None)[:2]


def add_pairs(pieces, gots, after):
    if not tiled(pieces[0].shape[0]):
        return jnp.stack([a + b for a, b in zip(pieces, gots)])
    many = len(pieces)

    def kernel(*refs):
        for i in range(many):
            refs[-1][i] = refs[i][...] + refs[many + i][...]

    out = shape_of((many, *pieces[0].shape), BF)
    return kernel_call(
        kernel,
        1,
        [*pieces, *gots],
        (1,),
        [whole(pieces[0].shape)] * (2 * many),
        whole(out.shape),
        out,
        after=after,
        vmem=16,
    )


def join(piece, got, late, after):
    rows, width = piece.shape[-2:]
    if not tiled(rows):
        return ordered(late[0] == 1, piece, got, axis=-2)
    lead = math.prod(piece.shape[:-2])

    def kernel(late_ref, piece_ref, got_ref, out_ref):
        place = pl.multiple_of(late_ref[0] * rows, 16)
        for i in range(lead):
            out_ref[i, pl.ds(place, rows), :] = piece_ref[i]
            out_ref[i, pl.ds(rows - place, rows), :] = got_ref[i]

    part = whole((lead, rows, width))
    out = kernel_call(
        kernel,
        1,
        [t.reshape(lead, rows, width) for t in (piece, got)],
        (1,),
        [part, part],
        whole((lead, 2 * rows, width)),
        shape_of((lead, 2 * rows, width), BF),
        after=after,
        pick=late,
        vmem=16,
    )
    return out.reshape(*piece.shape[:-2], 2 * rows, width)


class Sum:
    def __init__(self, links, relative, halves, small=None):
        self.links, self.relative, self.small = links, relative, small
        self.halves = list(halves)
        steps = links.steps()
        self.adding, self.passing = steps, [s for s in self.way_back(steps[:-1])]
        self.held = self.piece = None
        self.flying = None
        self.place = 0

    def way_back(self, steps):
        links = self.links
        for step in reversed(steps):
            crosses = [mask in links.seg for mask in step]
            if self.relative and crosses[0]:
                if not crosses[1]:
                    yield (links.y, links.y)
            elif not (self.relative and crosses[1]):
                yield step

    def keep(self, index):
        return self.links.keep_index(self.adding[index], self.relative).reshape(1)

    def advance(self, after=()):
        links, index = self.links, self.place
        self.place += 1
        last = len(self.adding) - 1
        if index == 0:
            send, self.held = self.halves
            if self.small is not None:
                send = jnp.concatenate([send, self.small])
        elif index < last:
            send, self.held, self.small = add_halves(self.held, self.flying, self.keep(index), self.small, after)
        elif index == last:
            self.held, self.small = add_whole(self.held, self.flying, self.small, after)
            send = self.held if self.small is None else jnp.concatenate([self.held, self.small])
        elif index == last + 1:
            send, self.small = add_whole(self.held, self.flying, self.small, after)
            self.piece = send
        else:
            done = self.passing[index - last - 2]
            send = self.piece = join(self.piece, self.flying, links.bit(*done).reshape(1), after)
        step = self.adding[index] if index <= last else self.passing[index - last - 1]
        self.flying = links.swap(send, *step)
        return [send]

    def left(self):
        return len(self.adding) + len(self.passing) - self.place

    def finish(self, after=()):
        while self.left():
            self.advance(after)
        return self.piece, self.flying


class Merged:
    def __init__(self, links, sums):
        self.links, self.sums = links, sums
        self.passing = sums[0].passing
        self.place = 0

    def advance(self, after=()):
        index = self.place
        self.place += 1
        if index == 0:
            for s in self.sums:
                while s.place < len(s.adding):
                    s.advance(after)
            self.piece = add_pairs([s.held for s in self.sums], [s.flying for s in self.sums], after)
        else:
            done = self.links.bit(*self.passing[index - 1]).reshape(1)
            self.piece = join(self.piece, self.flying, done, after)
        self.flying = self.links.swap(self.piece, *self.passing[index])
        return [self.piece]

    def left(self):
        return len(self.passing) - self.place

    def finish(self, after=()):
        while self.left():
            self.advance(after)
        return self.piece, self.flying


class Gather:
    def __init__(self, links, up, up_bias, down):
        self.links = links
        width, hidden = up.shape
        self.width, self.hidden = width, hidden
        z, y, core = links.z[0], links.y, links.core
        self.steps = [(links.seg[0], links.seg[0]), (z, y), (y, z), (core, core)]
        self.place = 0
        place = links.bit(core, core) * 4 + links.bit(y, z) * 2 + links.bit(z, y)
        self.wide = hidden // width
        cut, deep, wide = width // 8, hidden // 8, self.wide
        rows = wide * cut + deep + 16

        def kernel(_, up_ref, down_ref, bias_ref, out_ref):
            for i in range(wide):
                out_ref[i * cut : (i + 1) * cut, :] = up_ref[:, i * width : (i + 1) * width]
            out_ref[wide * cut : wide * cut + deep, :] = down_ref[...]
            lines, rest = [], bias_ref[...]
            for _ in range(3):
                term = rest.astype(BF).astype(F32)
                lines += [term[:, i * width : (i + 1) * width] for i in range(wide)]
                rest = rest - term
            lines.append(jnp.zeros((16 - len(lines), width), F32))
            out_ref[rows - 16 :, :] = jnp.concatenate(lines).astype(BF)

        self.piece = kernel_call(
            kernel,
            2,
            [up, down, up_bias],
            (1,),
            [
                pl.BlockSpec((cut, hidden), lambda _, e: (e[0], 0)),
                pl.BlockSpec((deep, width), lambda _, e: (e[0], 0)),
                whole((1, hidden)),
            ],
            whole((rows, width)),
            shape_of((rows, width), BF),
            pick=place.reshape(1),
            vmem=16,
        )

    def advance(self, after=()):
        index = self.place
        self.place += 1
        if index == 1:
            self.piece = self.flying[None]
        elif index > 1:
            done = self.links.bit(*self.steps[index - 1]).reshape(1)
            joined = join(self.piece, self.flying, done, after)
            self.piece = joined
        self.flying = self.links.swap(self.piece, *self.steps[index])
        return [self.piece]

    def finish(self, after=()):
        while self.place < len(self.steps):
            self.advance(after)
        width, hidden, wide = self.width, self.hidden, self.wide
        cut, deep = width // 8, hidden // 8
        rows = wide * cut + deep + 16
        piece, got = (t.reshape(4 * rows, width) for t in (self.piece, self.flying))

        def kernel(core_ref, piece_ref, got_ref, up_ref, bias_ref, down_ref):
            for i in range(8):
                ref = piece_ref if i < 4 else got_ref
                start = (i % 4) * rows
                place = (core_ref[0] ^ (i // 4)) * 4 + i % 4
                at = pl.ds(pl.multiple_of(place * cut, 16), cut)
                for j in range(wide):
                    up_ref[at, j * width : (j + 1) * width] = ref[start + j * cut : start + (j + 1) * cut, :]
                at = pl.ds(pl.multiple_of(place * deep, 16), deep)
                down_ref[at, :] = ref[start + wide * cut : start + wide * cut + deep, :]
            lines = piece_ref[rows - 16 : rows, :].astype(F32)
            for j in range(wide):
                bias_ref[:, j * width : (j + 1) * width] = sum(lines[i * wide + j : i * wide + j + 1] for i in range(3))

        return kernel_call(
            kernel,
            3,
            [piece, got],
            (1,),
            [whole(piece.shape)] * 2,
            [whole((width, hidden)), whole((1, hidden)), whole((hidden, width))],
            [shape_of((width, hidden), BF), shape_of((1, hidden), F32), shape_of((hidden, width), BF)],
            after=after,
            pick=self.links.bit(self.links.core, self.links.core).reshape(1),
        )


class GatherAny:
    def __init__(self, *args):
        self.args = args

    def advance(self, after=()):
        return []

    def finish(self, after=()):
        return other_shards(*self.args)


def other_shards(links, up, up_bias, down):
    shards = links.shards
    hidden = down.shape[0]
    ups = lax.all_gather(up, "seg", axis=0)
    downs = lax.all_gather(down, "seg", axis=0)
    biases = lax.all_gather(up_bias, "seg", axis=0)
    order = lax.axis_index("seg") ^ jnp.arange(1, shards)
    ups = jnp.moveaxis(jnp.take(ups, order, axis=0), 0, 1).reshape(up.shape[0], -1)
    return ups, jnp.take(biases, order, axis=0).reshape(1, -1), jnp.take(downs, order, axis=0).reshape(-1, down.shape[1])


def core_halves(core, array):
    half = array.shape[0] // 2
    return tuple(lax.dynamic_slice_in_dim(array, c[0] * half, half) for c in (1 - core, core))


def pack_small(links, core, vec_ffn, vec_attn, g_lines, bias_send, bias_keep, shards):
    width = vec_ffn.shape[1]
    if shards != 2 or bias_send.shape[1] != 2 * width:
        halves = ordered(core[0] == 1, bias_keep, bias_send).reshape(2, shards, -1)
        by_shard = jnp.moveaxis(halves, 0, 1).reshape(shards, -1)
        by_shard = jnp.take(by_shard, jnp.arange(shards) ^ lax.axis_index("seg"), axis=0).reshape(-1, width)
        lines = [
            in_lanes([g[:, i * 3 * PAIR : (i + 1) * 3 * PAIR] for g in g_lines for i in range(2)], i) for i in (0, 2)
        ]
        small = jnp.concatenate([vec_ffn[:3], vec_attn[:3], *lines, by_shard])
        pad = -(-small.shape[0] // 16) * 16 - small.shape[0]
        return jnp.pad(small, ((0, pad), (0, 0))).astype(BF)

    def kernel(at_ref, ffn_ref, attn_ref, *rest):
        line_refs, send_ref, keep_ref, out_ref, rows_ref = rest[:-4], *rest[-4:]
        rows_ref[...] = jnp.zeros_like(rows_ref)
        rows_ref[0:3, :] = ffn_ref[0:3, :]
        rows_ref[3:6, :] = attn_ref[0:3, :]
        for g, line_ref in enumerate(line_refs):
            for i in range(2):
                for row, part in ((6, 0), (7, 2)):
                    at = (3 * i + part) * PAIR
                    place = (2 * g + i) * PAIR
                    rows_ref[row : row + 1, place : place + PAIR] = line_ref[:, at : at + PAIR]
        for ref, half in ((send_ref, 1 - at_ref[0]), (keep_ref, at_ref[0])):
            for i in range(2):
                row = 8 + 2 * (at_ref[1] ^ i) + half
                rows_ref[pl.ds(row, 1), :] = ref[:, i * width : (i + 1) * width]
        out_ref[...] = rows_ref[...].astype(BF)

    operands = [vec_ffn, vec_attn, *g_lines, bias_send, bias_keep]
    return kernel_call(
        kernel,
        1,
        operands,
        (1,),
        [whole(t.shape) for t in operands],
        whole((16, width)),
        shape_of((16, width), BF),
        pick=jnp.concatenate([core, lax.axis_index("seg").reshape(1)]),
        scratch_shapes=[pltpu.VMEM((16, width), F32)],
        vmem=16,
    )


def ffn_outputs(core, piece, got):
    _, rows, width = piece.shape
    if rows % PAIR:
        down, up = ordered(core[0] == 1, piece, got, axis=1).astype(F32)
        return down, up.T

    def kernel(core_ref, piece_ref, got_ref, down_ref, up_ref):
        def store(ref):
            down_ref[...] = ref[0].astype(F32)
            up_ref[...] = ref[1].astype(F32).T

        mine = pl.program_id(0) == core_ref[0]
        pl.when(mine)(lambda: store(piece_ref))
        pl.when(jnp.logical_not(mine))(lambda: store(got_ref))

    return kernel_call(
        kernel,
        5,
        [piece, got],
        (2,),
        [whole(piece.shape)] * 2,
        [pl.BlockSpec((rows, width), lambda h, _: (h, 0)), pl.BlockSpec((width, rows), lambda h, _: (0, h))],
        [shape_of((2 * rows, width), F32), shape_of((width, 2 * rows), F32)],
        pick=core,
    )


def square_outputs(core, group, groups, halves, before):
    rows, width = halves[0].shape
    wide = 2 * PAIR

    def kernel(core_ref, *refs):
        half_refs, out_refs = refs[: len(halves)], refs[len(halves) + len(before) :]

        def store(ref):
            for i, out_ref in enumerate(out_refs):
                for j in range(2):
                    at = (3 * j + i) * PAIR
                    out_ref[:, j * PAIR : (j + 1) * PAIR] = ref[:, at : at + PAIR].astype(F32)

        if len(halves) == 1:
            store(half_refs[0])
        else:
            mine = pl.program_id(0) == core_ref[0]
            pl.when(mine)(lambda: store(half_refs[0]))
            pl.when(jnp.logical_not(mine))(lambda: store(half_refs[1]))

    total = rows * len(halves)
    out = shape_of((total, groups * wide), F32)
    return kernel_call(
        kernel,
        2,
        [*halves, *before],
        (len(halves),),
        [whole((rows, width))] * len(halves) + [pl.BlockSpec(memory_space=pl.ANY)] * len(before),
        [pl.BlockSpec((rows, wide), lambda h, _: (h, group))] * 3,
        [out] * 3,
        pick=core,
        aliases={1 + len(halves) + i: i for i in range(len(before))},
    )


def in_halves(array, axis, shards):
    shape = list(array.shape)
    parts = array.reshape(shape[:axis] + [shards, 2, -1] + shape[axis + 1 :])
    return jnp.moveaxis(parts, axis + 1, axis).reshape(shape)


def body(
    activations,
    tok_count,
    w_query,
    w_key,
    w_value,
    w_proj,
    b_query,
    b_value,
    b_proj,
    gain_attn,
    shift_attn,
    w_up,
    b_up,
    w_down,
    b_down,
    gain_ffn,
    shift_ffn,
    cotangent,
    items,
    shards,
):
    slots, rows, width = activations.shape
    padded = -(-rows // 16) * 16
    total = slots * padded
    links = Links(items, shards)
    core = links.bit(links.core, links.core).reshape(1)
    count = tok_count[:, 0]
    line = lambda vector: vector.reshape(1, -1)
    flat = lambda array: array.reshape(total, -1)
    own = (w_up, line(b_up), w_down)
    every = w_up.shape[1] * shards
    weights = (Gather if shards == 2 and links.z else GatherAny)(links, w_up, line(b_up), w_down)

    squares = [w_query, w_key, w_value, w_proj]
    vectors = [line(t) for t in (b_query, b_value, b_proj, gain_attn, shift_attn)]
    state = []
    for slot in range(slots):
        after = weights.advance([t for t in state[-1:]])
        state = attend(rows, padded, slot, count, activations, squares, vectors, state, after)
    q, extra, k, v, ctx, normed, xhat, rstd = state
    normed = flat(normed)
    act, slope, first = ffn_first(normed, own, every, weights.advance([rstd]))
    others = weights.finish([first])
    act, slope, layer_out, g_sum, g_branch, vec_ffn = ffn_last(
        rows,
        padded,
        count,
        normed,
        others,
        first,
        cotangent,
        [line(t) for t in (b_down, gain_ffn, shift_ffn)],
        act,
        slope,
    )
    if shards == 2:
        pieces = [own[2], own[0], others[2], others[0]]
    else:
        act, slope = (in_halves(t, 1, shards) for t in (act, slope))
        ups = in_halves(jnp.concatenate([own[0], others[0]], 1), 1, shards)
        downs = in_halves(jnp.concatenate([own[2], others[2]]), 0, shards)
        pieces = [downs, ups, downs, ups]

    send = down_grad(1 - core, act, g_branch, shards, [])
    keep = down_grad(core, act, g_branch, shards, [send])
    down_sum = Sum(links, True, (send, keep))
    after = down_sum.advance()
    send, bias_send, so_far = up_grad(1 - core, g_branch, normed, slope, pieces, shards, [], after)
    after = down_sum.advance([bias_send])
    keep, bias_keep, g_norm = up_grad(core, g_branch, normed, slope, pieces, shards, [so_far], after + [send])
    up_sum = Sum(links, True, (send, keep))
    after = up_sum.advance() + down_sum.advance([bias_keep])
    g_pre, g_ctx, g_proj, vec_attn = proj_grad(
        padded, g_sum, g_norm, flat(xhat), flat(rstd), flat(ctx), w_proj, line(gain_attn), after
    )
    last_done = [vec_attn]

    arrays = [q, extra, k, v, ctx, g_ctx.reshape(q.shape)]
    d_parts, g_weights, g_lines = [], [], []
    ffn_sum = Merged(links, [down_sum, up_sum])
    on_core1 = core[0] == 1
    plan = [[up_sum], [], [up_sum, down_sum], [up_sum, down_sum], [up_sum], []]
    for pair in range(width // PAIR):
        after = [t for s in plan[pair] for t in s.advance(last_done)]
        if pair % 2 == 0:
            (d,) = attend_back(rows, pair, count, activations, arrays, None, after + last_done)
            last_done = [d]
        else:
            d, gw, gl = attend_back(rows, pair, count, activations, arrays, d_parts[-1], after + last_done)
            g_weights.append(gw)
            g_lines.append(gl)
            last_done = [gl]
        d_parts.append(d)
        if pair == 1:
            first_sum = Sum(
                links, False, (jnp.where(on_core1, g_proj, gw), jnp.where(on_core1, gw, g_proj))
            )
            plan[2].append(first_sum)
            plan[3].append(first_sum)
            plan[4].append(first_sum)
        if pair == 3:
            second_sum = Sum(links, False, core_halves(core, gw))
            plan[4].append(second_sum)
            plan[5].append(second_sum)
    small = pack_small(links, core, vec_ffn, vec_attn, g_lines, bias_send, bias_keep, shards)
    third_sum = Sum(links, False, core_halves(core, g_weights[2]), small)
    after = third_sum.advance(last_done) + second_sum.advance(last_done) + first_sum.advance(last_done)
    grad_input = input_grad(
        activations.shape, g_pre.reshape(q.shape), d_parts, [w_query, w_key, w_value], after
    )
    sums = [third_sum, second_sum, first_sum, ffn_sum]
    while any(s.left() for s in sums):
        for s in sums:
            if s.left():
                s.advance([])
    grad_w_down, grad_w_up = ffn_outputs(core, *ffn_sum.finish())
    piece, got = first_sum.finish()
    grad_w_proj = jnp.where(on_core1, got, piece).astype(F32)
    halves = [(jnp.where(on_core1, piece, got),), second_sum.finish(), third_sum.finish()]
    outputs = []
    for group, half in enumerate(halves):
        outputs = square_outputs(core, group, len(halves), half, outputs)
    g_query, g_key, g_value = outputs
    small = third_sum.small.astype(F32)
    biases = small[8 : 8 + every // width].reshape(shards, -1)
    grad_b_up = lax.dynamic_index_in_dim(biases, lax.axis_index("seg"), keepdims=False)
    return (
        layer_out,
        grad_input,
        g_query,
        g_key,
        g_value,
        grad_w_proj,
        small[6],
        small[7],
        small[5],
        small[3],
        small[4],
        grad_w_up,
        grad_b_up,
        grad_w_down,
        small[2],
        small[0],
        small[1],
    )


def solution(mesh):
    rows, everywhere = P("dp", "seg", None), P()
    return jax.shard_map(
        functools.partial(body, items=mesh.shape["dp"], shards=mesh.shape["seg"]),
        mesh=mesh,
        in_specs=(rows, P("dp", "seg"))
        + (everywhere,) * 9
        + (P(None, "seg"), P("seg"), P("seg", None))
        + (everywhere,) * 3
        + (rows,),
        out_specs=(rows, rows)
        + (everywhere,) * 9
        + (P(None, "seg"), P("seg"), P("seg", None))
        + (everywhere,) * 3,
        check_vma=False,
    )
```

```python
import functools
import math

import jax
import jax.numpy as jnp
from jax import lax
from jax.experimental import pallas as pl
from jax.experimental.pallas import tpu as pltpu
from jax.sharding import PartitionSpec as P

HEAD = 64
MEM = 10
EPSILON = 1e-05
NEG_BIG = -1e30
PAIR = 2 * HEAD
BF = jnp.bfloat16
F32 = jnp.float32
VMEM_MIB = 16
PASS_MIB = 6
ATTEND_MIB = 10
FFN_MIB = 10
UP_MIB = 6
BACK_MIB = 6
JOINT = ("dp", "seg")


def nn(left, right):
    return jnp.dot(left, right, preferred_element_type=F32)


def tn(left, right):
    return lax.dot_general(left, right, (((0,), (0,)), ((), ())), preferred_element_type=F32)


def nt(left, right):
    return lax.dot_general(left, right, (((1,), (1,)), ((), ())), preferred_element_type=F32)


def colsum(values):
    return jnp.sum(values, 0, keepdims=True)


def rowmean(values):
    return jnp.mean(values, -1, keepdims=True)


def kernel_call(kernel, micros, operands, out_shape, scalars=0, after=(), scratch_shapes=(), vmem=VMEM_MIB, far=()):
    many = len(operands)
    anywhere = pl.BlockSpec(memory_space=pl.ANY)
    near = pl.BlockSpec(memory_space=pltpu.VMEM)

    def run(*refs):
        kernel(*refs[:many], *refs[many + len(after) :])

    specs = [pl.BlockSpec(memory_space=pltpu.SMEM) if i < scalars else near for i in range(many)]
    outs = out_shape if isinstance(out_shape, list) else [out_shape]
    outs = [t if i in far else pltpu.VMEM(t.shape, t.dtype) for i, t in enumerate(outs)]
    results = pl.pallas_call(
        run,
        in_specs=specs + [anywhere] * len(after),
        out_specs=[near] * len(outs),
        out_shape=outs,
        scratch_shapes=scratch_shapes,
        compiler_params=pltpu.CompilerParams(vmem_limit_bytes=vmem * 2**20),
        cost_estimate=pl.CostEstimate(
            flops=int(micros * 1.0e9), bytes_accessed=1 << 20, transcendentals=0
        ),
    )(*operands, *after)
    return results if isinstance(out_shape, list) else results[0]


def shape_of(shape, dtype):
    return jax.ShapeDtypeStruct(shape, dtype)


def like(array):
    return shape_of(array.shape, array.dtype)


def flat_line(ref):
    return ref[...].reshape(1, -1)


def tile_rows(start, rows):
    return pl.ds(pl.multiple_of(start, 16), rows)


def tile_lanes(start, lanes):
    return pl.ds(pl.multiple_of(start, PAIR), lanes)


def key_bias(count, rows, padded):
    row = lax.broadcasted_iota(jnp.int32, (padded, PAIR), 0)
    valid = ((row < MEM + count) | (row >= rows - MEM)) & (row < rows)
    return jnp.where(valid, 0.0, NEG_BIG).astype(BF)


def attend_kernel(
    rows,
    slot,
    count_ref,
    x_ref,
    wq_ref,
    wk_ref,
    wv_ref,
    wp_ref,
    bq_ref,
    bv_ref,
    bp_ref,
    gain_ref,
    shift_ref,
    q_ref,
    aux_ref,
    k_ref,
    v_ref,
    ctx_ref,
    normed_ref,
    xhat_ref,
    rstd_ref,
):
    padded, width = x_ref.shape[1:]
    x = x_ref[slot]
    q_ref[...] = ((nn(x, wq_ref[...]) + flat_line(bq_ref)) * (1.0 / math.sqrt(HEAD))).astype(BF)
    k_ref[...] = nn(x, wk_ref[...]).astype(BF)
    v_ref[...] = (nn(x, wv_ref[...]) + flat_line(bv_ref)).astype(BF)
    lane = lax.broadcasted_iota(jnp.int32, (padded, PAIR), 1)
    bias = key_bias(count_ref[slot], rows, padded)
    one = jnp.ones((), BF)
    zero = jnp.zeros((), BF)
    for pair in range(width // PAIR):
        lanes = slice(pair * PAIR, (pair + 1) * PAIR)
        q, k, v = q_ref[:, lanes], k_ref[:, lanes], v_ref[:, lanes]
        contexts, extras = [], []
        for head in range(2):
            own = (lane < HEAD) if head == 0 else (lane >= HEAD)
            aux = HEAD if head == 0 else 0
            at_aux = jnp.where(lane == aux, one, zero)
            scores = nt(
                jnp.where(own, q, at_aux),
                jnp.where(own, k, jnp.where(lane == aux, bias, zero)),
            )
            top = jnp.max(scores, -1, keepdims=True)
            exps = jnp.exp(scores - top).astype(BF)
            weighted = nn(exps, jnp.where(own, v, at_aux))
            total = weighted[:, aux : aux + 1]
            contexts.append(weighted * (1.0 / total))
            rest = -(top + jnp.log(total))
            high = rest.astype(BF)
            rest = rest - high.astype(F32)
            middle = rest.astype(BF)
            low = (rest - middle.astype(F32)).astype(BF)
            extras.append(
                jnp.where(
                    lane == aux + 1,
                    high,
                    jnp.where(lane == aux + 2, middle, jnp.where(lane == aux + 3, low, at_aux)),
                )
            )
        ctx_ref[:, lanes] = jnp.where(lane < HEAD, contexts[0], contexts[1]).astype(BF)
        aux_ref[:, lanes] = jnp.where(lane < HEAD, extras[1], extras[0])
    pre_norm = x.astype(F32) + nn(ctx_ref[...], wp_ref[...]) + flat_line(bp_ref)
    center = pre_norm - rowmean(pre_norm)
    rstd = lax.rsqrt(rowmean(center * center) + EPSILON)
    xhat = center * rstd
    normed_ref[...] = (xhat * flat_line(gain_ref) + flat_line(shift_ref)).astype(BF)
    xhat_ref[...] = xhat.astype(BF)
    rstd_ref[...] = rstd


def attend(rows, slot, count, x, weights, vectors, after):
    array = shape_of(x.shape[1:], BF)
    return kernel_call(
        functools.partial(attend_kernel, rows, slot),
        11,
        [count, x, *weights, *vectors],
        [array] * 7 + [shape_of((x.shape[1], 1), F32)],
        scalars=1,
        after=after,
        vmem=ATTEND_MIB,
    )


def hidden_units(n_refs, up_ref, ub_ref, act_ref, slope_ref):
    size = up_ref.shape[1]
    bias = flat_line(ub_ref)
    cut = math.gcd(256, size)
    padded = n_refs[0].shape[0]
    for at in range(0, size, cut):
        part = slice(at, at + cut)
        for slot, n_ref in enumerate(n_refs):
            rows = slice(slot * padded, (slot + 1) * padded)
            pre = nn(n_ref[...], up_ref[:, part]) + bias[:, part]
            cdf = 0.5 + 0.5 * lax.erf(pre * math.sqrt(0.5))
            act_ref[rows, part] = (pre * cdf).astype(BF)
            slope = cdf + pre * (jnp.exp(-0.5 * (pre * pre)) * (1.0 / math.sqrt(2.0 * math.pi)))
            slope_ref[rows, part] = slope.astype(BF)


def ffn_first_kernel(slots, *refs):
    up_ref, ub_ref, down_ref, act_ref, slope_ref, sum_ref = refs[slots:]
    hidden_units(refs[:slots], up_ref, ub_ref, act_ref, slope_ref)
    sum_ref[...] = nn(act_ref[...], down_ref[...])


def ffn_last_kernel(rows, slots, count_ref, *refs):
    n_refs, refs = refs[:slots], refs[slots:]
    up_ref, ub_ref, down_ref, first_ref, cot_ref, bd_ref, gain_ref, shift_ref, *refs = refs
    act_ref, slope_ref, out_ref, gsum_ref, gbranch_ref, vec_ref = refs
    hidden_units(n_refs, up_ref, ub_ref, act_ref, slope_ref)
    _, padded, width = cot_ref.shape
    row = lax.broadcasted_iota(jnp.int32, (padded, width), 0)
    gain = flat_line(gain_ref)
    sums = [jnp.zeros((1, width), F32)] * 3
    for slot, n_ref in enumerate(n_refs):
        part = slice(slot * padded, (slot + 1) * padded)
        count = count_ref[slot]
        keep = ((row < MEM + count) | (row >= rows - MEM)) & (row < rows) & (count > 0)
        branch = first_ref[part, :] + nn(act_ref[part, :], down_ref[...])
        summed = n_ref[...].astype(F32) + branch + flat_line(bd_ref)
        center = summed - rowmean(summed)
        rstd = lax.rsqrt(rowmean(center * center) + EPSILON)
        xhat = center * rstd
        out_ref[slot] = jnp.where(keep, xhat * gain + flat_line(shift_ref), 0.0).astype(BF)[:rows]
        g_out = jnp.where(keep, cot_ref[slot].astype(F32), 0.0)
        g_xhat = g_out * gain
        g_sum = rstd * (g_xhat - rowmean(g_xhat) - xhat * rowmean(g_xhat * xhat))
        gsum_ref[part, :] = g_sum
        gbranch_ref[part, :] = g_sum.astype(BF)
        new = (colsum(g_out * xhat), colsum(g_out), colsum(g_sum))
        sums = [a + b for a, b in zip(sums, new)]
    vec_ref[...] = jnp.concatenate(sums + [jnp.zeros((5, width), F32)])


def ffn_first(normed, own, after):
    total, width = len(normed) * normed[0].shape[0], normed[0].shape[1]
    acts = shape_of((total, own[0].shape[1]), BF)
    return kernel_call(
        functools.partial(ffn_first_kernel, len(normed)),
        7.5,
        [*normed, *own],
        [acts, acts, shape_of((total, width), F32)],
        after=after,
        vmem=FFN_MIB,
    )


def ffn_last(rows, count, normed, others, first, cot, vectors):
    total, width = first.shape
    acts = shape_of((total, others[0].shape[1]), BF)
    return kernel_call(
        functools.partial(ffn_last_kernel, rows, len(normed)),
        10.5,
        [count, *normed, *others, first, cot, *vectors],
        [
            acts,
            acts,
            shape_of((len(normed), rows, width), BF),
            shape_of(first.shape, F32),
            shape_of(first.shape, BF),
            shape_of((8, width), F32),
        ],
        scalars=1,
        vmem=FFN_MIB,
        far=(2,),
    )


def store_half(piece_ref, values, step, half, unit, shards):
    per = values.shape[0] // unit
    for i in range(per):
        block = step * per + i
        shard, y = block // 2, block % 2
        low, high = shard % 2, shard // 2
        place = jnp.where(half == 0, low * 2 + y, y * 2 + low) * (shards // 2) + high
        piece_ref[tile_rows(place * unit, unit), :] = values[i * unit : (i + 1) * unit].astype(BF)


def block_start(shards, j, half, size):
    return half * size if shards == 2 else (half * 2 + j) * size


def down_grad_kernel(unit, shards, other, at, table_ref, act0_ref, act1_ref, g_ref, piece_ref):
    half = table_ref[at] ^ other
    size = piece_ref.shape[0] // 2
    for j, act_ref in enumerate((act0_ref, act1_ref)):
        act = act_ref[:, tile_lanes(block_start(shards, j, half, size), size)]
        store_half(piece_ref, tn(act, g_ref[...]), j, half, unit, shards)


def down_grad(links, other, acts, g_branch, every, after):
    shards = links.shards
    return kernel_call(
        functools.partial(down_grad_kernel, every // shards // 4, shards, other, links.at("core")),
        4,
        [links.table, *acts, g_branch],
        shape_of((every // 2, g_branch.shape[1]), BF),
        scalars=1,
        after=after,
        vmem=FFN_MIB,
    )


def up_grad_kernel(unit, shards, slots, other, at_core, table_ref, g_ref, *refs):
    n_refs, refs = refs[:slots], refs[slots:]
    slope0_ref, slope1_ref, down0_ref, up0_ref, down1_ref, up1_ref, *so_far, piece_ref, gb_ref, gn_ref, pre_ref = refs
    half = table_ref[at_core] ^ other
    size = piece_ref.shape[0] // 2
    cut = math.gcd(256, size)
    for j, (slope_ref, down_ref, up_ref) in enumerate(
        ((slope0_ref, down0_ref, up0_ref), (slope1_ref, down1_ref, up1_ref))
    ):
        start = block_start(shards, j, half, size)
        for at in range(0, size, cut):
            g_pre = nt(g_ref[...], down_ref[tile_rows(start + at, cut), :])
            g_pre = g_pre * slope_ref[:, tile_lanes(start + at, cut)].astype(F32)
            pre_ref[:, at : at + cut] = g_pre.astype(BF)
        normed = jnp.concatenate([ref[...] for ref in n_refs])
        store_half(piece_ref, tn(pre_ref[...], normed), j, half, unit, shards)
        gb_ref[:, j * size : (j + 1) * size] = colsum(pre_ref[...].astype(F32))
        share = nt(pre_ref[...], up_ref[:, tile_lanes(start, size)])
        if j:
            gn_ref[...] += share
        else:
            gn_ref[...] = so_far[0][...] + share if so_far else share


def up_grad(links, other, g_branch, normed, slopes, weights, every, so_far, after):
    total, width = g_branch.shape
    shards = links.shards
    return kernel_call(
        functools.partial(up_grad_kernel, every // shards // 4, shards, len(normed), other, links.at("core")),
        9.5,
        [links.table, g_branch, *normed, *slopes, *weights, *so_far],
        [
            shape_of((every // 2, width), BF),
            shape_of((1, every // 2), F32),
            shape_of((total, width), F32),
        ],
        scalars=1,
        after=after,
        scratch_shapes=[pltpu.VMEM((total, every // 4), BF)],
        vmem=UP_MIB,
    )


def proj_grad_kernel(slots, gsum_ref, gn_ref, wp_ref, gain_ref, *refs):
    xhat_refs, rstd_refs, ctx_refs = (refs[i * slots : (i + 1) * slots] for i in range(3))
    gpre_ref, gctx_ref, gw_ref, vec_ref, attn_ref = refs[3 * slots :]
    padded, width = xhat_refs[0].shape
    sums = [jnp.zeros((1, width), F32)] * 3
    for slot in range(slots):
        part = slice(slot * padded, (slot + 1) * padded)
        g_normed = gsum_ref[part, :] + gn_ref[part, :]
        xhat = xhat_refs[slot][...].astype(F32)
        g_xhat = g_normed * flat_line(gain_ref)
        g_pre = rstd_refs[slot][...] * (g_xhat - rowmean(g_xhat) - xhat * rowmean(g_xhat * xhat))
        gpre_ref[slot] = g_pre
        g_attn = g_pre.astype(BF)
        attn_ref[part, :] = g_attn
        gctx_ref[slot] = nt(g_attn, wp_ref[...]).astype(BF)
        new = (colsum(g_normed * xhat), colsum(g_normed), colsum(g_pre))
        sums = [a + b for a, b in zip(sums, new)]
    gw_ref[...] = tn(jnp.concatenate([ref[...] for ref in ctx_refs]), attn_ref[...]).astype(BF)
    vec_ref[...] = jnp.concatenate(sums + [jnp.zeros((5, width), F32)])


def proj_grad(g_sum, g_norm, wp, gain, xhat, rstd, ctx, after):
    slots, (padded, width) = len(xhat), xhat[0].shape
    return kernel_call(
        functools.partial(proj_grad_kernel, slots),
        4,
        [g_sum, g_norm, wp, gain, *xhat, *rstd, *ctx],
        [
            shape_of((slots, padded, width), F32),
            shape_of((slots, padded, width), BF),
            shape_of((width, width), BF),
            shape_of((8, width), F32),
        ],
        after=after,
        scratch_shapes=[pltpu.VMEM((slots * padded, width), BF)],
        vmem=UP_MIB,
    )


def attend_back_kernel(rows, pair, slots, at_core, table_ref, count_ref, g_ref, *rest):
    arrays, rest = rest[: 5 * slots], rest[5 * slots :]
    x_ref = None
    if len(rest) > 1:
        x_ref, before_ref, *beside, d_ref, send_ref, keep_ref, vec_ref = rest
    else:
        (d_ref,) = rest
    padded = d_ref.shape[1]
    lanes = slice(pair * PAIR, (pair + 1) * PAIR)
    lane = lax.broadcasted_iota(jnp.int32, (padded, PAIR), 1)
    one = jnp.ones((), BF)
    zero = jnp.zeros((), BF)
    for slot in range(slots):
        bias = key_bias(count_ref[slot], rows, padded)
        g = g_ref[slot, :, lanes]
        q, extra, k, v, ctx = (ref[:, lanes] for ref in arrays[slot::slots])
        products = g.astype(F32) * ctx.astype(F32)
        parts = []
        for head in range(2):
            own = (lane < HEAD) if head == 0 else (lane >= HEAD)
            aux = HEAD if head == 0 else 0
            delta = -jnp.sum(jnp.where(own, products, 0.0), -1, keepdims=True)
            high = delta.astype(BF)
            low = (delta - high.astype(F32)).astype(BF)
            after = (lane > aux) & (lane < aux + 4)
            k_more = jnp.where(own, k, jnp.where(lane == aux, bias, jnp.where(after, one, zero)))
            v_more = jnp.where(own, v, jnp.where((lane >= aux) & (lane < aux + 2), one, zero))
            q_more = jnp.where(own, q, extra)
            g_more = jnp.where(own, g, jnp.where(lane == aux, high, jnp.where(lane == aux + 1, low, zero)))
            probs = jnp.exp(nt(k_more, q_more))
            g_scores = (probs * nt(v_more, g_more)).astype(BF)
            parts.append((tn(g_scores, k_more), nn(g_scores, q_more), nn(probs.astype(BF), g_more)))
        g_q, g_k, g_v = (jnp.where(lane < HEAD, a, b) for a, b in zip(*parts))
        g_q = (g_q.astype(BF).astype(F32) * (1.0 / math.sqrt(HEAD))).astype(BF)
        for i, part in enumerate((g_q, g_k.astype(BF), g_v.astype(BF))):
            d_ref[slot, :, i * PAIR : (i + 1) * PAIR] = part
    if x_ref is None:
        return
    both = slots * padded
    d = [ref[...].reshape(both, 3 * PAIR) for ref in (before_ref, d_ref)]
    d = jnp.concatenate(d, axis=1)
    g_weights = tn(x_ref[...].reshape(both, x_ref.shape[2]), d).astype(BF)
    vec_ref[...] = colsum(d.astype(F32))
    half = g_weights.shape[0] // 2
    first, second = (beside[0][...], g_weights) if beside else (g_weights[:half], g_weights[half:])

    @pl.when(table_ref[at_core] == 0)
    def _():
        keep_ref[...] = first
        send_ref[...] = second

    @pl.when(table_ref[at_core] == 1)
    def _():
        keep_ref[...] = second
        send_ref[...] = first


def attend_back(links, rows, pair, count, x, g_ctx, arrays, before, beside, after):
    slots, padded, width = x.shape
    operands = [links.table, count, g_ctx, *[t for of_slots in arrays for t in of_slots]]
    outs = [shape_of((slots, padded, 3 * PAIR), BF)]
    if before is not None:
        operands += [x, before, *beside]
        part = shape_of((width if beside else width // 2, 6 * PAIR), BF)
        outs += [part, part, shape_of((1, 6 * PAIR), F32)]
    return kernel_call(
        functools.partial(attend_back_kernel, rows, pair, slots, links.at("core")),
        5 if before is None else 7,
        operands,
        outs,
        scalars=2,
        after=after,
        vmem=BACK_MIB,
    )


def in_lanes(pairs, i):
    return jnp.concatenate([p[..., i * PAIR : (i + 1) * PAIR] for p in pairs], axis=-1)


def input_grad_kernel(many, gpre_ref, *refs):
    d_refs, w_refs, out_ref = refs[:many], refs[many : many + 3], refs[-1]
    slots, rows, _ = out_ref.shape
    for slot in range(slots):
        total = gpre_ref[slot]
        for i, w_ref in enumerate(w_refs):
            total = total + nt(in_lanes([d[slot] for d in d_refs], i), w_ref[...])
        out_ref[slot] = total[:rows]


def input_grad(shape, g_pre, parts, weights, after):
    return kernel_call(
        functools.partial(input_grad_kernel, len(parts)),
        4.5,
        [g_pre, *parts, *weights],
        shape_of(shape, F32),
        after=after,
        far=(0,),
    )


class Links:
    def __init__(self, items, shards):
        self.items, self.shards = items, shards
        self.joint = lax.axis_index("dp") * shards + lax.axis_index("seg")
        self.core = shards
        self.y = 2 * shards
        self.seg = [1 << i for i in range(shards.bit_length() - 1)]
        self.z = [shards << i for i in range(2, items.bit_length() - 1)]
        first = self.seg[0] if self.seg else self.y
        self.steps = (
            [(self.core, self.core), (first, self.y), (self.y, first)]
            + [(m, m) for m in reversed(self.seg[1:])]
            + [(m, m) for m in self.z]
        )
        self.numbers = {"core": self.bit(self.core, self.core), "seg": lax.axis_index("seg")}
        for masks in [*self.steps, (self.z[0], self.y), (self.y, self.z[0]), (self.y, self.y)]:
            self.numbers[masks] = self.bit(*masks)
        for masks in self.steps:
            self.numbers["own", masks] = self.keep_own(masks)
        self.names = list(self.numbers)
        self.table = jnp.stack(list(self.numbers.values())).astype(jnp.int32)

    def at(self, name):
        return self.names.index(name)

    def swap(self, value, mask0, mask1):
        count = self.items * self.shards
        pairs = [(i, i ^ (mask1 if i & self.core else mask0)) for i in range(count)]
        return lax.ppermute(value, JOINT, pairs)

    def bit(self, mask0, mask1):
        on_core1 = (self.joint & self.core) != 0
        return jnp.where(on_core1, (self.joint & mask1) != 0, (self.joint & mask0) != 0).astype(jnp.int32)

    def keep_own(self, masks):
        own = [mask in self.seg for mask in masks]
        on_core1 = (self.joint & self.core) != 0
        return jnp.where(jnp.where(on_core1, own[1], own[0]), 0, self.bit(*masks))


def tiled(rows):
    return rows % 16 == 0


def ordered(late, a, b, axis=0):
    return jnp.concatenate([jnp.where(late, b, a), jnp.where(late, a, b)], axis=axis)


def add_halves(links, name, held, got, small, after):
    rows, width = held.shape
    half = rows // 2
    extra = 0 if small is None else small.shape[0]
    if not tiled(half):
        keep = links.numbers[name]
        total = held + got[:rows]
        send = lax.dynamic_slice_in_dim(total, (1 - keep) * half, half)
        held = lax.dynamic_slice_in_dim(total, keep * half, half)
        if extra:
            small = small + got[rows:]
            send = jnp.concatenate([send, small])
        return send, held, small
    at = links.at(name)

    def kernel(table_ref, held_ref, got_ref, *rest):
        keep = table_ref[at]
        if extra:
            small_in, send_ref, keep_out, small_ref = rest
            small_ref[...] = small_in[...] + got_ref[rows:, :]
            send_ref[half:, :] = small_ref[...]
        else:
            send_ref, keep_out = rest
        other, mine = tile_rows((1 - keep) * half, half), tile_rows(keep * half, half)
        send_ref[:half, :] = held_ref[other, :] + got_ref[other, :]
        keep_out[...] = held_ref[mine, :] + got_ref[mine, :]

    outs = [shape_of((half + extra, width), BF), shape_of((half, width), BF)]
    smalls = [] if small is None else [small]
    out = kernel_call(
        kernel,
        1,
        [links.table, held, got, *smalls],
        outs + [like(t) for t in smalls],
        scalars=1,
        after=after,
        vmem=PASS_MIB,
    )
    return (*out, None)[:3]


def add_whole(held, got, small, after):
    rows, width = held.shape
    extra = 0 if small is None else small.shape[0]
    if not tiled(rows):
        piece = held[:rows] + got[:rows]
        if small is None:
            return piece, None
        small = small + got[rows:]
        return jnp.concatenate([piece, small]), small

    def kernel(held_ref, got_ref, *rest):
        if extra:
            small_in, piece_ref, small_ref = rest
            small_ref[...] = small_in[...] + got_ref[rows:, :]
            piece_ref[rows:, :] = small_ref[...]
        else:
            (piece_ref,) = rest
        piece_ref[:rows, :] = held_ref[...] + got_ref[:rows, :]

    smalls = [] if small is None else [small]
    out = kernel_call(
        kernel,
        1,
        [held, got, *smalls],
        [shape_of((rows + extra, width), BF)] + [like(t) for t in smalls],
        after=after,
        vmem=PASS_MIB,
    )
    return (*out, None)[:2]


def add_apart(held, got, rows, after):
    if not tiled(rows):
        both = held + got
        return both[:rows], both[rows:]

    def kernel(held_ref, got_ref, piece_ref, small_ref):
        piece_ref[...] = held_ref[:rows, :] + got_ref[:rows, :]
        small_ref[...] = held_ref[rows:, :] + got_ref[rows:, :]

    outs = [shape_of((n, held.shape[1]), BF) for n in (rows, held.shape[0] - rows)]
    return kernel_call(kernel, 1, [held, got], outs, after=after, vmem=PASS_MIB)


def add_pairs(pieces, gots, after):
    if not tiled(pieces[0].shape[0]):
        return jnp.stack([a + b for a, b in zip(pieces, gots)])
    many = len(pieces)

    def kernel(*refs):
        for i in range(many):
            refs[-1][i] = refs[i][...] + refs[many + i][...]

    out = shape_of((many, *pieces[0].shape), BF)
    return kernel_call(kernel, 1, [*pieces, *gots], out, after=after, vmem=PASS_MIB)


def join(links, name, piece, got, after):
    rows, width = piece.shape[-2:]
    if not tiled(rows):
        return ordered(links.numbers[name] == 1, piece, got, axis=-2)
    at = links.at(name)

    def kernel(table_ref, piece_ref, got_ref, out_ref):
        late = table_ref[at]
        mine, other = tile_rows(late * rows, rows), tile_rows((1 - late) * rows, rows)
        for i in [()] if piece.ndim == 2 else [(i,) for i in range(piece.shape[0])]:
            out_ref[(*i, mine, slice(None))] = piece_ref[i]
            out_ref[(*i, other, slice(None))] = got_ref[i]

    out = shape_of((*piece.shape[:-2], 2 * rows, width), BF)
    return kernel_call(
        kernel, 1, [links.table, piece, got], out, scalars=1, after=after, vmem=PASS_MIB
    )


class Sum:
    def __init__(self, links, relative, halves, small=None):
        self.links, self.relative, self.small = links, relative, small
        self.halves = halves
        self.adding = links.steps
        self.passing = list(self.way_back(links.steps[:-1]))
        self.held = self.piece = self.flying = None
        self.place = 0

    def way_back(self, steps):
        links = self.links
        for step in reversed(steps):
            crosses = [mask in links.seg for mask in step]
            if self.relative and crosses[0]:
                if not crosses[1]:
                    yield (links.y, links.y)
            elif not (self.relative and crosses[1]):
                yield step

    def advance(self, after=()):
        links, index = self.links, self.place
        self.place += 1
        last = len(self.adding) - 1
        if index == 0:
            send, self.held = self.halves
        elif index < last:
            name = self.adding[index]
            name = ("own", name) if self.relative else name
            send, self.held, self.small = add_halves(links, name, self.held, self.flying, self.small, after)
        elif index == last:
            send, self.small = add_whole(self.held, self.flying, self.small, after)
            self.held = send
        elif index == last + 1:
            rows = self.held.shape[0] - (0 if self.small is None else self.small.shape[0])
            if self.small is None:
                self.piece, _ = add_whole(self.held, self.flying, None, after)
            else:
                self.piece, self.small = add_apart(self.held, self.flying, rows, after)
            send = self.piece
        else:
            send = self.piece = join(links, self.passing[index - last - 2], self.piece, self.flying, after)
        step = self.adding[index] if index <= last else self.passing[index - last - 1]
        self.flying = links.swap(send, *step)
        return [send]

    def left(self):
        return len(self.adding) + len(self.passing) - self.place

    def finish(self, after=()):
        while self.left():
            self.advance(after)
        return self.piece, self.flying


class Merged:
    def __init__(self, links, sums):
        self.links, self.sums = links, sums
        self.passing = sums[0].passing
        self.place = 0

    def advance(self, after=()):
        index = self.place
        self.place += 1
        if index == 0:
            for s in self.sums:
                while s.place < len(s.adding):
                    s.advance(after)
            self.piece = add_pairs([s.held for s in self.sums], [s.flying for s in self.sums], after)
        else:
            self.piece = join(self.links, self.passing[index - 1], self.piece, self.flying, after)
        self.flying = self.links.swap(self.piece, *self.passing[index])
        return [self.piece]

    def left(self):
        return len(self.passing) - self.place

    def finish(self, after=()):
        while self.left():
            self.advance(after)
        return self.piece, self.flying


class Gather:
    def __init__(self, links, up, up_bias, down):
        self.links = links
        width, hidden = up.shape
        self.width, self.hidden = width, hidden
        z, y, core = links.z[0], links.y, links.core
        self.steps = [(links.seg[0], links.seg[0]), (z, y), (y, z), (core, core)]
        self.place = 0
        places = [links.at(name) for name in ("core", (y, z), (z, y))]
        self.wide = hidden // width
        cut, deep, wide = width // 8, hidden // 8, self.wide
        rows = wide * cut + deep + 16

        def kernel(table_ref, bias_ref, up_ref, down_ref, out_ref, up_cut, down_cut, sems):
            place = sum(table_ref[at] * weight for at, weight in zip(places, (4, 2, 1)))
            copies = [
                pltpu.make_async_copy(up_ref.at[tile_rows(place * cut, cut), :], up_cut, sems.at[0]),
                pltpu.make_async_copy(down_ref.at[tile_rows(place * deep, deep), :], down_cut, sems.at[1]),
            ]
            for copy in copies:
                copy.start()
            lines, rest = [], flat_line(bias_ref)
            for _ in range(3):
                term = rest.astype(BF).astype(F32)
                lines += [term[:, i * width : (i + 1) * width] for i in range(wide)]
                rest = rest - term
            lines.append(jnp.zeros((16 - len(lines), width), F32))
            out_ref[rows - 16 :, :] = jnp.concatenate(lines).astype(BF)
            for copy in copies:
                copy.wait()
            for i in range(wide):
                out_ref[i * cut : (i + 1) * cut, :] = up_cut[:, i * width : (i + 1) * width]
            out_ref[wide * cut : wide * cut + deep, :] = down_cut[...]

        anywhere = pl.BlockSpec(memory_space=pl.ANY)
        self.piece = pl.pallas_call(
            kernel,
            in_specs=[pl.BlockSpec(memory_space=pltpu.SMEM), pl.BlockSpec(memory_space=pltpu.VMEM), anywhere, anywhere],
            out_shape=shape_of((rows, width), BF),
            scratch_shapes=[
                pltpu.VMEM((cut, hidden), BF),
                pltpu.VMEM((deep, width), BF),
                pltpu.SemaphoreType.DMA((2,)),
            ],
            compiler_params=pltpu.CompilerParams(vmem_limit_bytes=4 * 2**20),
        )(links.table, up_bias, *(pltpu.with_memory_space_constraint(t, pltpu.HBM) for t in (up, down)))

    def advance(self, after=()):
        index = self.place
        self.place += 1
        if index == 1:
            self.piece = self.flying[None]
        elif index > 1:
            self.piece = join(self.links, self.steps[index - 1], self.piece, self.flying, after)
        self.flying = self.links.swap(self.piece, *self.steps[index])
        return [self.piece]

    def finish(self, after=()):
        while self.place < len(self.steps):
            self.advance(after)
        width, hidden, wide = self.width, self.hidden, self.wide
        cut, deep = width // 8, hidden // 8
        rows = wide * cut + deep + 16
        piece, got = (t.reshape(4 * rows, width) for t in (self.piece, self.flying))

        at_core = self.links.at("core")

        def kernel(table_ref, piece_ref, got_ref, up_ref, bias_ref, down_ref):
            for i in range(8):
                ref = piece_ref if i < 4 else got_ref
                start = (i % 4) * rows
                place = (table_ref[at_core] ^ (i // 4)) * 4 + i % 4
                at = tile_rows(place * cut, cut)
                for j in range(wide):
                    up_ref[at, j * width : (j + 1) * width] = ref[start + j * cut : start + (j + 1) * cut, :]
                down_ref[tile_rows(place * deep, deep), :] = ref[start + wide * cut : start + wide * cut + deep, :]
            lines = piece_ref[rows - 16 : rows, :].astype(F32)
            parts = [sum(lines[i * wide + j : i * wide + j + 1] for i in range(3)) for j in range(wide)]
            bias_ref[...] = jnp.concatenate(parts, 1).reshape(hidden)

        return kernel_call(
            kernel,
            2,
            [self.links.table, piece, got],
            [shape_of((width, hidden), BF), shape_of((hidden,), F32), shape_of((hidden, width), BF)],
            scalars=1,
            after=after,
            vmem=10,
        )


class GatherAny:
    def __init__(self, *args):
        self.args = args

    def advance(self, after=()):
        return []

    def finish(self, after=()):
        return other_shards(*self.args)


def other_shards(links, up, up_bias, down):
    shards = links.shards
    hidden = down.shape[0]
    ups = lax.all_gather(up, "seg", axis=0)
    downs = lax.all_gather(down, "seg", axis=0)
    biases = lax.all_gather(up_bias.reshape(1, -1), "seg", axis=0)
    order = lax.axis_index("seg") ^ jnp.arange(1, shards)
    ups = jnp.moveaxis(jnp.take(ups, order, axis=0), 0, 1).reshape(up.shape[0], -1)
    return ups, jnp.take(biases, order, axis=0).reshape(-1), jnp.take(downs, order, axis=0).reshape(-1, down.shape[1])


def pack_small(links, vec_ffn, vec_attn, g_lines, bias_send, bias_keep, send):
    width = vec_ffn.shape[1]
    shards = links.shards
    if shards != 2 or bias_send.shape[1] != 2 * width or not tiled(send.shape[0]):
        halves = ordered(links.numbers["core"] == 1, bias_keep, bias_send).reshape(2, shards, -1)
        by_shard = jnp.moveaxis(halves, 0, 1).reshape(shards, -1)
        by_shard = jnp.take(by_shard, jnp.arange(shards) ^ lax.axis_index("seg"), axis=0).reshape(-1, width)
        lines = [
            in_lanes([g[:, i * 3 * PAIR : (i + 1) * 3 * PAIR] for g in g_lines for i in range(2)], i) for i in (0, 2)
        ]
        small = jnp.concatenate([vec_ffn[:3], vec_attn[:3], *lines, by_shard])
        pad = -(-small.shape[0] // 16) * 16 - small.shape[0]
        small = jnp.pad(small, ((0, pad), (0, 0))).astype(BF)
        return jnp.concatenate([send, small]), small
    at_core, at_seg = links.at("core"), links.at("seg")
    rows = send.shape[0]

    def kernel(table_ref, send_ref, ffn_ref, attn_ref, *rest):
        line_refs, (bias_send_ref, bias_keep_ref, out_ref, small_ref, rows_ref) = rest[:-5], rest[-5:]
        rows_ref[...] = jnp.zeros_like(rows_ref)
        rows_ref[0:3, :] = ffn_ref[0:3, :]
        rows_ref[3:6, :] = attn_ref[0:3, :]
        for g, line_ref in enumerate(line_refs):
            for i in range(2):
                for row, part in ((6, 0), (7, 2)):
                    at = (3 * i + part) * PAIR
                    place = (2 * g + i) * PAIR
                    rows_ref[row : row + 1, place : place + PAIR] = line_ref[:, at : at + PAIR]
        for ref, half in ((bias_send_ref, 1 - table_ref[at_core]), (bias_keep_ref, table_ref[at_core])):
            for i in range(2):
                row = 8 + 2 * (table_ref[at_seg] ^ i) + half
                rows_ref[pl.ds(row, 1), :] = ref[:, i * width : (i + 1) * width]
        small_ref[...] = rows_ref[...].astype(BF)
        out_ref[:rows, :] = send_ref[...]
        out_ref[rows:, :] = small_ref[...]

    return kernel_call(
        kernel,
        1,
        [links.table, send, vec_ffn, vec_attn, *g_lines, bias_send, bias_keep],
        [shape_of((rows + 16, width), BF), shape_of((16, width), BF)],
        scalars=1,
        scratch_shapes=[pltpu.VMEM((16, width), F32)],
        vmem=PASS_MIB,
    )


def ffn_outputs(links, piece, got):
    _, rows, width = piece.shape
    if rows % PAIR:
        down, up = ordered(links.numbers["core"] == 1, piece, got, axis=1).astype(F32)
        return down, up.T
    at_core = links.at("core")

    def kernel(table_ref, piece_ref, got_ref, down_ref, up_ref):
        def store(*refs):
            for half, ref in enumerate(refs):
                part = slice(half * rows, (half + 1) * rows)
                down_ref[part, :] = ref[0].astype(F32)
                up_ref[:, part] = ref[1].astype(F32).T

        pl.when(table_ref[at_core] == 0)(lambda: store(piece_ref, got_ref))
        pl.when(table_ref[at_core] == 1)(lambda: store(got_ref, piece_ref))

    return kernel_call(
        kernel,
        5,
        [links.table, piece, got],
        [shape_of((2 * rows, width), F32), shape_of((width, 2 * rows), F32)],
        scalars=1,
        far=(0, 1),
    )


def attention_outputs(links, first, groups, small, hidden):
    width = first[0].shape[1]
    wide = 2 * PAIR
    at_core, at_seg = links.at("core"), links.at("seg")
    lines = hidden // width

    def kernel(table_ref, *refs):
        *pairs, small_ref = refs[: 2 * len(groups) + 3]
        outs = refs[2 * len(groups) + 3 :]
        proj_out, square_outs, vector_outs, bias_out = outs[0], outs[1:4], outs[4:12], outs[12]

        def store(group, halves):
            rows = width // len(halves)
            for half, ref in enumerate(halves):
                for i, out_ref in enumerate(square_outs):
                    for j in range(2):
                        at = (3 * j + i) * PAIR
                        place = group * wide + j * PAIR
                        values = ref[:, at : at + PAIR].astype(F32)
                        out_ref[half * rows : (half + 1) * rows, place : place + PAIR] = values

        def store_all(core):
            proj_out[...] = pairs[core][...].astype(F32)
            store(0, [pairs[1 - core]])
            for g in range(len(groups)):
                store(g + 1, [pairs[2 + 2 * g + core], pairs[2 + 2 * g + 1 - core]])

        pl.when(table_ref[at_core] == 0)(lambda: store_all(0))
        pl.when(table_ref[at_core] == 1)(lambda: store_all(1))
        rows = small_ref[...].astype(F32)
        for i, out_ref in enumerate(vector_outs):
            out_ref[...] = rows[i : i + 1].reshape(width)
        seg = table_ref[at_seg]
        for shard in range(2):

            @pl.when(seg == shard)
            def _():
                at = 8 + shard * lines
                parts = [rows[at + i : at + i + 1] for i in range(lines)]
                bias_out[...] = jnp.concatenate(parts, 1).reshape(hidden)

    square, vector = shape_of((width, width), F32), shape_of((width,), F32)
    return kernel_call(
        kernel,
        3,
        [links.table, *first, *[t for pair in groups for t in pair], small],
        [square] * 4 + [vector] * 8 + [shape_of((hidden,), F32)],
        scalars=1,
        far=range(13),
    )


def attention_outputs_any(links, first, groups, small, hidden):
    on_core1 = links.numbers["core"] == 1
    whole = [ordered(on_core1, *pair) for pair in (first, *groups)]
    width = whole[0].shape[1]
    grads = [whole[0][width:], *whole[1:]]
    pairs = [g[:, i * 3 * PAIR : (i + 1) * 3 * PAIR] for g in grads for i in range(2)]
    small = small.astype(F32)
    biases = small[8 : 8 + hidden * links.shards // width].reshape(links.shards, -1)
    bias = lax.dynamic_index_in_dim(biases, lax.axis_index("seg"), keepdims=False)
    squares = [in_lanes(pairs, i).astype(F32) for i in range(3)]
    return [whole[0][:width].astype(F32), *squares, *[small[i] for i in range(8)], bias]


def in_halves(array, axis, shards):
    shape = list(array.shape)
    parts = array.reshape(shape[:axis] + [shards, 2, -1] + shape[axis + 1 :])
    return jnp.moveaxis(parts, axis + 1, axis).reshape(shape)


def body(
    activations,
    tok_count,
    w_query,
    w_key,
    w_value,
    w_proj,
    b_query,
    b_value,
    b_proj,
    gain_attn,
    shift_attn,
    w_up,
    b_up,
    w_down,
    b_down,
    gain_ffn,
    shift_ffn,
    cotangent,
    items,
    shards,
):
    slots, rows, width = activations.shape
    padded = -(-rows // 16) * 16
    links = Links(items, shards)
    count = tok_count[:, 0]
    more = ((0, 0), (0, padded - rows), (0, 0))
    x = jnp.pad(activations, more)
    cot = jnp.pad(cotangent, more)
    own = (w_up, b_up, w_down)
    hidden = w_up.shape[1]
    every = hidden * shards
    weights = (Gather if shards == 2 and links.z else GatherAny)(links, *own)

    squares = [w_query, w_key, w_value, w_proj]
    vectors = [b_query, b_value, b_proj, gain_attn, shift_attn]
    state, done = [], [cot]
    for slot in range(slots):
        state.append(attend(rows, slot, count, x, squares, vectors, weights.advance(done) + done))
        done = [state[-1][-1]]
    q, extra, k, v, ctx, normed, xhat, rstd = zip(*state)
    act0, slope0, first = ffn_first(normed, own, weights.advance(done))
    others = weights.finish([first])
    act1, slope1, layer_out, g_sum, g_branch, vec_ffn = ffn_last(
        rows, count, normed, others, first, cot, [b_down, gain_ffn, shift_ffn]
    )
    acts, slopes = [act0, act1], [slope0, slope1]
    if shards == 2:
        pieces = [own[2], own[0], others[2], others[0]]
    else:
        acts, slopes = ([in_halves(jnp.concatenate(t, 1), 1, shards)] * 2 for t in (acts, slopes))
        ups = in_halves(jnp.concatenate([own[0], others[0]], 1), 1, shards)
        downs = in_halves(jnp.concatenate([own[2], others[2]]), 0, shards)
        pieces = [downs, ups, downs, ups]

    send = down_grad(links, 1, acts, g_branch, every, [])
    keep = down_grad(links, 0, acts, g_branch, every, [send])
    down_sum = Sum(links, True, (send, keep))
    after = down_sum.advance() + [keep]
    send, bias_send, so_far = up_grad(links, 1, g_branch, normed, slopes, pieces, every, [], after)
    after = down_sum.advance([bias_send])
    keep, bias_keep, g_norm = up_grad(
        links, 0, g_branch, normed, slopes, pieces, every, [so_far], after + [send]
    )
    up_sum = Sum(links, True, (send, keep))
    after = up_sum.advance() + down_sum.advance([bias_keep])
    g_pre, g_ctx, g_proj, vec_attn = proj_grad(
        g_sum, g_norm, w_proj, gain_attn, xhat, rstd, ctx, after
    )

    arrays = [q, extra, k, v, ctx]
    done = [vec_attn]
    d_parts, g_lines, sums = [], [], []
    plan = [[up_sum], [], [up_sum, down_sum], [up_sum, down_sum], [up_sum], []]
    for pair in range(width // PAIR):
        after = [t for s in plan[pair] for t in s.advance(done)] + done
        if pair % 2 == 0:
            (d,) = attend_back(links, rows, pair, count, x, g_ctx, arrays, None, [], after)
            done = [d]
        else:
            beside = [g_proj] if pair == 1 else []
            d, send, keep, lines = attend_back(
                links, rows, pair, count, x, g_ctx, arrays, d_parts[-1], beside, after
            )
            g_lines.append(lines)
            done = [lines]
            small = None
            if pair == width // PAIR - 1:
                send, small = pack_small(links, vec_ffn, vec_attn, g_lines, bias_send, bias_keep, send)
            sums.append(Sum(links, False, (send, keep), small))
            for later in plan[pair + 1 : pair + 4]:
                later.append(sums[-1])
        d_parts.append(d)
    ffn_sum = Merged(links, [down_sum, up_sum])
    after = [t for s in sums[::-1] for t in s.advance(done)]
    grad_input = input_grad(activations.shape, g_pre, d_parts, [w_query, w_key, w_value], after)
    waiting = [*sums[::-1], ffn_sum]
    while any(s.left() for s in waiting):
        for s in waiting:
            if s.left():
                s.advance([])
    grad_w_down, grad_w_up = ffn_outputs(links, *ffn_sum.finish())
    first, *groups = (s.finish() for s in sums)
    last = attention_outputs if shards == 2 and tiled(groups[0][0].shape[0]) else attention_outputs_any
    g_proj, g_query, g_key, g_value, *vectors, grad_b_up = last(links, first, groups, sums[-1].small, hidden)
    g_gain_ffn, g_shift_ffn, g_b_down, g_gain_attn, g_shift_attn, g_b_proj, g_b_query, g_b_value = vectors
    return (
        layer_out,
        grad_input,
        g_query,
        g_key,
        g_value,
        g_proj,
        g_b_query,
        g_b_value,
        g_b_proj,
        g_gain_attn,
        g_shift_attn,
        grad_w_up,
        grad_b_up,
        grad_w_down,
        g_b_down,
        g_gain_ffn,
        g_shift_ffn,
    )


def solution(mesh):
    rows, everywhere = P("dp", "seg", None), P()
    return jax.shard_map(
        functools.partial(body, items=mesh.shape["dp"], shards=mesh.shape["seg"]),
        mesh=mesh,
        in_specs=(rows, P("dp", "seg"))
        + (everywhere,) * 9
        + (P(None, "seg"), P("seg"), P("seg", None))
        + (everywhere,) * 3
        + (rows,),
        out_specs=(rows, rows)
        + (everywhere,) * 9
        + (P(None, "seg"), P("seg"), P("seg", None))
        + (everywhere,) * 3,
        check_vma=False,
    )
```

```python
import functools
import math

import jax
import jax.numpy as jnp
from jax import lax
from jax.experimental import pallas as pl
from jax.experimental.pallas import tpu as pltpu
from jax.sharding import PartitionSpec as P

HEAD = 64
MEM = 10
EPSILON = 1e-05
NEG_BIG = -1e30
PAIR = 2 * HEAD
BF = jnp.bfloat16
F32 = jnp.float32
VMEM_MIB = 16
PASS_MIB = 5
ATTEND_MIB = 9
FFN_MIB = 9
DOWN_MIB = 5
UP_MIB = 6
BACK_MIB = 5
JOINT = ("dp", "seg")
TOKEN = jax.ShapeDtypeStruct((8, PAIR), F32)
PLAN = (
    "down send", "down keep", "down", "up send", "down", "up keep", "proj", "down", "up", "pair", "up",
    "down", "pair", "pair", "down", "up", "heads 0", "pair", "heads 1", "heads 0", "up", "pair", "down back",
    "heads 0", "heads 1", "up", "pair", "heads 2", "heads 1", "layer", "heads 2", "down back", "heads 0",
    "heads 1", "heads 2", "up back", "heads 0", "input", "up back", "heads 1", "heads 2", "heads 0",
    "down back", "heads 2", "heads 1", "heads 0", "down out", "heads 2", "heads 1", "heads 0", "up back",
    "heads 2", "heads 1", "up out", "heads 0", "heads 2", "heads 1", "squares", "heads 2",
)


def nn(left, right):
    return jnp.dot(left, right, preferred_element_type=F32)


def tn(left, right):
    return lax.dot_general(left, right, (((0,), (0,)), ((), ())), preferred_element_type=F32)


def nt(left, right):
    return lax.dot_general(left, right, (((1,), (1,)), ((), ())), preferred_element_type=F32)


def colsum(values):
    return jnp.sum(values, 0, keepdims=True)


def rowmean(values):
    return jnp.mean(values, -1, keepdims=True)


def kernel_call(kernel, micros, operands, out_shape, scalars=0, after=(), scratch_shapes=(), vmem=VMEM_MIB, far=()):
    many = len(operands)
    anywhere = pl.BlockSpec(memory_space=pl.ANY)
    near = pl.BlockSpec(memory_space=pltpu.VMEM)

    def run(*refs):
        kernel(*refs[:many], *refs[many + len(after) :])

    specs = [pl.BlockSpec(memory_space=pltpu.SMEM) if i < scalars else near for i in range(many)]
    outs = out_shape if isinstance(out_shape, list) else [out_shape]
    outs = [t if i in far else pltpu.VMEM(t.shape, t.dtype) for i, t in enumerate(outs)]
    results = pl.pallas_call(
        run,
        in_specs=specs + [anywhere] * len(after),
        out_specs=[near] * len(outs),
        out_shape=outs,
        scratch_shapes=scratch_shapes,
        compiler_params=pltpu.CompilerParams(vmem_limit_bytes=vmem * 2**20),
        cost_estimate=pl.CostEstimate(
            flops=int(micros * 1.0e9), bytes_accessed=1 << 20, transcendentals=0
        ),
    )(*operands, *after)
    return results if isinstance(out_shape, list) else results[0]


def leaving_call(kernel, micros, operands, out_shape, parts, after, vmem):
    def run(*refs):
        ins, (out, token, buffer, sems) = refs[: len(operands)], refs[-4:]
        token[...] = jnp.zeros_like(token)
        copies = [pltpu.make_async_copy(buffer.at[part], out.at[part], sems.at[i]) for i, part in enumerate(parts)]
        kernel(lambda i: copies[i].start(), *ins, buffer)
        for copy in copies:
            copy.wait()

    near, anywhere = pl.BlockSpec(memory_space=pltpu.VMEM), pl.BlockSpec(memory_space=pl.ANY)
    return pl.pallas_call(
        run,
        in_specs=[near] * len(operands) + [anywhere] * len(after),
        out_specs=[pl.BlockSpec(memory_space=pltpu.HBM), near],
        out_shape=[pltpu.HBM(out_shape.shape, out_shape.dtype), TOKEN],
        scratch_shapes=[pltpu.VMEM(out_shape.shape, out_shape.dtype), pltpu.SemaphoreType.DMA((len(parts),))],
        compiler_params=pltpu.CompilerParams(vmem_limit_bytes=vmem * 2**20),
        cost_estimate=pl.CostEstimate(
            flops=int(micros * 1.0e9), bytes_accessed=1 << 20, transcendentals=0
        ),
    )(*operands, *after)


def shape_of(shape, dtype):
    return jax.ShapeDtypeStruct(shape, dtype)


def like(array):
    return shape_of(array.shape, array.dtype)


def flat_line(ref):
    return ref[...].reshape(1, -1)


def either(mask_ref, at, width):
    mask = jnp.concatenate([mask_ref[at : at + 1, :]] * (width // PAIR), 1) > 0.5

    def choose(one, zero):
        return jnp.where(jnp.broadcast_to(mask, one.shape), one, zero)

    return choose


def tile_rows(start, rows):
    return pl.ds(pl.multiple_of(start, 16), rows)


def tile_lanes(start, lanes):
    return pl.ds(pl.multiple_of(start, PAIR), lanes)


def key_bias(count, rows, padded):
    row = lax.broadcasted_iota(jnp.int32, (padded, PAIR), 0)
    valid = ((row < MEM + count) | (row >= rows - MEM)) & (row < rows)
    return jnp.where(valid, 0.0, NEG_BIG).astype(BF)


def attend_kernel(
    rows,
    slot,
    count_ref,
    x_ref,
    wq_ref,
    wk_ref,
    wv_ref,
    bq_ref,
    bv_ref,
    q_ref,
    aux_ref,
    k_ref,
    v_ref,
    ctx_ref,
    bias_ref,
):
    padded, width = x_ref.shape[1:]
    x = x_ref[slot]
    q_ref[...] = ((nn(x, wq_ref[...]) + flat_line(bq_ref)) * (1.0 / math.sqrt(HEAD))).astype(BF)
    k_ref[...] = nn(x, wk_ref[...]).astype(BF)
    v_ref[...] = (nn(x, wv_ref[...]) + flat_line(bv_ref)).astype(BF)
    lane = lax.broadcasted_iota(jnp.int32, (padded, PAIR), 1)
    bias_ref[...] = key_bias(count_ref[slot], rows, padded)
    bias = bias_ref[...]
    one = jnp.ones((), BF)
    zero = jnp.zeros((), BF)
    for pair in range(width // PAIR):
        lanes = slice(pair * PAIR, (pair + 1) * PAIR)
        q, k, v = q_ref[:, lanes], k_ref[:, lanes], v_ref[:, lanes]
        contexts, extras = [], []
        for head in range(2):
            own = (lane < HEAD) if head == 0 else (lane >= HEAD)
            aux = HEAD if head == 0 else 0
            at_aux = jnp.where(lane == aux, one, zero)
            scores = nt(
                jnp.where(own, q, at_aux),
                jnp.where(own, k, jnp.where(lane == aux, bias, zero)),
            )
            top = jnp.max(scores, -1, keepdims=True)
            exps = jnp.exp(scores - top).astype(BF)
            weighted = nn(exps, jnp.where(own, v, at_aux))
            total = weighted[:, aux : aux + 1]
            contexts.append(weighted * (1.0 / total))
            rest = -(top + jnp.log(total))
            high = rest.astype(BF)
            rest = rest - high.astype(F32)
            middle = rest.astype(BF)
            low = (rest - middle.astype(F32)).astype(BF)
            extras.append(
                jnp.where(
                    lane == aux + 1,
                    high,
                    jnp.where(lane == aux + 2, middle, jnp.where(lane == aux + 3, low, at_aux)),
                )
            )
        ctx_ref[:, lanes] = jnp.where(lane < HEAD, contexts[0], contexts[1]).astype(BF)
        aux_ref[:, lanes] = jnp.where(lane < HEAD, extras[1], extras[0])


def attend(rows, slot, count, x, weights, vectors, after):
    array = shape_of(x.shape[1:], BF)
    return kernel_call(
        functools.partial(attend_kernel, rows, slot),
        9,
        [count, x, *weights, *vectors],
        [array] * 5 + [shape_of((x.shape[1], PAIR), BF)],
        scalars=1,
        after=after,
        vmem=ATTEND_MIB,
    )


def first_norm_kernel(slots, x_ref, wp_ref, bp_ref, gain_ref, shift_ref, *refs):
    ctx_refs, normed_refs, xhat_refs, rstd_refs = (refs[i * slots : (i + 1) * slots] for i in range(4))
    for slot in range(slots):
        pre_norm = x_ref[slot].astype(F32) + nn(ctx_refs[slot][...], wp_ref[...]) + flat_line(bp_ref)
        center = pre_norm - rowmean(pre_norm)
        rstd = lax.rsqrt(rowmean(center * center) + EPSILON)
        xhat = center * rstd
        normed_refs[slot][...] = (xhat * flat_line(gain_ref) + flat_line(shift_ref)).astype(BF)
        xhat_refs[slot][...] = xhat.astype(BF)
        rstd_refs[slot][...] = rstd


def first_norm(x, wp, vectors, ctx, after):
    slots, padded, width = x.shape
    array, column = shape_of((padded, width), BF), shape_of((padded, 1), F32)
    out = kernel_call(
        functools.partial(first_norm_kernel, slots),
        3,
        [x, wp, *vectors, *ctx],
        [array] * (2 * slots) + [column] * slots,
        after=after,
        vmem=FFN_MIB,
    )
    return [out[i * slots : (i + 1) * slots] for i in range(3)]


def hidden_units(n_refs, up_ref, ub_ref, act_ref, slope_ref):
    size = up_ref.shape[1]
    bias = flat_line(ub_ref)
    cut = math.gcd(256, size)
    padded = n_refs[0].shape[0]
    for at in range(0, size, cut):
        part = slice(at, at + cut)
        for slot, n_ref in enumerate(n_refs):
            rows = slice(slot * padded, (slot + 1) * padded)
            pre = nn(n_ref[...], up_ref[:, part]) + bias[:, part]
            cdf = 0.5 + 0.5 * lax.erf(pre * math.sqrt(0.5))
            act_ref[rows, part] = (pre * cdf).astype(BF)
            slope = cdf + pre * (jnp.exp(-0.5 * (pre * pre)) * (1.0 / math.sqrt(2.0 * math.pi)))
            slope_ref[rows, part] = slope.astype(BF)


def ffn_first_kernel(slots, *refs):
    up_ref, ub_ref, down_ref, act_ref, slope_ref, sum_ref = refs[slots:]
    hidden_units(refs[:slots], up_ref, ub_ref, act_ref, slope_ref)
    sum_ref[...] = nn(act_ref[...], down_ref[...])


def ffn_last_kernel(rows, slots, count_ref, *refs):
    n_refs, refs = refs[:slots], refs[slots:]
    up_ref, ub_ref, down_ref, first_ref, cot_ref, bd_ref, gain_ref, shift_ref, *refs = refs
    act_ref, slope_ref, out_ref, gsum_ref, gbranch_ref, vec_ref = refs
    hidden_units(n_refs, up_ref, ub_ref, act_ref, slope_ref)
    padded, width = n_refs[0].shape
    row = lax.broadcasted_iota(jnp.int32, (padded, width), 0)
    gain = flat_line(gain_ref)
    sums = [jnp.zeros((1, width), F32)] * 3
    for slot, n_ref in enumerate(n_refs):
        part = slice(slot * padded, (slot + 1) * padded)
        count = count_ref[slot]
        keep = ((row < MEM + count) | (row >= rows - MEM)) & (row < rows) & (count > 0)
        branch = first_ref[part, :] + nn(act_ref[part, :], down_ref[...])
        summed = n_ref[...].astype(F32) + branch + flat_line(bd_ref)
        center = summed - rowmean(summed)
        rstd = lax.rsqrt(rowmean(center * center) + EPSILON)
        xhat = center * rstd
        out_ref[slot] = jnp.where(keep, xhat * gain + flat_line(shift_ref), 0.0).astype(BF)
        g_out = jnp.where(keep, cot_ref[slot].astype(F32), 0.0)
        g_xhat = g_out * gain
        g_sum = rstd * (g_xhat - rowmean(g_xhat) - xhat * rowmean(g_xhat * xhat))
        gsum_ref[part, :] = g_sum
        gbranch_ref[part, :] = g_sum.astype(BF)
        new = (colsum(g_out * xhat), colsum(g_out), colsum(g_sum))
        sums = [a + b for a, b in zip(sums, new)]
    vec_ref[...] = jnp.concatenate(sums + [jnp.zeros((5, width), F32)])


def ffn_first(normed, own, after):
    total, width = len(normed) * normed[0].shape[0], normed[0].shape[1]
    acts = shape_of((total, own[0].shape[1]), BF)
    return kernel_call(
        functools.partial(ffn_first_kernel, len(normed)),
        7.5,
        [*normed, *own],
        [acts, acts, shape_of((total, width), F32)],
        after=after,
        vmem=FFN_MIB,
    )


def ffn_last(rows, count, normed, others, first, cot, vectors):
    total, width = first.shape
    acts = shape_of((total, others[0].shape[1]), BF)
    return kernel_call(
        functools.partial(ffn_last_kernel, rows, len(normed)),
        10.5,
        [count, *normed, *others, first, cot, *vectors],
        [
            acts,
            acts,
            shape_of(cot.shape, BF),
            shape_of(first.shape, F32),
            shape_of(first.shape, BF),
            shape_of((8, width), F32),
        ],
        scalars=1,
        vmem=FFN_MIB,
    )


def slots_last(array, rows, after):
    slots, _, width = array.shape
    parts = row_parts(rows)

    def kernel(leave, in_ref, out_ref):
        for i, (part,) in enumerate(parts):
            for slot in range(slots):
                out_ref[part, slot, :] = in_ref[slot, part, :]
            leave(i)

    return leaving_call(kernel, 8, [array], shape_of((rows, slots, width), array.dtype), parts, after, 8)


def row_parts(rows):
    cut = rows // 32 * 16
    return [(slice(0, cut),), (slice(cut, rows),)]


def store_half(piece_ref, values, step, half, unit, shards):
    per = values.shape[0] // unit
    for i in range(per):
        block = step * per + i
        shard, y = block // 2, block % 2
        low, high = shard % 2, shard // 2
        place = jnp.where(half == 0, low * 2 + y, y * 2 + low) * (shards // 2) + high
        piece_ref[tile_rows(place * unit, unit), :] = values[i * unit : (i + 1) * unit].astype(BF)


def block_start(shards, j, half, size):
    return half * size if shards == 2 else (half * 2 + j) * size


def down_grad_kernel(unit, shards, other, at, table_ref, act0_ref, act1_ref, g_ref, piece_ref):
    half = table_ref[at] ^ other
    size = piece_ref.shape[0] // 2
    for j, act_ref in enumerate((act0_ref, act1_ref)):
        act = act_ref[:, tile_lanes(block_start(shards, j, half, size), size)]
        store_half(piece_ref, tn(act, g_ref[...]), j, half, unit, shards)


def down_grad(links, other, acts, g_branch, every, after):
    shards = links.shards
    return kernel_call(
        functools.partial(down_grad_kernel, every // shards // 4, shards, other, links.at("core")),
        4,
        [links.table, *acts, g_branch],
        shape_of((every // 2, g_branch.shape[1]), BF),
        scalars=1,
        after=after,
        vmem=DOWN_MIB,
    )


def up_grad_kernel(unit, shards, slots, other, at_core, table_ref, g_ref, *refs):
    n_refs, refs = refs[:slots], refs[slots:]
    slope0_ref, slope1_ref, down0_ref, up0_ref, down1_ref, up1_ref, *so_far, piece_ref, gb_ref, gn_ref, pre_ref = refs
    half = table_ref[at_core] ^ other
    size = piece_ref.shape[0] // 2
    cut = math.gcd(256, size)
    for j, (slope_ref, down_ref, up_ref) in enumerate(
        ((slope0_ref, down0_ref, up0_ref), (slope1_ref, down1_ref, up1_ref))
    ):
        start = block_start(shards, j, half, size)
        for at in range(0, size, cut):
            g_pre = nt(g_ref[...], down_ref[tile_rows(start + at, cut), :])
            g_pre = g_pre * slope_ref[:, tile_lanes(start + at, cut)].astype(F32)
            pre_ref[:, at : at + cut] = g_pre.astype(BF)
        normed = jnp.concatenate([ref[...] for ref in n_refs])
        store_half(piece_ref, tn(pre_ref[...], normed), j, half, unit, shards)
        gb_ref[:, j * size : (j + 1) * size] = colsum(pre_ref[...].astype(F32))
        share = nt(pre_ref[...], up_ref[:, tile_lanes(start, size)])
        if j:
            gn_ref[...] += share
        else:
            gn_ref[...] = so_far[0][...] + share if so_far else share


def up_grad(links, other, g_branch, normed, slopes, weights, every, so_far, after):
    total, width = g_branch.shape
    shards = links.shards
    return kernel_call(
        functools.partial(up_grad_kernel, every // shards // 4, shards, len(normed), other, links.at("core")),
        9.5,
        [links.table, g_branch, *normed, *slopes, *weights, *so_far],
        [
            shape_of((every // 2, width), BF),
            shape_of((1, every // 2), F32),
            shape_of((total, width), F32),
        ],
        scalars=1,
        after=after,
        scratch_shapes=[pltpu.VMEM((total, every // 4), BF)],
        vmem=UP_MIB,
    )


def proj_grad_kernel(slots, gsum_ref, gn_ref, wp_ref, gain_ref, *refs):
    xhat_refs, rstd_refs, ctx_refs = (refs[i * slots : (i + 1) * slots] for i in range(3))
    gpre_ref, gctx_ref, gw_ref, vec_ref, attn_ref = refs[3 * slots :]
    padded, width = xhat_refs[0].shape
    sums = [jnp.zeros((1, width), F32)] * 3
    for slot in range(slots):
        part = slice(slot * padded, (slot + 1) * padded)
        g_normed = gsum_ref[part, :] + gn_ref[part, :]
        xhat = xhat_refs[slot][...].astype(F32)
        g_xhat = g_normed * flat_line(gain_ref)
        g_pre = rstd_refs[slot][...] * (g_xhat - rowmean(g_xhat) - xhat * rowmean(g_xhat * xhat))
        gpre_ref[slot] = g_pre
        g_attn = g_pre.astype(BF)
        attn_ref[part, :] = g_attn
        gctx_ref[slot] = nt(g_attn, wp_ref[...]).astype(BF)
        new = (colsum(g_normed * xhat), colsum(g_normed), colsum(g_pre))
        sums = [a + b for a, b in zip(sums, new)]
    gw_ref[...] = tn(jnp.concatenate([ref[...] for ref in ctx_refs]), attn_ref[...]).astype(BF)
    vec_ref[...] = jnp.concatenate(sums + [jnp.zeros((5, width), F32)])


def proj_grad(g_sum, g_norm, wp, gain, xhat, rstd, ctx, after):
    slots, (padded, width) = len(xhat), xhat[0].shape
    return kernel_call(
        functools.partial(proj_grad_kernel, slots),
        4,
        [g_sum, g_norm, wp, gain, *xhat, *rstd, *ctx],
        [
            shape_of((slots, padded, width), F32),
            shape_of((slots, padded, width), BF),
            shape_of((width, width), BF),
            shape_of((8, width), F32),
        ],
        after=after,
        scratch_shapes=[pltpu.VMEM((slots * padded, width), BF)],
        vmem=UP_MIB,
    )


def attend_back_kernel(pair, slots, at_core, g_ref, *rest):
    arrays, bias_refs, rest = rest[: 5 * slots], rest[5 * slots : 6 * slots], rest[6 * slots :]
    x_ref = None
    if len(rest) > 1:
        x_ref, mask_ref, before_ref, *beside, d_ref, send_ref, keep_ref, vec_ref = rest
    else:
        (d_ref,) = rest
    padded = d_ref.shape[1]
    lanes = slice(pair * PAIR, (pair + 1) * PAIR)
    lane = lax.broadcasted_iota(jnp.int32, (padded, PAIR), 1)
    one = jnp.ones((), BF)
    zero = jnp.zeros((), BF)
    for slot in range(slots):
        bias = bias_refs[slot][...]
        g = g_ref[slot, :, lanes]
        q, extra, k, v, ctx = (ref[:, lanes] for ref in arrays[slot::slots])
        products = g.astype(F32) * ctx.astype(F32)
        parts = []
        for head in range(2):
            own = (lane < HEAD) if head == 0 else (lane >= HEAD)
            aux = HEAD if head == 0 else 0
            delta = -jnp.sum(jnp.where(own, products, 0.0), -1, keepdims=True)
            high = delta.astype(BF)
            low = (delta - high.astype(F32)).astype(BF)
            after = (lane > aux) & (lane < aux + 4)
            k_more = jnp.where(own, k, jnp.where(lane == aux, bias, jnp.where(after, one, zero)))
            v_more = jnp.where(own, v, jnp.where((lane >= aux) & (lane < aux + 2), one, zero))
            q_more = jnp.where(own, q, extra)
            g_more = jnp.where(own, g, jnp.where(lane == aux, high, jnp.where(lane == aux + 1, low, zero)))
            probs = jnp.exp(nt(k_more, q_more))
            g_scores = (probs * nt(v_more, g_more)).astype(BF)
            parts.append((tn(g_scores, k_more), nn(g_scores, q_more), nn(probs.astype(BF), g_more)))
        g_q, g_k, g_v = (jnp.where(lane < HEAD, a, b) for a, b in zip(*parts))
        g_q = (g_q.astype(BF).astype(F32) * (1.0 / math.sqrt(HEAD))).astype(BF)
        for i, part in enumerate((g_q, g_k.astype(BF), g_v.astype(BF))):
            d_ref[slot, :, i * PAIR : (i + 1) * PAIR] = part
    if x_ref is None:
        return
    both = slots * padded
    d = [ref[...].reshape(both, 3 * PAIR) for ref in (before_ref, d_ref)]
    d = jnp.concatenate(d, axis=1)
    g_weights = tn(x_ref[...].reshape(both, x_ref.shape[2]), d).astype(BF)
    vec_ref[...] = colsum(d.astype(F32))
    half = g_weights.shape[0] // 2
    first, second = (beside[0][...], g_weights) if beside else (g_weights[:half], g_weights[half:])
    choose = either(mask_ref, at_core, g_weights.shape[1])
    keep_ref[...] = choose(second, first)
    send_ref[...] = choose(first, second)


def attend_back(links, pair, g_ctx, arrays, bias, x, before, beside, after):
    slots, padded, width = g_ctx.shape
    operands = [g_ctx, *[t for of_slots in arrays for t in of_slots], *bias]
    outs = [shape_of((slots, padded, 3 * PAIR), BF)]
    if before is not None:
        operands += [x, links.masks, before, *beside]
        part = shape_of((width if beside else width // 2, 6 * PAIR), BF)
        outs += [part, part, shape_of((1, 6 * PAIR), F32)]
    return kernel_call(
        functools.partial(attend_back_kernel, pair, slots, links.at("core")),
        5 if before is None else 7,
        operands,
        outs,
        after=after,
        vmem=BACK_MIB,
    )


def in_lanes(pairs, i):
    return jnp.concatenate([p[..., i * PAIR : (i + 1) * PAIR] for p in pairs], axis=-1)


def input_grad(rows, g_pre, parts, weights, after):
    slots, _, width = g_pre.shape
    cuts = row_parts(rows)

    def kernel(leave, gpre_ref, *refs):
        d_refs, w_refs, out_ref = refs[: len(parts)], refs[len(parts) : len(parts) + 3], refs[-1]
        totals = []
        for slot in range(slots):
            total = gpre_ref[slot]
            for i, w_ref in enumerate(w_refs):
                total = total + nt(in_lanes([d[slot] for d in d_refs], i), w_ref[...])
            totals.append(total)
        for i, (cut,) in enumerate(cuts):
            for slot in range(slots):
                out_ref[cut, slot, :] = totals[slot][cut]
            leave(i)

    return leaving_call(
        kernel, 9, [g_pre, *parts, *weights], shape_of((rows, slots, width), F32), cuts, after, 14
    )


class Links:
    def __init__(self, items, shards):
        self.items, self.shards = items, shards
        self.joint = lax.axis_index("dp") * shards + lax.axis_index("seg")
        self.core = shards
        self.y = 2 * shards
        self.seg = [1 << i for i in range(shards.bit_length() - 1)]
        self.z = [shards << i for i in range(2, items.bit_length() - 1)]
        first = self.seg[0] if self.seg else self.y
        self.steps = (
            [(self.core, self.core), (first, self.y), (self.y, first)]
            + [(m, m) for m in reversed(self.seg[1:])]
            + [(m, m) for m in self.z]
        )
        self.numbers = {"core": self.bit(self.core, self.core), "seg": lax.axis_index("seg")}
        for masks in [*self.steps, (self.z[0], self.y), (self.y, self.z[0]), (self.y, self.y)]:
            self.numbers[masks] = self.bit(*masks)
        for masks in self.steps:
            self.numbers["own", masks] = self.keep_own(masks)
        self.names = list(self.numbers)
        self.table = jnp.stack(list(self.numbers.values())).astype(jnp.int32)
        self.masks = jnp.broadcast_to(self.table[:, None], (len(self.names), PAIR)).astype(F32)

    def at(self, name):
        return self.names.index(name)

    def swap(self, value, mask0, mask1):
        count = self.items * self.shards
        pairs = [(i, i ^ (mask1 if i & self.core else mask0)) for i in range(count)]
        return lax.ppermute(value, JOINT, pairs)

    def bit(self, mask0, mask1):
        on_core1 = (self.joint & self.core) != 0
        return jnp.where(on_core1, (self.joint & mask1) != 0, (self.joint & mask0) != 0).astype(jnp.int32)

    def keep_own(self, masks):
        own = [mask in self.seg for mask in masks]
        on_core1 = (self.joint & self.core) != 0
        return jnp.where(jnp.where(on_core1, own[1], own[0]), 0, self.bit(*masks))


def tiled(rows):
    return rows % 16 == 0


def ordered(late, a, b, axis=0):
    return jnp.concatenate([jnp.where(late, b, a), jnp.where(late, a, b)], axis=axis)


def add_halves(links, name, held, got, small, after):
    rows, width = held.shape
    half = rows // 2
    extra = 0 if small is None else small.shape[0]
    if not tiled(half):
        keep = links.numbers[name]
        total = held + got[:rows]
        send = lax.dynamic_slice_in_dim(total, (1 - keep) * half, half)
        held = lax.dynamic_slice_in_dim(total, keep * half, half)
        if extra:
            small = small + got[rows:]
            send = jnp.concatenate([send, small])
        return send, held, small
    at = links.at(name)

    def kernel(mask_ref, held_ref, got_ref, *rest):
        choose = either(mask_ref, at, width)
        if extra:
            small_in, send_ref, keep_out, small_ref = rest
            small_ref[...] = small_in[...] + got_ref[rows:, :]
            send_ref[half:, :] = small_ref[...]
        else:
            send_ref, keep_out = rest
        first = held_ref[:half, :] + got_ref[:half, :]
        second = held_ref[half:, :] + got_ref[half:rows, :]
        send_ref[:half, :] = choose(first, second)
        keep_out[...] = choose(second, first)

    outs = [shape_of((half + extra, width), BF), shape_of((half, width), BF)]
    smalls = [] if small is None else [small]
    out = kernel_call(
        kernel,
        1,
        [links.masks, held, got, *smalls],
        outs + [like(t) for t in smalls],
        after=after,
        vmem=PASS_MIB,
    )
    return (*out, None)[:3]


def add_whole(held, got, small, after):
    rows, width = held.shape
    extra = 0 if small is None else small.shape[0]
    if not tiled(rows):
        piece = held[:rows] + got[:rows]
        if small is None:
            return piece, None
        small = small + got[rows:]
        return jnp.concatenate([piece, small]), small

    def kernel(held_ref, got_ref, *rest):
        if extra:
            small_in, piece_ref, small_ref = rest
            small_ref[...] = small_in[...] + got_ref[rows:, :]
            piece_ref[rows:, :] = small_ref[...]
        else:
            (piece_ref,) = rest
        piece_ref[:rows, :] = held_ref[...] + got_ref[:rows, :]

    smalls = [] if small is None else [small]
    out = kernel_call(
        kernel,
        1,
        [held, got, *smalls],
        [shape_of((rows + extra, width), BF)] + [like(t) for t in smalls],
        after=after,
        vmem=PASS_MIB,
    )
    return (*out, None)[:2]


def add_apart(held, got, rows, after):
    if not tiled(rows):
        both = held + got
        return both[:rows], both[rows:]

    def kernel(held_ref, got_ref, piece_ref, small_ref):
        piece_ref[...] = held_ref[:rows, :] + got_ref[:rows, :]
        small_ref[...] = held_ref[rows:, :] + got_ref[rows:, :]

    outs = [shape_of((n, held.shape[1]), BF) for n in (rows, held.shape[0] - rows)]
    return kernel_call(kernel, 1, [held, got], outs, after=after, vmem=PASS_MIB)


def add_pairs(pieces, gots, after):
    if not tiled(pieces[0].shape[0]):
        return jnp.stack([a + b for a, b in zip(pieces, gots)])
    many = len(pieces)

    def kernel(*refs):
        for i in range(many):
            refs[-1][i] = refs[i][...] + refs[many + i][...]

    out = shape_of((many, *pieces[0].shape), BF)
    return kernel_call(kernel, 1, [*pieces, *gots], out, after=after, vmem=PASS_MIB)


def join(links, name, piece, got, after):
    rows, width = piece.shape[-2:]
    if not tiled(rows):
        return ordered(links.numbers[name] == 1, piece, got, axis=-2)
    at = links.at(name)

    def kernel(mask_ref, piece_ref, got_ref, out_ref):
        choose = either(mask_ref, at, width)
        for i in [()] if piece.ndim == 2 else [(i,) for i in range(piece.shape[0])]:
            mine, other = piece_ref[i], got_ref[i]
            out_ref[(*i, slice(0, rows), slice(None))] = choose(other, mine)
            out_ref[(*i, slice(rows, 2 * rows), slice(None))] = choose(mine, other)

    out = shape_of((*piece.shape[:-2], 2 * rows, width), BF)
    return kernel_call(kernel, 1, [links.masks, piece, got], out, after=after, vmem=PASS_MIB)


class Sum:
    def __init__(self, links, relative, halves, small=None):
        self.links, self.relative, self.small = links, relative, small
        self.halves = halves
        self.adding = links.steps
        self.passing = list(self.way_back(links.steps[:-1]))
        self.held = self.piece = self.flying = None
        self.place = 0

    def way_back(self, steps):
        links = self.links
        for step in reversed(steps):
            crosses = [mask in links.seg for mask in step]
            if self.relative and crosses[0]:
                if not crosses[1]:
                    yield (links.y, links.y)
            elif not (self.relative and crosses[1]):
                yield step

    def advance(self, after=()):
        links, index = self.links, self.place
        self.place += 1
        last = len(self.adding) - 1
        if index == 0:
            send, self.held = self.halves
        elif index < last:
            name = self.adding[index]
            name = ("own", name) if self.relative else name
            send, self.held, self.small = add_halves(links, name, self.held, self.flying, self.small, after)
        elif index == last:
            send, self.small = add_whole(self.held, self.flying, self.small, after)
            self.held = send
        elif index == last + 1:
            rows = self.held.shape[0] - (0 if self.small is None else self.small.shape[0])
            if self.small is None:
                self.piece, _ = add_whole(self.held, self.flying, None, after)
            else:
                self.piece, self.small = add_apart(self.held, self.flying, rows, after)
            send = self.piece
        else:
            send = self.piece = join(links, self.passing[index - last - 2], self.piece, self.flying, after)
        step = self.adding[index] if index <= last else self.passing[index - last - 1]
        self.flying = links.swap(send, *step)
        return [send]

    def left(self):
        return len(self.adding) + len(self.passing) - self.place

    def finish(self, after=()):
        while self.left():
            self.advance(after)
        return self.piece, self.flying


class Merged:
    def __init__(self, links, sums):
        self.links, self.sums = links, sums
        self.passing = sums[0].passing
        self.place = 0

    def advance(self, after=()):
        index = self.place
        self.place += 1
        if index == 0:
            for s in self.sums:
                while s.place < len(s.adding):
                    s.advance(after)
            self.piece = add_pairs([s.held for s in self.sums], [s.flying for s in self.sums], after)
            if len(self.sums) == 1:
                self.piece = self.piece.reshape(self.piece.shape[1:])
        else:
            self.piece = join(self.links, self.passing[index - 1], self.piece, self.flying, after)
        self.flying = self.links.swap(self.piece, *self.passing[index])
        return [self.piece]

    def left(self):
        return len(self.passing) - self.place

    def finish(self, after=()):
        while self.left():
            self.advance(after)
        return self.piece, self.flying


class Gather:
    def __init__(self, links, up, up_bias, down):
        self.links = links
        width, hidden = up.shape
        self.width, self.hidden = width, hidden
        z, y, core = links.z[0], links.y, links.core
        self.steps = [(links.seg[0], links.seg[0]), (z, y), (y, z), (core, core)]
        self.place = 0
        places = [links.at(name) for name in ("core", (y, z), (z, y))]
        self.wide = hidden // width
        cut, deep, wide = width // 8, hidden // 8, self.wide
        rows = wide * cut + deep + 16

        def kernel(table_ref, bias_ref, up_ref, down_ref, out_ref, up_cut, down_cut, sems):
            place = sum(table_ref[at] * weight for at, weight in zip(places, (4, 2, 1)))
            copies = [
                pltpu.make_async_copy(up_ref.at[tile_rows(place * cut, cut), :], up_cut, sems.at[0]),
                pltpu.make_async_copy(down_ref.at[tile_rows(place * deep, deep), :], down_cut, sems.at[1]),
            ]
            for copy in copies:
                copy.start()
            lines, rest = [], flat_line(bias_ref)
            for _ in range(3):
                term = rest.astype(BF).astype(F32)
                lines += [term[:, i * width : (i + 1) * width] for i in range(wide)]
                rest = rest - term
            lines.append(jnp.zeros((16 - len(lines), width), F32))
            out_ref[rows - 16 :, :] = jnp.concatenate(lines).astype(BF)
            for copy in copies:
                copy.wait()
            for i in range(wide):
                out_ref[i * cut : (i + 1) * cut, :] = up_cut[:, i * width : (i + 1) * width]
            out_ref[wide * cut : wide * cut + deep, :] = down_cut[...]

        anywhere = pl.BlockSpec(memory_space=pl.ANY)
        self.piece = pl.pallas_call(
            kernel,
            in_specs=[pl.BlockSpec(memory_space=pltpu.SMEM), pl.BlockSpec(memory_space=pltpu.VMEM), anywhere, anywhere],
            out_shape=shape_of((rows, width), BF),
            scratch_shapes=[
                pltpu.VMEM((cut, hidden), BF),
                pltpu.VMEM((deep, width), BF),
                pltpu.SemaphoreType.DMA((2,)),
            ],
            compiler_params=pltpu.CompilerParams(vmem_limit_bytes=4 * 2**20),
        )(links.table, up_bias, *(pltpu.with_memory_space_constraint(t, pltpu.HBM) for t in (up, down)))

    def advance(self, after=()):
        index = self.place
        self.place += 1
        if index == 1:
            self.piece = self.flying[None]
        elif index > 1:
            self.piece = join(self.links, self.steps[index - 1], self.piece, self.flying, after)
        self.flying = self.links.swap(self.piece, *self.steps[index])
        return [self.piece]

    def finish(self, after=()):
        while self.place < len(self.steps):
            self.advance(after)
        width, hidden, wide = self.width, self.hidden, self.wide
        cut, deep = width // 8, hidden // 8
        rows = wide * cut + deep + 16
        piece, got = (t.reshape(4 * rows, width) for t in (self.piece, self.flying))

        at_core = self.links.at("core")

        def kernel(table_ref, piece_ref, got_ref, up_ref, bias_ref, down_ref):
            for i in range(8):
                ref = piece_ref if i < 4 else got_ref
                start = (i % 4) * rows
                place = (table_ref[at_core] ^ (i // 4)) * 4 + i % 4
                at = tile_rows(place * cut, cut)
                for j in range(wide):
                    up_ref[at, j * width : (j + 1) * width] = ref[start + j * cut : start + (j + 1) * cut, :]
                down_ref[tile_rows(place * deep, deep), :] = ref[start + wide * cut : start + wide * cut + deep, :]
            lines = piece_ref[rows - 16 : rows, :].astype(F32)
            parts = [sum(lines[i * wide + j : i * wide + j + 1] for i in range(3)) for j in range(wide)]
            bias_ref[...] = jnp.concatenate(parts, 1).reshape(hidden)

        return kernel_call(
            kernel,
            2,
            [self.links.table, piece, got],
            [shape_of((width, hidden), BF), shape_of((hidden,), F32), shape_of((hidden, width), BF)],
            scalars=1,
            after=after,
            vmem=10,
        )


class GatherAny:
    def __init__(self, *args):
        self.args = args

    def advance(self, after=()):
        return []

    def finish(self, after=()):
        return other_shards(*self.args)


def other_shards(links, up, up_bias, down):
    shards = links.shards
    hidden = down.shape[0]
    ups = lax.all_gather(up, "seg", axis=0)
    downs = lax.all_gather(down, "seg", axis=0)
    biases = lax.all_gather(up_bias.reshape(1, -1), "seg", axis=0)
    order = lax.axis_index("seg") ^ jnp.arange(1, shards)
    ups = jnp.moveaxis(jnp.take(ups, order, axis=0), 0, 1).reshape(up.shape[0], -1)
    return ups, jnp.take(biases, order, axis=0).reshape(-1), jnp.take(downs, order, axis=0).reshape(-1, down.shape[1])


def pack_small(links, vec_ffn, vec_attn, g_lines, bias_send, bias_keep, send):
    width = vec_ffn.shape[1]
    shards = links.shards
    if shards != 2 or bias_send.shape[1] != 2 * width or not tiled(send.shape[0]):
        halves = ordered(links.numbers["core"] == 1, bias_keep, bias_send).reshape(2, shards, -1)
        by_shard = jnp.moveaxis(halves, 0, 1).reshape(shards, -1)
        by_shard = jnp.take(by_shard, jnp.arange(shards) ^ lax.axis_index("seg"), axis=0).reshape(-1, width)
        lines = [
            in_lanes([g[:, i * 3 * PAIR : (i + 1) * 3 * PAIR] for g in g_lines for i in range(2)], i) for i in (0, 2)
        ]
        small = jnp.concatenate([vec_ffn[:3], vec_attn[:3], *lines, by_shard])
        pad = -(-small.shape[0] // 16) * 16 - small.shape[0]
        small = jnp.pad(small, ((0, pad), (0, 0))).astype(BF)
        return jnp.concatenate([send, small]), small
    at_core, at_seg = links.at("core"), links.at("seg")
    rows = send.shape[0]

    def kernel(table_ref, send_ref, ffn_ref, attn_ref, *rest):
        line_refs, (bias_send_ref, bias_keep_ref, out_ref, small_ref, rows_ref) = rest[:-5], rest[-5:]
        rows_ref[...] = jnp.zeros_like(rows_ref)
        rows_ref[0:3, :] = ffn_ref[0:3, :]
        rows_ref[3:6, :] = attn_ref[0:3, :]
        for g, line_ref in enumerate(line_refs):
            for i in range(2):
                for row, part in ((6, 0), (7, 2)):
                    at = (3 * i + part) * PAIR
                    place = (2 * g + i) * PAIR
                    rows_ref[row : row + 1, place : place + PAIR] = line_ref[:, at : at + PAIR]
        for ref, half in ((bias_send_ref, 1 - table_ref[at_core]), (bias_keep_ref, table_ref[at_core])):
            for i in range(2):
                row = 8 + 2 * (table_ref[at_seg] ^ i) + half
                rows_ref[pl.ds(row, 1), :] = ref[:, i * width : (i + 1) * width]
        small_ref[...] = rows_ref[...].astype(BF)
        out_ref[:rows, :] = send_ref[...]
        out_ref[rows:, :] = small_ref[...]

    return kernel_call(
        kernel,
        1,
        [links.table, send, vec_ffn, vec_attn, *g_lines, bias_send, bias_keep],
        [shape_of((rows + 16, width), BF), shape_of((16, width), BF)],
        scalars=1,
        scratch_shapes=[pltpu.VMEM((16, width), F32)],
        vmem=PASS_MIB,
    )


def ffn_output(links, pair, turned, after):
    rows, width = pair[0].shape
    if rows % PAIR:
        array = ordered(links.numbers["core"] == 1, *pair).astype(F32)
        return [array.T if turned else array]
    at_core = links.at("core")
    halves = [slice(0, rows), slice(rows, 2 * rows)]
    parts = [(slice(None), h) if turned else (h,) for h in halves]

    def kernel(leave, mask_ref, mine_ref, other_ref, out_ref):
        choose = either(mask_ref, at_core, width)
        for i, order in enumerate(((other_ref, mine_ref), (mine_ref, other_ref))):
            values = choose(order[0][...], order[1][...]).astype(F32)
            out_ref[parts[i]] = values.T if turned else values
            leave(i)

    shape = (width, 2 * rows) if turned else (2 * rows, width)
    return leaving_call(kernel, 9, [links.masks, *pair], shape_of(shape, F32), parts, after, 10)


def square_outputs(links, first, groups, begin, before, small, hidden, after):
    given = [t for pair in [*first, *groups] for t in pair]
    width = given[0].shape[1]
    wide = 2 * PAIR
    at_core, at_seg = links.at("core"), links.at("seg")
    lines = hidden // width
    many = len(first) + len(groups)
    smalls = [] if small is None else [small]

    def kernel(mask_ref, *refs):
        refs = list(refs)
        pairs = [refs[2 * i : 2 * i + 2] for i in range(many)]
        small_refs = refs[2 * many : 2 * many + len(smalls)]
        refs = refs[2 * many + len(smalls) + len(before) + len(after) :]
        *outs, sems = refs
        token = outs.pop(len(outs) - 3 * many - len(first) - 1)
        token[...] = jnp.zeros_like(token)
        outs, scratch = outs[: len(outs) - 3 * many - len(first)], outs[len(outs) - 3 * many - len(first) :]
        choose = either(mask_ref, at_core, width)
        copies = []

        def leave(values, out, lanes):
            buffer = scratch[len(copies)]
            buffer[...] = values
            copy = pltpu.make_async_copy(buffer, out.at[:, lanes], sems.at[len(copies)])
            copy.start()
            copies.append(copy)

        for number, (mine, other) in enumerate(pairs):
            group = number + begin
            if first and number == 0:
                leave(choose(other[...], mine[...]).astype(F32), outs[3], slice(0, width))
                values = choose(mine[...], other[...])
            else:
                values = jnp.concatenate([choose(other[...], mine[...]), choose(mine[...], other[...])])
            for i in range(3):
                parts = [values[:, (3 * j + i) * PAIR : (3 * j + i + 1) * PAIR] for j in range(2)]
                leave(jnp.concatenate(parts, 1).astype(F32), outs[i], slice(group * wide, (group + 1) * wide))
        if small_refs:
            vector_outs, bias_out = outs[3:11], outs[11]
            rows = small_refs[0][...].astype(F32)
            for i, out_ref in enumerate(vector_outs):
                out_ref[...] = rows[i : i + 1].reshape(width)
            by_shard = [
                jnp.concatenate([rows[8 + n * lines + i : 9 + n * lines + i] for i in range(lines)], 1)
                for n in range(2)
            ]
            bias_out[...] = either(mask_ref, at_seg, hidden)(by_shard[1], by_shard[0]).reshape(hidden)
        for copy in copies:
            copy.wait()

    square, vector = pltpu.HBM((width, width), F32), shape_of((width,), F32)
    anywhere, near = pl.BlockSpec(memory_space=pl.ANY), pl.BlockSpec(memory_space=pltpu.VMEM)
    far = pl.BlockSpec(memory_space=pltpu.HBM)
    outs, out_specs = [square] * 3, [far] * 3
    if first:
        outs, out_specs = outs + [square], out_specs + [far]
    if smalls:
        outs, out_specs = outs + [vector] * 8 + [shape_of((hidden,), F32)], out_specs + [near] * 9
    outs, out_specs = outs + [TOKEN], out_specs + [near]
    scratch = []
    for number in range(many):
        if first and number == 0:
            scratch.append(pltpu.VMEM((width, width), F32))
        scratch += [pltpu.VMEM((width, wide), F32)] * 3
    operands = [links.masks, *given, *smalls]
    return pl.pallas_call(
        kernel,
        in_specs=[near] * len(operands) + [far] * len(before) + [anywhere] * len(after),
        out_specs=out_specs,
        out_shape=outs,
        scratch_shapes=scratch + [pltpu.SemaphoreType.DMA((len(scratch),))],
        input_output_aliases={len(operands) + i: i for i in range(len(before))},
        compiler_params=pltpu.CompilerParams(vmem_limit_bytes=16 * 2**20),
        cost_estimate=pl.CostEstimate(flops=9 * 10**9, bytes_accessed=1 << 20, transcendentals=0),
    )(*operands, *before, *after)


def attention_outputs_any(links, first, groups, small, hidden):
    on_core1 = links.numbers["core"] == 1
    whole = [ordered(on_core1, *pair) for pair in (first, *groups)]
    width = whole[0].shape[1]
    grads = [whole[0][width:], *whole[1:]]
    pairs = [g[:, i * 3 * PAIR : (i + 1) * 3 * PAIR] for g in grads for i in range(2)]
    small = small.astype(F32)
    biases = small[8 : 8 + hidden * links.shards // width].reshape(links.shards, -1)
    bias = lax.dynamic_index_in_dim(biases, lax.axis_index("seg"), keepdims=False)
    squares = [in_lanes(pairs, i).astype(F32) for i in range(3)]
    return [whole[0][:width].astype(F32), *squares, *[small[i] for i in range(8)], bias]


def in_halves(array, axis, shards):
    shape = list(array.shape)
    parts = array.reshape(shape[:axis] + [shards, 2, -1] + shape[axis + 1 :])
    return jnp.moveaxis(parts, axis + 1, axis).reshape(shape)


def body(
    activations,
    tok_count,
    w_query,
    w_key,
    w_value,
    w_proj,
    b_query,
    b_value,
    b_proj,
    gain_attn,
    shift_attn,
    w_up,
    b_up,
    w_down,
    b_down,
    gain_ffn,
    shift_ffn,
    cotangent,
    items,
    shards,
):
    slots, rows, width = activations.shape
    links = Links(items, shards)
    count = tok_count[:, 0]
    more = ((0, 0), (0, -rows % 16), (0, 0))
    x, cot = jnp.pad(activations, more), jnp.pad(cotangent, more)
    own = (w_up, b_up, w_down)
    hidden = w_up.shape[1]
    every = hidden * shards
    weights = (Gather if shards == 2 and links.z else GatherAny)(links, *own)

    state, done = [], [cot]
    for slot in range(slots):
        weights_in = [w_query, w_key, w_value]
        after = weights.advance(done) + done
        state.append(attend(rows, slot, count, x, weights_in, [b_query, b_value], after))
        done = [state[-1][-1]]
    q, extra, k, v, ctx, bias = zip(*state)
    after = weights.advance(done) + done
    normed, xhat, rstd = first_norm(x, w_proj, [b_proj, gain_attn, shift_attn], ctx, after)
    done = [rstd[-1]]
    act0, slope0, first = ffn_first(normed, own, done)
    others = weights.finish([first])
    act1, slope1, layer_out, g_sum, g_branch, vec_ffn = ffn_last(
        rows, count, normed, others, first, cot, [b_down, gain_ffn, shift_ffn]
    )
    acts, slopes = [act0, act1], [slope0, slope1]
    if shards == 2:
        pieces = [own[2], own[0], others[2], others[0]]
    else:
        acts, slopes = ([in_halves(jnp.concatenate(t, 1), 1, shards)] * 2 for t in (acts, slopes))
        ups = in_halves(jnp.concatenate([own[0], others[0]], 1), 1, shards)
        downs = in_halves(jnp.concatenate([own[2], others[2]]), 0, shards)
        pieces = [downs, ups, downs, ups]

    done = [vec_ffn]
    made, sums = {}, {}
    d_parts, g_lines, small = [], [], None
    arrays = [q, extra, k, v, ctx]
    count_pairs = width // PAIR
    whole_tiles = shards == 2 and tiled(width >> (len(links.steps) - 1))

    def step(name):
        nonlocal done
        sent = sums[name].advance(done)
        done = sent if sums[name].place > 1 else done + sent

    def run(name):
        nonlocal done, small
        if name == "down send":
            made["down"] = [down_grad(links, 1, acts, g_branch, every, done)]
            done = made["down"]
        elif name == "down keep":
            made["down"].append(down_grad(links, 0, acts, g_branch, every, done))
            sums["down"] = Sum(links, True, made["down"])
            done = made["down"][1:]
        elif name == "up send":
            *made["up send"], made["g_norm"] = up_grad(links, 1, g_branch, normed, slopes, pieces, every, [], done)
            done = [made["g_norm"]]
        elif name == "up keep":
            *made["up keep"], made["g_norm"] = up_grad(
                links, 0, g_branch, normed, slopes, pieces, every, [made["g_norm"]], done
            )
            sums["up"] = Sum(links, True, (made["up send"][0], made["up keep"][0]))
            done = [made["g_norm"]]
        elif name == "proj":
            made["g_pre"], made["g_ctx"], made["g_proj"], made["vec"] = proj_grad(
                g_sum, made["g_norm"], w_proj, gain_attn, xhat, rstd, ctx, done
            )
            done = [made["vec"]]
        elif name == "pair":
            pair = len(d_parts)
            before = None if pair % 2 == 0 else d_parts[-1]
            beside = [made["g_proj"]] if pair == 1 else []
            d, *rest = attend_back(links, pair, made["g_ctx"], arrays, bias, x, before, beside, done)
            d_parts.append(d)
            done = [d]
            if rest:
                send, keep, lines = rest
                g_lines.append(lines)
                if pair == count_pairs - 1:
                    hidden_bias = [made[n][1] for n in ("up send", "up keep")]
                    send, small = pack_small(links, vec_ffn, made["vec"], g_lines, *hidden_bias, send)
                    done = [small]
                sums["heads %d" % (pair // 2)] = Sum(links, False, (send, keep), small)
        elif name == "input":
            made["input"], *done = input_grad(
                rows, made["g_pre"], d_parts, [w_query, w_key, w_value], done
            )
        elif name == "layer":
            made["layer"], *done = slots_last(layer_out, rows, done)
        elif name in ("down out", "up out"):
            pair = sums[name[:-3] + "back"].finish()
            made[name], *done = ffn_output(links, pair, name == "up out", done)
        elif name == "squares":
            if whole_tiles:
                pairs = [sums["heads %d" % i].finish() for i in range(count_pairs // 2 - 1)]
                *made["squares"], token = square_outputs(links, pairs[:1], pairs[1:], 0, [], None, hidden, done)
                done = [token]
        elif name in ("down back", "up back") and name not in sums:
            sums[name] = Merged(links, [sums[name[:-5]]])
            step(name)
        elif sums[name].left():
            step(name)

    for name in PLAN:
        run(name)
    for name in ("down back", "up back"):
        if name not in sums:
            run(name)
    while any(s.left() for s in sums.values()):
        for s in sums.values():
            if s.left():
                s.advance([])
    for name in ("down out", "up out", "squares", "layer"):
        if name not in made:
            run(name)
    grad_w_down, grad_w_up = made["down out"], made["up out"]
    layer_out, grad_input = (jnp.transpose(t, (1, 0, 2)) for t in (made["layer"], made["input"]))
    last = sums["heads %d" % (count_pairs // 2 - 1)]
    if whole_tiles:
        *squares, g_proj = made["squares"]
        g_query, g_key, g_value, *vectors, grad_b_up, _ = square_outputs(
            links, [], [last.finish()], count_pairs // 2 - 1, squares, last.small, hidden, []
        )
    else:
        pairs = [sums["heads %d" % i].finish() for i in range(count_pairs // 2)]
        g_proj, g_query, g_key, g_value, *vectors, grad_b_up = attention_outputs_any(
            links, pairs[0], pairs[1:], last.small, hidden
        )
    g_gain_ffn, g_shift_ffn, g_b_down, g_gain_attn, g_shift_attn, g_b_proj, g_b_query, g_b_value = vectors
    return (
        layer_out,
        grad_input,
        g_query,
        g_key,
        g_value,
        g_proj,
        g_b_query,
        g_b_value,
        g_b_proj,
        g_gain_attn,
        g_shift_attn,
        grad_w_up,
        grad_b_up,
        grad_w_down,
        g_b_down,
        g_gain_ffn,
        g_shift_ffn,
    )


def solution(mesh):
    rows, everywhere = P("dp", "seg", None), P()
    return jax.shard_map(
        functools.partial(body, items=mesh.shape["dp"], shards=mesh.shape["seg"]),
        mesh=mesh,
        in_specs=(rows, P("dp", "seg"))
        + (everywhere,) * 9
        + (P(None, "seg"), P("seg"), P("seg", None))
        + (everywhere,) * 3
        + (rows,),
        out_specs=(rows, rows)
        + (everywhere,) * 9
        + (P(None, "seg"), P("seg"), P("seg", None))
        + (everywhere,) * 3,
        check_vma=False,
    )
```

```python
import functools
import math

import jax
import jax.numpy as jnp
from jax import lax
from jax.experimental import pallas as pl
from jax.experimental.pallas import tpu as pltpu
from jax.sharding import PartitionSpec as P

HEAD = 64
MEM = 10
EPSILON = 1e-05
NEG_BIG = -1e30
PAIR = 2 * HEAD
BF = jnp.bfloat16
F32 = jnp.float32
VMEM_MIB = 16
PASS_MIB = 5
ATTEND_MIB = 9
FFN_MIB = 9
DOWN_MIB = 5
UP_MIB = 6
BACK_MIB = 5
JOINT = ("dp", "seg")
TOKEN = jax.ShapeDtypeStruct((8, PAIR), F32)
PLAN = (
    "down send", "down keep", "down", "up send", "down", "up keep", "proj", "down", "up", "pair", "up",
    "down", "pair", "pair", "down", "up", "heads 0", "pair", "heads 1", "heads 0", "up", "pair", "down back",
    "heads 0", "heads 1", "up", "pair", "heads 2", "heads 1", "layer", "heads 2", "down back", "heads 0",
    "heads 1", "heads 2", "up back", "heads 0", "input", "up back", "heads 1", "heads 2", "heads 0",
    "down back", "heads 2", "heads 1", "heads 0", "down out", "heads 2", "heads 1", "heads 0", "up back",
    "heads 2", "heads 1", "up out", "heads 0", "heads 2", "heads 1", "squares", "heads 2",
)


def nn(left, right):
    return jnp.dot(left, right, preferred_element_type=F32)


def tn(left, right):
    return lax.dot_general(left, right, (((0,), (0,)), ((), ())), preferred_element_type=F32)


def nt(left, right):
    return lax.dot_general(left, right, (((1,), (1,)), ((), ())), preferred_element_type=F32)


def colsum(values):
    return jnp.sum(values, 0, keepdims=True)


def rowmean(values):
    return jnp.mean(values, -1, keepdims=True)


def kernel_call(kernel, micros, operands, out_shape, scalars=0, after=(), scratch_shapes=(), vmem=VMEM_MIB, far=()):
    many = len(operands)
    anywhere = pl.BlockSpec(memory_space=pl.ANY)
    near = pl.BlockSpec(memory_space=pltpu.VMEM)

    def run(*refs):
        kernel(*refs[:many], *refs[many + len(after) :])

    specs = [pl.BlockSpec(memory_space=pltpu.SMEM) if i < scalars else near for i in range(many)]
    outs = out_shape if isinstance(out_shape, list) else [out_shape]
    outs = [t if i in far else pltpu.VMEM(t.shape, t.dtype) for i, t in enumerate(outs)]
    results = pl.pallas_call(
        run,
        in_specs=specs + [anywhere] * len(after),
        out_specs=[near] * len(outs),
        out_shape=outs,
        scratch_shapes=scratch_shapes,
        compiler_params=pltpu.CompilerParams(vmem_limit_bytes=vmem * 2**20),
        cost_estimate=pl.CostEstimate(
            flops=int(micros * 1.0e9), bytes_accessed=1 << 20, transcendentals=0
        ),
    )(*operands, *after)
    return results if isinstance(out_shape, list) else results[0]


def leaving_call(kernel, micros, operands, out_shape, parts, after, vmem):
    def run(*refs):
        ins, (out, token, buffer, sems) = refs[: len(operands)], refs[-4:]
        token[...] = jnp.zeros_like(token)
        copies = [pltpu.make_async_copy(buffer.at[part], out.at[part], sems.at[i]) for i, part in enumerate(parts)]
        kernel(lambda i: copies[i].start(), *ins, buffer)
        for copy in copies:
            copy.wait()

    near, anywhere = pl.BlockSpec(memory_space=pltpu.VMEM), pl.BlockSpec(memory_space=pl.ANY)
    return pl.pallas_call(
        run,
        in_specs=[near] * len(operands) + [anywhere] * len(after),
        out_specs=[pl.BlockSpec(memory_space=pltpu.HBM), near],
        out_shape=[pltpu.HBM(out_shape.shape, out_shape.dtype), TOKEN],
        scratch_shapes=[pltpu.VMEM(out_shape.shape, out_shape.dtype), pltpu.SemaphoreType.DMA((len(parts),))],
        compiler_params=pltpu.CompilerParams(vmem_limit_bytes=vmem * 2**20),
        cost_estimate=pl.CostEstimate(
            flops=int(micros * 1.0e9), bytes_accessed=1 << 20, transcendentals=0
        ),
    )(*operands, *after)


def shape_of(shape, dtype):
    return jax.ShapeDtypeStruct(shape, dtype)


def like(array):
    return shape_of(array.shape, array.dtype)


def flat_line(ref):
    return ref[...].reshape(1, -1)


def either(mask_ref, at, width):
    mask = jnp.concatenate([mask_ref[at : at + 1, :]] * (width // PAIR), 1) > 0.5

    def choose(one, zero):
        return jnp.where(jnp.broadcast_to(mask, one.shape), one, zero)

    return choose


def tile_rows(start, rows):
    return pl.ds(pl.multiple_of(start, 16), rows)


def tile_lanes(start, lanes):
    return pl.ds(pl.multiple_of(start, PAIR), lanes)


def key_bias(count, rows, padded):
    row = lax.broadcasted_iota(jnp.int32, (padded, PAIR), 0)
    valid = ((row < MEM + count) | (row >= rows - MEM)) & (row < rows)
    return jnp.where(valid, 0.0, NEG_BIG).astype(BF)


def attend_kernel(
    rows,
    slot,
    count_ref,
    x_ref,
    wq_ref,
    wk_ref,
    wv_ref,
    bq_ref,
    bv_ref,
    q_ref,
    aux_ref,
    k_ref,
    v_ref,
    ctx_ref,
    bias_ref,
):
    padded, width = x_ref.shape[1:]
    x = x_ref[slot]
    q_ref[...] = ((nn(x, wq_ref[...]) + flat_line(bq_ref)) * (1.0 / math.sqrt(HEAD))).astype(BF)
    k_ref[...] = nn(x, wk_ref[...]).astype(BF)
    v_ref[...] = (nn(x, wv_ref[...]) + flat_line(bv_ref)).astype(BF)
    lane = lax.broadcasted_iota(jnp.int32, (padded, PAIR), 1)
    bias_ref[...] = key_bias(count_ref[slot], rows, padded)
    bias = bias_ref[...]
    one = jnp.ones((), BF)
    zero = jnp.zeros((), BF)
    for pair in range(width // PAIR):
        lanes = slice(pair * PAIR, (pair + 1) * PAIR)
        q, k, v = q_ref[:, lanes], k_ref[:, lanes], v_ref[:, lanes]
        contexts, extras = [], []
        for head in range(2):
            own = (lane < HEAD) if head == 0 else (lane >= HEAD)
            aux = HEAD if head == 0 else 0
            at_aux = jnp.where(lane == aux, one, zero)
            scores = nt(
                jnp.where(own, q, at_aux),
                jnp.where(own, k, jnp.where(lane == aux, bias, zero)),
            )
            top = jnp.max(scores, -1, keepdims=True)
            exps = jnp.exp(scores - top).astype(BF)
            weighted = nn(exps, jnp.where(own, v, at_aux))
            total = weighted[:, aux : aux + 1]
            contexts.append(weighted * (1.0 / total))
            rest = -(top + jnp.log(total))
            high = rest.astype(BF)
            rest = rest - high.astype(F32)
            middle = rest.astype(BF)
            low = (rest - middle.astype(F32)).astype(BF)
            extras.append(
                jnp.where(
                    lane == aux + 1,
                    high,
                    jnp.where(lane == aux + 2, middle, jnp.where(lane == aux + 3, low, at_aux)),
                )
            )
        ctx_ref[:, lanes] = jnp.where(lane < HEAD, contexts[0], contexts[1]).astype(BF)
        aux_ref[:, lanes] = jnp.where(lane < HEAD, extras[1], extras[0])


def attend(rows, slot, count, x, weights, vectors, after):
    array = shape_of(x.shape[1:], BF)
    return kernel_call(
        functools.partial(attend_kernel, rows, slot),
        9,
        [count, x, *weights, *vectors],
        [array] * 5 + [shape_of((x.shape[1], PAIR), BF)],
        scalars=1,
        after=after,
        vmem=ATTEND_MIB,
    )


def first_norm_kernel(slots, x_ref, wp_ref, bp_ref, gain_ref, shift_ref, *refs):
    ctx_refs, normed_refs, xhat_refs, rstd_refs = (refs[i * slots : (i + 1) * slots] for i in range(4))
    for slot in range(slots):
        pre_norm = x_ref[slot].astype(F32) + nn(ctx_refs[slot][...], wp_ref[...]) + flat_line(bp_ref)
        center = pre_norm - rowmean(pre_norm)
        rstd = lax.rsqrt(rowmean(center * center) + EPSILON)
        xhat = center * rstd
        normed_refs[slot][...] = (xhat * flat_line(gain_ref) + flat_line(shift_ref)).astype(BF)
        xhat_refs[slot][...] = xhat.astype(BF)
        rstd_refs[slot][...] = rstd


def first_norm(x, wp, vectors, ctx, after):
    slots, padded, width = x.shape
    array, column = shape_of((padded, width), BF), shape_of((padded, 1), F32)
    out = kernel_call(
        functools.partial(first_norm_kernel, slots),
        3,
        [x, wp, *vectors, *ctx],
        [array] * (2 * slots) + [column] * slots,
        after=after,
        vmem=FFN_MIB,
    )
    return [out[i * slots : (i + 1) * slots] for i in range(3)]


def hidden_units(n_refs, up_ref, ub_ref, act_ref, slope_ref):
    size = up_ref.shape[1]
    bias = flat_line(ub_ref)
    cut = math.gcd(256, size)
    padded = n_refs[0].shape[0]
    for at in range(0, size, cut):
        part = slice(at, at + cut)
        for slot, n_ref in enumerate(n_refs):
            rows = slice(slot * padded, (slot + 1) * padded)
            pre = nn(n_ref[...], up_ref[:, part]) + bias[:, part]
            cdf = 0.5 + 0.5 * lax.erf(pre * math.sqrt(0.5))
            act_ref[rows, part] = (pre * cdf).astype(BF)
            slope = cdf + pre * (jnp.exp(-0.5 * (pre * pre)) * (1.0 / math.sqrt(2.0 * math.pi)))
            slope_ref[rows, part] = slope.astype(BF)


def ffn_first_kernel(slots, *refs):
    up_ref, ub_ref, down_ref, act_ref, slope_ref, sum_ref = refs[slots:]
    hidden_units(refs[:slots], up_ref, ub_ref, act_ref, slope_ref)
    sum_ref[...] = nn(act_ref[...], down_ref[...])


def ffn_last_kernel(rows, slots, count_ref, *refs):
    n_refs, refs = refs[:slots], refs[slots:]
    up_ref, ub_ref, down_ref, first_ref, cot_ref, bd_ref, gain_ref, shift_ref, *refs = refs
    act_ref, slope_ref, out_ref, gsum_ref, gbranch_ref, vec_ref = refs
    hidden_units(n_refs, up_ref, ub_ref, act_ref, slope_ref)
    padded, width = n_refs[0].shape
    row = lax.broadcasted_iota(jnp.int32, (padded, width), 0)
    gain = flat_line(gain_ref)
    sums = [jnp.zeros((1, width), F32)] * 3
    for slot, n_ref in enumerate(n_refs):
        part = slice(slot * padded, (slot + 1) * padded)
        count = count_ref[slot]
        keep = ((row < MEM + count) | (row >= rows - MEM)) & (row < rows) & (count > 0)
        branch = first_ref[part, :] + nn(act_ref[part, :], down_ref[...])
        summed = n_ref[...].astype(F32) + branch + flat_line(bd_ref)
        center = summed - rowmean(summed)
        rstd = lax.rsqrt(rowmean(center * center) + EPSILON)
        xhat = center * rstd
        out_ref[slot] = jnp.where(keep, xhat * gain + flat_line(shift_ref), 0.0).astype(BF)
        g_out = jnp.where(keep, cot_ref[slot].astype(F32), 0.0)
        g_xhat = g_out * gain
        g_sum = rstd * (g_xhat - rowmean(g_xhat) - xhat * rowmean(g_xhat * xhat))
        gsum_ref[part, :] = g_sum
        gbranch_ref[part, :] = g_sum.astype(BF)
        new = (colsum(g_out * xhat), colsum(g_out), colsum(g_sum))
        sums = [a + b for a, b in zip(sums, new)]
    vec_ref[...] = jnp.concatenate(sums + [jnp.zeros((5, width), F32)])


def ffn_first(normed, own, after):
    total, width = len(normed) * normed[0].shape[0], normed[0].shape[1]
    acts = shape_of((total, own[0].shape[1]), BF)
    return kernel_call(
        functools.partial(ffn_first_kernel, len(normed)),
        7.5,
        [*normed, *own],
        [acts, acts, shape_of((total, width), F32)],
        after=after,
        vmem=FFN_MIB,
    )


def ffn_last(rows, count, normed, others, first, cot, vectors):
    total, width = first.shape
    acts = shape_of((total, others[0].shape[1]), BF)
    return kernel_call(
        functools.partial(ffn_last_kernel, rows, len(normed)),
        10.5,
        [count, *normed, *others, first, cot, *vectors],
        [
            acts,
            acts,
            shape_of(cot.shape, BF),
            shape_of(first.shape, F32),
            shape_of(first.shape, BF),
            shape_of((8, width), F32),
        ],
        scalars=1,
        vmem=FFN_MIB,
    )


def slots_last(array, rows, after):
    slots, _, width = array.shape
    parts = row_parts(rows)

    def kernel(leave, in_ref, out_ref):
        for i, (part,) in enumerate(parts):
            for slot in range(slots):
                out_ref[part, slot, :] = in_ref[slot, part, :]
            leave(i)

    return leaving_call(kernel, 8, [array], shape_of((rows, slots, width), array.dtype), parts, after, 8)


def row_parts(rows):
    cut = rows // 32 * 16
    return [(slice(0, cut),), (slice(cut, rows),)]


def store_half(piece_ref, values, step, half, unit, shards):
    per = values.shape[0] // unit
    for i in range(per):
        block = step * per + i
        shard, y = block // 2, block % 2
        low, high = shard % 2, shard // 2
        place = jnp.where(half == 0, low * 2 + y, y * 2 + low) * (shards // 2) + high
        piece_ref[tile_rows(place * unit, unit), :] = values[i * unit : (i + 1) * unit].astype(BF)


def block_start(shards, j, half, size):
    return half * size if shards == 2 else (half * 2 + j) * size


def down_grad_kernel(unit, shards, other, at, table_ref, act0_ref, act1_ref, g_ref, piece_ref):
    half = table_ref[at] ^ other
    size = piece_ref.shape[0] // 2
    for j, act_ref in enumerate((act0_ref, act1_ref)):
        act = act_ref[:, tile_lanes(block_start(shards, j, half, size), size)]
        store_half(piece_ref, tn(act, g_ref[...]), j, half, unit, shards)


def down_grad(links, other, acts, g_branch, every, after):
    shards = links.shards
    return kernel_call(
        functools.partial(down_grad_kernel, every // shards // 4, shards, other, links.at("core")),
        4,
        [links.table, *acts, g_branch],
        shape_of((every // 2, g_branch.shape[1]), BF),
        scalars=1,
        after=after,
        vmem=DOWN_MIB,
    )


def up_grad_kernel(unit, shards, slots, other, at_core, table_ref, g_ref, *refs):
    n_refs, refs = refs[:slots], refs[slots:]
    slope0_ref, slope1_ref, down0_ref, up0_ref, down1_ref, up1_ref, *so_far, piece_ref, gb_ref, gn_ref, pre_ref = refs
    half = table_ref[at_core] ^ other
    size = piece_ref.shape[0] // 2
    cut = math.gcd(256, size)
    for j, (slope_ref, down_ref, up_ref) in enumerate(
        ((slope0_ref, down0_ref, up0_ref), (slope1_ref, down1_ref, up1_ref))
    ):
        start = block_start(shards, j, half, size)
        for at in range(0, size, cut):
            g_pre = nt(g_ref[...], down_ref[tile_rows(start + at, cut), :])
            g_pre = g_pre * slope_ref[:, tile_lanes(start + at, cut)].astype(F32)
            pre_ref[:, at : at + cut] = g_pre.astype(BF)
        normed = jnp.concatenate([ref[...] for ref in n_refs])
        store_half(piece_ref, tn(pre_ref[...], normed), j, half, unit, shards)
        gb_ref[:, j * size : (j + 1) * size] = colsum(pre_ref[...].astype(F32))
        share = nt(pre_ref[...], up_ref[:, tile_lanes(start, size)])
        if j:
            gn_ref[...] += share
        else:
            gn_ref[...] = so_far[0][...] + share if so_far else share


def up_grad(links, other, g_branch, normed, slopes, weights, every, so_far, after):
    total, width = g_branch.shape
    shards = links.shards
    return kernel_call(
        functools.partial(up_grad_kernel, every // shards // 4, shards, len(normed), other, links.at("core")),
        9.5,
        [links.table, g_branch, *normed, *slopes, *weights, *so_far],
        [
            shape_of((every // 2, width), BF),
            shape_of((1, every // 2), F32),
            shape_of((total, width), F32),
        ],
        scalars=1,
        after=after,
        scratch_shapes=[pltpu.VMEM((total, every // 4), BF)],
        vmem=UP_MIB,
    )


def proj_grad_kernel(slots, gsum_ref, gn_ref, wp_ref, gain_ref, *refs):
    xhat_refs, rstd_refs, ctx_refs = (refs[i * slots : (i + 1) * slots] for i in range(3))
    gpre_ref, gctx_ref, gw_ref, vec_ref, attn_ref = refs[3 * slots :]
    padded, width = xhat_refs[0].shape
    sums = [jnp.zeros((1, width), F32)] * 3
    for slot in range(slots):
        part = slice(slot * padded, (slot + 1) * padded)
        g_normed = gsum_ref[part, :] + gn_ref[part, :]
        xhat = xhat_refs[slot][...].astype(F32)
        g_xhat = g_normed * flat_line(gain_ref)
        g_pre = rstd_refs[slot][...] * (g_xhat - rowmean(g_xhat) - xhat * rowmean(g_xhat * xhat))
        gpre_ref[slot] = g_pre
        g_attn = g_pre.astype(BF)
        attn_ref[part, :] = g_attn
        gctx_ref[slot] = nt(g_attn, wp_ref[...]).astype(BF)
        new = (colsum(g_normed * xhat), colsum(g_normed), colsum(g_pre))
        sums = [a + b for a, b in zip(sums, new)]
    gw_ref[...] = tn(jnp.concatenate([ref[...] for ref in ctx_refs]), attn_ref[...]).astype(BF)
    vec_ref[...] = jnp.concatenate(sums + [jnp.zeros((5, width), F32)])


def proj_grad(g_sum, g_norm, wp, gain, xhat, rstd, ctx, after):
    slots, (padded, width) = len(xhat), xhat[0].shape
    return kernel_call(
        functools.partial(proj_grad_kernel, slots),
        4,
        [g_sum, g_norm, wp, gain, *xhat, *rstd, *ctx],
        [
            shape_of((slots, padded, width), F32),
            shape_of((slots, padded, width), BF),
            shape_of((width, width), BF),
            shape_of((8, width), F32),
        ],
        after=after,
        scratch_shapes=[pltpu.VMEM((slots * padded, width), BF)],
        vmem=UP_MIB,
    )


def attend_back_kernel(pair, slots, at_core, g_ref, *rest):
    arrays, bias_refs, rest = rest[: 5 * slots], rest[5 * slots : 6 * slots], rest[6 * slots :]
    x_ref = None
    if len(rest) > 1:
        x_ref, mask_ref, before_ref, *beside, d_ref, send_ref, keep_ref, vec_ref = rest
    else:
        (d_ref,) = rest
    padded = d_ref.shape[1]
    lanes = slice(pair * PAIR, (pair + 1) * PAIR)
    lane = lax.broadcasted_iota(jnp.int32, (padded, PAIR), 1)
    one = jnp.ones((), BF)
    zero = jnp.zeros((), BF)
    for slot in range(slots):
        bias = bias_refs[slot][...]
        g = g_ref[slot, :, lanes]
        q, extra, k, v, ctx = (ref[:, lanes] for ref in arrays[slot::slots])
        products = g.astype(F32) * ctx.astype(F32)
        parts = []
        for head in range(2):
            own = (lane < HEAD) if head == 0 else (lane >= HEAD)
            aux = HEAD if head == 0 else 0
            delta = -jnp.sum(jnp.where(own, products, 0.0), -1, keepdims=True)
            high = delta.astype(BF)
            low = (delta - high.astype(F32)).astype(BF)
            after = (lane > aux) & (lane < aux + 4)
            k_more = jnp.where(own, k, jnp.where(lane == aux, bias, jnp.where(after, one, zero)))
            v_more = jnp.where(own, v, jnp.where((lane >= aux) & (lane < aux + 2), one, zero))
            q_more = jnp.where(own, q, extra)
            g_more = jnp.where(own, g, jnp.where(lane == aux, high, jnp.where(lane == aux + 1, low, zero)))
            probs = jnp.exp(nt(k_more, q_more))
            g_scores = (probs * nt(v_more, g_more)).astype(BF)
            parts.append((tn(g_scores, k_more), nn(g_scores, q_more), nn(probs.astype(BF), g_more)))
        g_q, g_k, g_v = (jnp.where(lane < HEAD, a, b) for a, b in zip(*parts))
        g_q = (g_q.astype(BF).astype(F32) * (1.0 / math.sqrt(HEAD))).astype(BF)
        for i, part in enumerate((g_q, g_k.astype(BF), g_v.astype(BF))):
            d_ref[slot, :, i * PAIR : (i + 1) * PAIR] = part
    if x_ref is None:
        return
    both = slots * padded
    d = [ref[...].reshape(both, 3 * PAIR) for ref in (before_ref, d_ref)]
    d = jnp.concatenate(d, axis=1)
    g_weights = tn(x_ref[...].reshape(both, x_ref.shape[2]), d).astype(BF)
    vec_ref[...] = colsum(d.astype(F32))
    half = g_weights.shape[0] // 2
    first, second = (beside[0][...], g_weights) if beside else (g_weights[:half], g_weights[half:])
    choose = either(mask_ref, at_core, g_weights.shape[1])
    keep_ref[...] = choose(second, first)
    send_ref[...] = choose(first, second)


def attend_back(links, pair, g_ctx, arrays, bias, x, before, beside, after):
    slots, padded, width = g_ctx.shape
    operands = [g_ctx, *[t for of_slots in arrays for t in of_slots], *bias]
    outs = [shape_of((slots, padded, 3 * PAIR), BF)]
    if before is not None:
        operands += [x, links.masks, before, *beside]
        part = shape_of((width if beside else width // 2, 6 * PAIR), BF)
        outs += [part, part, shape_of((1, 6 * PAIR), F32)]
    return kernel_call(
        functools.partial(attend_back_kernel, pair, slots, links.at("core")),
        5 if before is None else 7,
        operands,
        outs,
        after=after,
        vmem=BACK_MIB,
    )


def in_lanes(pairs, i):
    return jnp.concatenate([p[..., i * PAIR : (i + 1) * PAIR] for p in pairs], axis=-1)


def input_grad(rows, g_pre, parts, weights, after):
    slots, _, width = g_pre.shape
    cuts = row_parts(rows)

    def kernel(leave, gpre_ref, *refs):
        d_refs, w_refs, out_ref = refs[: len(parts)], refs[len(parts) : len(parts) + 3], refs[-1]
        totals = []
        for slot in range(slots):
            total = gpre_ref[slot]
            for i, w_ref in enumerate(w_refs):
                total = total + nt(in_lanes([d[slot] for d in d_refs], i), w_ref[...])
            totals.append(total)
        for i, (cut,) in enumerate(cuts):
            for slot in range(slots):
                out_ref[cut, slot, :] = totals[slot][cut]
            leave(i)

    return leaving_call(
        kernel, 9, [g_pre, *parts, *weights], shape_of((rows, slots, width), F32), cuts, after, 14
    )


class Links:
    def __init__(self, items, shards):
        self.items, self.shards = items, shards
        self.joint = lax.axis_index("dp") * shards + lax.axis_index("seg")
        self.core = shards
        self.y = 2 * shards
        self.seg = [1 << i for i in range(shards.bit_length() - 1)]
        self.z = [shards << i for i in range(2, items.bit_length() - 1)]
        first = self.seg[0] if self.seg else self.y
        self.steps = (
            [(self.core, self.core), (first, self.y), (self.y, first)]
            + [(m, m) for m in reversed(self.seg[1:])]
            + [(m, m) for m in self.z]
        )
        self.numbers = {"core": self.bit(self.core, self.core), "seg": lax.axis_index("seg")}
        between = [(self.z[0], self.y), (self.y, self.z[0])] if self.z else []
        for masks in [*self.steps, *between, (self.y, self.y)]:
            self.numbers[masks] = self.bit(*masks)
        for masks in self.steps:
            self.numbers["own", masks] = self.keep_own(masks)
        self.names = list(self.numbers)
        self.table = jnp.stack(list(self.numbers.values())).astype(jnp.int32)
        self.masks = jnp.broadcast_to(self.table[:, None], (len(self.names), PAIR)).astype(F32)

    def at(self, name):
        return self.names.index(name)

    def swap(self, value, mask0, mask1):
        count = self.items * self.shards
        pairs = [(i, i ^ (mask1 if i & self.core else mask0)) for i in range(count)]
        return lax.ppermute(value, JOINT, pairs)

    def bit(self, mask0, mask1):
        on_core1 = (self.joint & self.core) != 0
        return jnp.where(on_core1, (self.joint & mask1) != 0, (self.joint & mask0) != 0).astype(jnp.int32)

    def keep_own(self, masks):
        own = [mask in self.seg for mask in masks]
        on_core1 = (self.joint & self.core) != 0
        return jnp.where(jnp.where(on_core1, own[1], own[0]), 0, self.bit(*masks))


def tiled(rows):
    return rows % 16 == 0


def ordered(late, a, b, axis=0):
    return jnp.concatenate([jnp.where(late, b, a), jnp.where(late, a, b)], axis=axis)


def add_halves(links, name, held, got, small, after):
    rows, width = held.shape
    half = rows // 2
    extra = 0 if small is None else small.shape[0]
    if not tiled(half):
        keep = links.numbers[name]
        total = held + got[:rows]
        send = lax.dynamic_slice_in_dim(total, (1 - keep) * half, half)
        held = lax.dynamic_slice_in_dim(total, keep * half, half)
        if extra:
            small = small + got[rows:]
            send = jnp.concatenate([send, small])
        return send, held, small
    at = links.at(name)

    def kernel(mask_ref, held_ref, got_ref, *rest):
        choose = either(mask_ref, at, width)
        if extra:
            small_in, send_ref, keep_out, small_ref = rest
            small_ref[...] = small_in[...] + got_ref[rows:, :]
            send_ref[half:, :] = small_ref[...]
        else:
            send_ref, keep_out = rest
        first = held_ref[:half, :] + got_ref[:half, :]
        second = held_ref[half:, :] + got_ref[half:rows, :]
        send_ref[:half, :] = choose(first, second)
        keep_out[...] = choose(second, first)

    outs = [shape_of((half + extra, width), BF), shape_of((half, width), BF)]
    smalls = [] if small is None else [small]
    out = kernel_call(
        kernel,
        1,
        [links.masks, held, got, *smalls],
        outs + [like(t) for t in smalls],
        after=after,
        vmem=PASS_MIB,
    )
    return (*out, None)[:3]


def add_whole(held, got, small, after):
    rows, width = held.shape
    extra = 0 if small is None else small.shape[0]
    if not tiled(rows):
        piece = held[:rows] + got[:rows]
        if small is None:
            return piece, None
        small = small + got[rows:]
        return jnp.concatenate([piece, small]), small

    def kernel(held_ref, got_ref, *rest):
        if extra:
            small_in, piece_ref, small_ref = rest
            small_ref[...] = small_in[...] + got_ref[rows:, :]
            piece_ref[rows:, :] = small_ref[...]
        else:
            (piece_ref,) = rest
        piece_ref[:rows, :] = held_ref[...] + got_ref[:rows, :]

    smalls = [] if small is None else [small]
    out = kernel_call(
        kernel,
        1,
        [held, got, *smalls],
        [shape_of((rows + extra, width), BF)] + [like(t) for t in smalls],
        after=after,
        vmem=PASS_MIB,
    )
    return (*out, None)[:2]


def add_apart(held, got, rows, after):
    if not tiled(rows):
        both = held + got
        return both[:rows], both[rows:]

    def kernel(held_ref, got_ref, piece_ref, small_ref):
        piece_ref[...] = held_ref[:rows, :] + got_ref[:rows, :]
        small_ref[...] = held_ref[rows:, :] + got_ref[rows:, :]

    outs = [shape_of((n, held.shape[1]), BF) for n in (rows, held.shape[0] - rows)]
    return kernel_call(kernel, 1, [held, got], outs, after=after, vmem=PASS_MIB)


def add_pairs(pieces, gots, after):
    if not tiled(pieces[0].shape[0]):
        return jnp.stack([a + b for a, b in zip(pieces, gots)])
    many = len(pieces)

    def kernel(*refs):
        for i in range(many):
            refs[-1][i] = refs[i][...] + refs[many + i][...]

    out = shape_of((many, *pieces[0].shape), BF)
    return kernel_call(kernel, 1, [*pieces, *gots], out, after=after, vmem=PASS_MIB)


def join(links, name, piece, got, after):
    rows, width = piece.shape[-2:]
    if not tiled(rows):
        return ordered(links.numbers[name] == 1, piece, got, axis=-2)
    at = links.at(name)

    def kernel(mask_ref, piece_ref, got_ref, out_ref):
        choose = either(mask_ref, at, width)
        for i in [()] if piece.ndim == 2 else [(i,) for i in range(piece.shape[0])]:
            mine, other = piece_ref[i], got_ref[i]
            out_ref[(*i, slice(0, rows), slice(None))] = choose(other, mine)
            out_ref[(*i, slice(rows, 2 * rows), slice(None))] = choose(mine, other)

    out = shape_of((*piece.shape[:-2], 2 * rows, width), BF)
    return kernel_call(kernel, 1, [links.masks, piece, got], out, after=after, vmem=PASS_MIB)


class Sum:
    def __init__(self, links, relative, halves, small=None):
        self.links, self.relative, self.small = links, relative, small
        self.halves = halves
        self.adding = links.steps
        self.passing = list(self.way_back(links.steps[:-1]))
        self.held = self.piece = self.flying = None
        self.place = 0

    def way_back(self, steps):
        links = self.links
        for step in reversed(steps):
            crosses = [mask in links.seg for mask in step]
            if self.relative and crosses[0]:
                if not crosses[1]:
                    yield (links.y, links.y)
            elif not (self.relative and crosses[1]):
                yield step

    def advance(self, after=()):
        links, index = self.links, self.place
        self.place += 1
        last = len(self.adding) - 1
        if index == 0:
            send, self.held = self.halves
        elif index < last:
            name = self.adding[index]
            name = ("own", name) if self.relative else name
            send, self.held, self.small = add_halves(links, name, self.held, self.flying, self.small, after)
        elif index == last:
            send, self.small = add_whole(self.held, self.flying, self.small, after)
            self.held = send
        elif index == last + 1:
            rows = self.held.shape[0] - (0 if self.small is None else self.small.shape[0])
            if self.small is None:
                self.piece, _ = add_whole(self.held, self.flying, None, after)
            else:
                self.piece, self.small = add_apart(self.held, self.flying, rows, after)
            send = self.piece
        else:
            send = self.piece = join(links, self.passing[index - last - 2], self.piece, self.flying, after)
        step = self.adding[index] if index <= last else self.passing[index - last - 1]
        self.flying = links.swap(send, *step)
        return [send]

    def left(self):
        return len(self.adding) + len(self.passing) - self.place

    def finish(self, after=()):
        while self.left():
            self.advance(after)
        return self.piece, self.flying


class Merged:
    def __init__(self, links, sums):
        self.links, self.sums = links, sums
        self.passing = sums[0].passing
        self.place = 0

    def advance(self, after=()):
        index = self.place
        self.place += 1
        if index == 0:
            for s in self.sums:
                while s.place < len(s.adding):
                    s.advance(after)
            self.piece = add_pairs([s.held for s in self.sums], [s.flying for s in self.sums], after)
            if len(self.sums) == 1:
                self.piece = self.piece.reshape(self.piece.shape[1:])
        else:
            self.piece = join(self.links, self.passing[index - 1], self.piece, self.flying, after)
        self.flying = self.links.swap(self.piece, *self.passing[index])
        return [self.piece]

    def left(self):
        return len(self.passing) - self.place

    def finish(self, after=()):
        while self.left():
            self.advance(after)
        return self.piece, self.flying


class Gather:
    def __init__(self, links, up, up_bias, down):
        self.links = links
        width, hidden = up.shape
        self.width, self.hidden = width, hidden
        self.wide = hidden // width
        cut, deep, wide = width // 8, hidden // 8, self.wide
        rows = wide * cut + deep + 16
        y, z = links.y, links.z[0]
        self.near = [(z, y), (y, z)]
        places = [links.at(name) for name in ("core", (y, z), (z, y))]
        self.sent = None

        def kernel(table_ref, bias_ref, up_ref, down_ref, *refs):
            outs, (up_cuts, down_cuts, sems) = refs[:2], refs[2:]
            place = sum(table_ref[at] * weight for at, weight in zip(places, (4, 2, 1)))
            copies = []
            for i, eighth in enumerate((place, place ^ 3)):
                for j, (ref, size, cuts) in enumerate(((up_ref, cut, up_cuts), (down_ref, deep, down_cuts))):
                    from_rows = ref.at[tile_rows(eighth * size, size), :]
                    copies.append(pltpu.make_async_copy(from_rows, cuts.at[i], sems.at[2 * i + j]))
            for copy in copies:
                copy.start()
            lines, rest = [], flat_line(bias_ref)
            for _ in range(3):
                term = rest.astype(BF).astype(F32)
                lines += [term[:, i * width : (i + 1) * width] for i in range(wide)]
                rest = rest - term
            lines.append(jnp.zeros((16 - len(lines), width), F32))
            for out_ref in outs:
                out_ref[rows - 16 :, :] = jnp.concatenate(lines).astype(BF)
            for copy in copies:
                copy.wait()
            for i, out_ref in enumerate(outs):
                for j in range(wide):
                    out_ref[j * cut : (j + 1) * cut, :] = up_cuts[i, :, j * width : (j + 1) * width]
                out_ref[wide * cut : wide * cut + deep, :] = down_cuts[i]

        near, anywhere = pl.BlockSpec(memory_space=pltpu.VMEM), pl.BlockSpec(memory_space=pl.ANY)
        self.mine = pl.pallas_call(
            kernel,
            in_specs=[pl.BlockSpec(memory_space=pltpu.SMEM), near, anywhere, anywhere],
            out_specs=[near, near],
            out_shape=[pltpu.VMEM((rows, width), BF)] * 2,
            scratch_shapes=[
                pltpu.VMEM((2, cut, hidden), BF),
                pltpu.VMEM((2, deep, width), BF),
                pltpu.SemaphoreType.DMA((4,)),
            ],
            compiler_params=pltpu.CompilerParams(vmem_limit_bytes=6 * 2**20),
        )(links.table, up_bias, *(pltpu.with_memory_space_constraint(t, pltpu.HBM) for t in (up, down)))

    def advance(self, after=()):
        links = self.links
        if self.sent is None:
            seg = links.seg[0]
            self.first, self.last = (links.swap(t, seg, seg) for t in self.mine)
            self.sent = list(self.mine)
        elif len(self.sent) == 2:
            self.between = [links.swap(self.first, *masks) for masks in self.near]
            self.sent = [self.first]
        else:
            eighths = [self.first, *self.between, self.last]
            rows, width = self.first.shape

            def kernel(*refs):
                for i, ref in enumerate(refs[:4]):
                    refs[4][i * rows : (i + 1) * rows, :] = ref[...]

            self.piece = kernel_call(
                kernel, 1, eighths, shape_of((4 * rows, width), BF), after=after, vmem=PASS_MIB
            )
            self.flying = links.swap(self.piece, links.core, links.core)
            self.sent = [self.piece]
        return self.sent

    def finish(self, after=()):
        links, width, hidden, wide = self.links, self.width, self.hidden, self.wide
        cut, deep = width // 8, hidden // 8
        rows = wide * cut + deep + 16
        y, z = links.y, links.z[0]
        at_core, at_first, at_second = (links.at(name) for name in ("core", (y, z), (z, y)))

        def kernel(table_ref, piece_ref, got_ref, up_ref, bias_ref, down_ref):
            core, first, second = table_ref[at_core], table_ref[at_first], table_ref[at_second]
            for ref, start in (
                (piece_ref, core * 4 + first * 2 + second),
                (got_ref, (1 - core) * 4 + second * 2 + first),
            ):
                for i in range(4):
                    place = start ^ i
                    at = tile_rows(place * cut, cut)
                    for j in range(wide):
                        from_row = i * rows + j * cut
                        up_ref[at, j * width : (j + 1) * width] = ref[from_row : from_row + cut, :]
                    from_row = i * rows + wide * cut
                    down_ref[tile_rows(place * deep, deep), :] = ref[from_row : from_row + deep, :]
            lines = piece_ref[rows - 16 : rows, :].astype(F32)
            parts = [sum(lines[i * wide + j : i * wide + j + 1] for i in range(3)) for j in range(wide)]
            bias_ref[...] = jnp.concatenate(parts, 1).reshape(hidden)

        return kernel_call(
            kernel,
            2,
            [links.table, self.piece, self.flying],
            [shape_of((width, hidden), BF), shape_of((hidden,), F32), shape_of((hidden, width), BF)],
            scalars=1,
            after=after,
            vmem=10,
        )


class GatherAny:
    def __init__(self, *args):
        self.args = args

    def advance(self, after=()):
        return []

    def finish(self, after=()):
        return other_shards(*self.args)


def other_shards(links, up, up_bias, down):
    shards = links.shards
    hidden = down.shape[0]
    ups = lax.all_gather(up, "seg", axis=0)
    downs = lax.all_gather(down, "seg", axis=0)
    biases = lax.all_gather(up_bias.reshape(1, -1), "seg", axis=0)
    order = lax.axis_index("seg") ^ jnp.arange(1, shards)
    ups = jnp.moveaxis(jnp.take(ups, order, axis=0), 0, 1).reshape(up.shape[0], -1)
    return ups, jnp.take(biases, order, axis=0).reshape(-1), jnp.take(downs, order, axis=0).reshape(-1, down.shape[1])


def pack_small(links, vec_ffn, vec_attn, g_lines, bias_send, bias_keep, send):
    width = vec_ffn.shape[1]
    shards = links.shards
    if shards != 2 or bias_send.shape[1] != 2 * width or not tiled(send.shape[0]):
        halves = ordered(links.numbers["core"] == 1, bias_keep, bias_send).reshape(2, shards, -1)
        by_shard = jnp.moveaxis(halves, 0, 1).reshape(shards, -1)
        by_shard = jnp.take(by_shard, jnp.arange(shards) ^ lax.axis_index("seg"), axis=0).reshape(-1, width)
        lines = [
            in_lanes([g[:, i * 3 * PAIR : (i + 1) * 3 * PAIR] for g in g_lines for i in range(2)], i) for i in (0, 2)
        ]
        small = jnp.concatenate([vec_ffn[:3], vec_attn[:3], *lines, by_shard])
        pad = -(-small.shape[0] // 16) * 16 - small.shape[0]
        small = jnp.pad(small, ((0, pad), (0, 0))).astype(BF)
        return jnp.concatenate([send, small]), small
    at_core, at_seg = links.at("core"), links.at("seg")
    rows = send.shape[0]

    def kernel(table_ref, send_ref, ffn_ref, attn_ref, *rest):
        line_refs, (bias_send_ref, bias_keep_ref, out_ref, small_ref, rows_ref) = rest[:-5], rest[-5:]
        rows_ref[...] = jnp.zeros_like(rows_ref)
        rows_ref[0:3, :] = ffn_ref[0:3, :]
        rows_ref[3:6, :] = attn_ref[0:3, :]
        for g, line_ref in enumerate(line_refs):
            for i in range(2):
                for row, part in ((6, 0), (7, 2)):
                    at = (3 * i + part) * PAIR
                    place = (2 * g + i) * PAIR
                    rows_ref[row : row + 1, place : place + PAIR] = line_ref[:, at : at + PAIR]
        for ref, half in ((bias_send_ref, 1 - table_ref[at_core]), (bias_keep_ref, table_ref[at_core])):
            for i in range(2):
                row = 8 + 2 * (table_ref[at_seg] ^ i) + half
                rows_ref[pl.ds(row, 1), :] = ref[:, i * width : (i + 1) * width]
        small_ref[...] = rows_ref[...].astype(BF)
        out_ref[:rows, :] = send_ref[...]
        out_ref[rows:, :] = small_ref[...]

    return kernel_call(
        kernel,
        1,
        [links.table, send, vec_ffn, vec_attn, *g_lines, bias_send, bias_keep],
        [shape_of((rows + 16, width), BF), shape_of((16, width), BF)],
        scalars=1,
        scratch_shapes=[pltpu.VMEM((16, width), F32)],
        vmem=PASS_MIB,
    )


def ffn_output(links, pair, turned, after):
    rows, width = pair[0].shape
    if rows % PAIR:
        array = ordered(links.numbers["core"] == 1, *pair).astype(F32)
        return [array.T if turned else array]
    at_core = links.at("core")
    halves = [slice(0, rows), slice(rows, 2 * rows)]
    parts = [(slice(None), h) if turned else (h,) for h in halves]

    def kernel(leave, mask_ref, mine_ref, other_ref, out_ref):
        choose = either(mask_ref, at_core, width)
        for i, order in enumerate(((other_ref, mine_ref), (mine_ref, other_ref))):
            values = choose(order[0][...], order[1][...]).astype(F32)
            out_ref[parts[i]] = values.T if turned else values
            leave(i)

    shape = (width, 2 * rows) if turned else (2 * rows, width)
    return leaving_call(kernel, 9, [links.masks, *pair], shape_of(shape, F32), parts, after, 10)


def square_outputs(links, first, groups, begin, before, small, hidden, after):
    given = [t for pair in [*first, *groups] for t in pair]
    width = given[0].shape[1]
    wide = 2 * PAIR
    at_core, at_seg = links.at("core"), links.at("seg")
    lines = hidden // width
    many = len(first) + len(groups)
    smalls = [] if small is None else [small]

    def kernel(mask_ref, *refs):
        refs = list(refs)
        pairs = [refs[2 * i : 2 * i + 2] for i in range(many)]
        small_refs = refs[2 * many : 2 * many + len(smalls)]
        refs = refs[2 * many + len(smalls) + len(before) + len(after) :]
        *outs, sems = refs
        token = outs.pop(len(outs) - 3 * many - len(first) - 1)
        token[...] = jnp.zeros_like(token)
        outs, scratch = outs[: len(outs) - 3 * many - len(first)], outs[len(outs) - 3 * many - len(first) :]
        choose = either(mask_ref, at_core, width)
        copies = []

        def leave(values, out, lanes):
            buffer = scratch[len(copies)]
            buffer[...] = values
            copy = pltpu.make_async_copy(buffer, out.at[:, lanes], sems.at[len(copies)])
            copy.start()
            copies.append(copy)

        for number, (mine, other) in enumerate(pairs):
            group = number + begin
            if first and number == 0:
                leave(choose(other[...], mine[...]).astype(F32), outs[3], slice(0, width))
                values = choose(mine[...], other[...])
            else:
                values = jnp.concatenate([choose(other[...], mine[...]), choose(mine[...], other[...])])
            for i in range(3):
                parts = [values[:, (3 * j + i) * PAIR : (3 * j + i + 1) * PAIR] for j in range(2)]
                leave(jnp.concatenate(parts, 1).astype(F32), outs[i], slice(group * wide, (group + 1) * wide))
        if small_refs:
            vector_outs, bias_out = outs[3:11], outs[11]
            rows = small_refs[0][...].astype(F32)
            for i, out_ref in enumerate(vector_outs):
                out_ref[...] = rows[i : i + 1].reshape(width)
            by_shard = [
                jnp.concatenate([rows[8 + n * lines + i : 9 + n * lines + i] for i in range(lines)], 1)
                for n in range(2)
            ]
            bias_out[...] = either(mask_ref, at_seg, hidden)(by_shard[1], by_shard[0]).reshape(hidden)
        for copy in copies:
            copy.wait()

    square, vector = pltpu.HBM((width, width), F32), shape_of((width,), F32)
    anywhere, near = pl.BlockSpec(memory_space=pl.ANY), pl.BlockSpec(memory_space=pltpu.VMEM)
    far = pl.BlockSpec(memory_space=pltpu.HBM)
    outs, out_specs = [square] * 3, [far] * 3
    if first:
        outs, out_specs = outs + [square], out_specs + [far]
    if smalls:
        outs, out_specs = outs + [vector] * 8 + [shape_of((hidden,), F32)], out_specs + [near] * 9
    outs, out_specs = outs + [TOKEN], out_specs + [near]
    scratch = []
    for number in range(many):
        if first and number == 0:
            scratch.append(pltpu.VMEM((width, width), F32))
        scratch += [pltpu.VMEM((width, wide), F32)] * 3
    operands = [links.masks, *given, *smalls]
    return pl.pallas_call(
        kernel,
        in_specs=[near] * len(operands) + [far] * len(before) + [anywhere] * len(after),
        out_specs=out_specs,
        out_shape=outs,
        scratch_shapes=scratch + [pltpu.SemaphoreType.DMA((len(scratch),))],
        input_output_aliases={len(operands) + i: i for i in range(len(before))},
        compiler_params=pltpu.CompilerParams(vmem_limit_bytes=16 * 2**20),
        cost_estimate=pl.CostEstimate(flops=9 * 10**9, bytes_accessed=1 << 20, transcendentals=0),
    )(*operands, *before, *after)


def attention_outputs_any(links, first, groups, small, hidden):
    on_core1 = links.numbers["core"] == 1
    whole = [ordered(on_core1, *pair) for pair in (first, *groups)]
    width = whole[0].shape[1]
    grads = [whole[0][width:], *whole[1:]]
    pairs = [g[:, i * 3 * PAIR : (i + 1) * 3 * PAIR] for g in grads for i in range(2)]
    small = small.astype(F32)
    biases = small[8 : 8 + hidden * links.shards // width].reshape(links.shards, -1)
    bias = lax.dynamic_index_in_dim(biases, lax.axis_index("seg"), keepdims=False)
    squares = [in_lanes(pairs, i).astype(F32) for i in range(3)]
    return [whole[0][:width].astype(F32), *squares, *[small[i] for i in range(8)], bias]


def in_halves(array, axis, shards):
    shape = list(array.shape)
    parts = array.reshape(shape[:axis] + [shards, 2, -1] + shape[axis + 1 :])
    return jnp.moveaxis(parts, axis + 1, axis).reshape(shape)


def body(
    activations,
    tok_count,
    w_query,
    w_key,
    w_value,
    w_proj,
    b_query,
    b_value,
    b_proj,
    gain_attn,
    shift_attn,
    w_up,
    b_up,
    w_down,
    b_down,
    gain_ffn,
    shift_ffn,
    cotangent,
    items,
    shards,
):
    slots, rows, width = activations.shape
    links = Links(items, shards)
    count = tok_count[:, 0]
    more = ((0, 0), (0, -rows % 16), (0, 0))
    x, cot = jnp.pad(activations, more), jnp.pad(cotangent, more)
    own = (w_up, b_up, w_down)
    hidden = w_up.shape[1]
    every = hidden * shards
    weights = (Gather if shards == 2 and links.z else GatherAny)(links, *own)

    state, done = [], [cot]
    for slot in range(slots):
        weights_in = [w_query, w_key, w_value]
        after = weights.advance(done) + done
        state.append(attend(rows, slot, count, x, weights_in, [b_query, b_value], after))
        done = [state[-1][-1]]
    q, extra, k, v, ctx, bias = zip(*state)
    normed, xhat, rstd = first_norm(x, w_proj, [b_proj, gain_attn, shift_attn], ctx, done)
    done = [rstd[-1]]
    act0, slope0, first = ffn_first(normed, own, weights.advance(done) + done)
    others = weights.finish([first])
    act1, slope1, layer_out, g_sum, g_branch, vec_ffn = ffn_last(
        rows, count, normed, others, first, cot, [b_down, gain_ffn, shift_ffn]
    )
    acts, slopes = [act0, act1], [slope0, slope1]
    if shards == 2:
        pieces = [own[2], own[0], others[2], others[0]]
    else:
        acts, slopes = ([in_halves(jnp.concatenate(t, 1), 1, shards)] * 2 for t in (acts, slopes))
        ups = in_halves(jnp.concatenate([own[0], others[0]], 1), 1, shards)
        downs = in_halves(jnp.concatenate([own[2], others[2]]), 0, shards)
        pieces = [downs, ups, downs, ups]

    done = [vec_ffn]
    made, sums = {}, {}
    d_parts, g_lines, small = [], [], None
    arrays = [q, extra, k, v, ctx]
    count_pairs = width // PAIR
    whole_tiles = shards == 2 and tiled(width >> (len(links.steps) - 1))

    def step(name):
        nonlocal done
        sent = sums[name].advance(done)
        done = sent if sums[name].place > 1 else done + sent

    def run(name):
        nonlocal done, small
        if name == "down send":
            made["down"] = [down_grad(links, 1, acts, g_branch, every, done)]
            done = made["down"]
        elif name == "down keep":
            made["down"].append(down_grad(links, 0, acts, g_branch, every, done))
            sums["down"] = Sum(links, True, made["down"])
            done = made["down"][1:]
        elif name == "up send":
            *made["up send"], made["g_norm"] = up_grad(links, 1, g_branch, normed, slopes, pieces, every, [], done)
            done = [made["g_norm"]]
        elif name == "up keep":
            *made["up keep"], made["g_norm"] = up_grad(
                links, 0, g_branch, normed, slopes, pieces, every, [made["g_norm"]], done
            )
            sums["up"] = Sum(links, True, (made["up send"][0], made["up keep"][0]))
            done = [made["g_norm"]]
        elif name == "proj":
            made["g_pre"], made["g_ctx"], made["g_proj"], made["vec"] = proj_grad(
                g_sum, made["g_norm"], w_proj, gain_attn, xhat, rstd, ctx, done
            )
            done = [made["vec"]]
        elif name == "pair":
            pair = len(d_parts)
            before = None if pair % 2 == 0 else d_parts[-1]
            beside = [made["g_proj"]] if pair == 1 else []
            d, *rest = attend_back(links, pair, made["g_ctx"], arrays, bias, x, before, beside, done)
            d_parts.append(d)
            done = [d]
            if rest:
                send, keep, lines = rest
                g_lines.append(lines)
                if pair == count_pairs - 1:
                    hidden_bias = [made[n][1] for n in ("up send", "up keep")]
                    send, small = pack_small(links, vec_ffn, made["vec"], g_lines, *hidden_bias, send)
                    done = [small]
                sums["heads %d" % (pair // 2)] = Sum(links, False, (send, keep), small)
        elif name == "input":
            made["input"], *done = input_grad(
                rows, made["g_pre"], d_parts, [w_query, w_key, w_value], done
            )
        elif name == "layer":
            made["layer"], *done = slots_last(layer_out, rows, done)
        elif name in ("down out", "up out"):
            pair = sums[name[:-3] + "back"].finish()
            made[name], *done = ffn_output(links, pair, name == "up out", done)
        elif name == "squares":
            if whole_tiles:
                pairs = [sums["heads %d" % i].finish() for i in range(count_pairs // 2 - 1)]
                *made["squares"], token = square_outputs(links, pairs[:1], pairs[1:], 0, [], None, hidden, done)
                done = [token]
        elif name in ("down back", "up back") and name not in sums:
            sums[name] = Merged(links, [sums[name[:-5]]])
            step(name)
        elif sums[name].left():
            step(name)

    for name in PLAN:
        run(name)
    for name in ("down back", "up back"):
        if name not in sums:
            run(name)
    while any(s.left() for s in sums.values()):
        for s in sums.values():
            if s.left():
                s.advance([])
    for name in ("down out", "up out", "squares", "layer"):
        if name not in made:
            run(name)
    grad_w_down, grad_w_up = made["down out"], made["up out"]
    layer_out, grad_input = (jnp.transpose(t, (1, 0, 2)) for t in (made["layer"], made["input"]))
    last = sums["heads %d" % (count_pairs // 2 - 1)]
    if whole_tiles:
        *squares, g_proj = made["squares"]
        g_query, g_key, g_value, *vectors, grad_b_up, _ = square_outputs(
            links, [], [last.finish()], count_pairs // 2 - 1, squares, last.small, hidden, []
        )
    else:
        pairs = [sums["heads %d" % i].finish() for i in range(count_pairs // 2)]
        g_proj, g_query, g_key, g_value, *vectors, grad_b_up = attention_outputs_any(
            links, pairs[0], pairs[1:], last.small, hidden
        )
    g_gain_ffn, g_shift_ffn, g_b_down, g_gain_attn, g_shift_attn, g_b_proj, g_b_query, g_b_value = vectors
    return (
        layer_out,
        grad_input,
        g_query,
        g_key,
        g_value,
        g_proj,
        g_b_query,
        g_b_value,
        g_b_proj,
        g_gain_attn,
        g_shift_attn,
        grad_w_up,
        grad_b_up,
        grad_w_down,
        g_b_down,
        g_gain_ffn,
        g_shift_ffn,
    )


def solution(mesh):
    rows, everywhere = P("dp", "seg", None), P()
    return jax.shard_map(
        functools.partial(body, items=mesh.shape["dp"], shards=mesh.shape["seg"]),
        mesh=mesh,
        in_specs=(rows, P("dp", "seg"))
        + (everywhere,) * 9
        + (P(None, "seg"), P("seg"), P("seg", None))
        + (everywhere,) * 3
        + (rows,),
        out_specs=(rows, rows)
        + (everywhere,) * 9
        + (P(None, "seg"), P("seg"), P("seg", None))
        + (everywhere,) * 3,
        check_vma=False,
    )
```

```python
import functools
import math

import jax
import jax.numpy as jnp
from jax import lax
from jax.experimental import pallas as pl
from jax.experimental.pallas import tpu as pltpu
from jax.sharding import PartitionSpec as P

HEAD = 64
MEM = 10
EPSILON = 1e-05
NEG_BIG = -1e30
PAIR = 2 * HEAD
BF = jnp.bfloat16
F32 = jnp.float32
VMEM_MIB = 16
PASS_MIB = 5
ATTEND_MIB = 9
FFN_MIB = 9
DOWN_MIB = 5
UP_MIB = 6
BACK_MIB = 5
JOINT = ("dp", "seg")
WIDE = (1, 2)
TOKEN = jax.ShapeDtypeStruct((8, PAIR), F32)
PLAN = (
    "down send", "down keep", "down", "up send", "down", "up keep", "proj", "down", "up", "pair", "up",
    "down", "pair", "pair", "down", "up", "heads 0", "pair", "heads 1", "heads 0", "up", "pair", "down back",
    "heads 0", "heads 1", "up", "pair", "heads 2", "heads 1", "layer", "heads 2", "down back", "heads 0",
    "heads 1", "heads 2", "up back", "heads 0", "input", "up back", "heads 1", "heads 2", "heads 0",
    "down back", "heads 2", "heads 1", "heads 0", "down out", "heads 2", "heads 1", "heads 0", "up back",
    "heads 2", "heads 1", "up out", "heads 0", "heads 2", "heads 1", "squares", "heads 2",
)


def nn(left, right):
    return jnp.dot(left, right, preferred_element_type=F32)


def tn(left, right):
    return lax.dot_general(left, right, (((0,), (0,)), ((), ())), preferred_element_type=F32)


def nt(left, right):
    return lax.dot_general(left, right, (((1,), (1,)), ((), ())), preferred_element_type=F32)


def colsum(values):
    return jnp.sum(values, 0, keepdims=True)


def rowmean(values):
    return jnp.mean(values, -1, keepdims=True)


def kernel_call(kernel, micros, operands, out_shape, scalars=0, after=(), scratch_shapes=(), vmem=VMEM_MIB, far=()):
    many = len(operands)
    anywhere = pl.BlockSpec(memory_space=pl.ANY)
    near = pl.BlockSpec(memory_space=pltpu.VMEM)

    def run(*refs):
        kernel(*refs[:many], *refs[many + len(after) :])

    specs = [pl.BlockSpec(memory_space=pltpu.SMEM) if i < scalars else near for i in range(many)]
    outs = out_shape if isinstance(out_shape, list) else [out_shape]
    outs = [t if i in far else pltpu.VMEM(t.shape, t.dtype) for i, t in enumerate(outs)]
    results = pl.pallas_call(
        run,
        in_specs=specs + [anywhere] * len(after),
        out_specs=[near] * len(outs),
        out_shape=outs,
        scratch_shapes=scratch_shapes,
        compiler_params=pltpu.CompilerParams(vmem_limit_bytes=vmem * 2**20),
        cost_estimate=pl.CostEstimate(
            flops=int(micros * 1.0e9), bytes_accessed=1 << 20, transcendentals=0
        ),
    )(*operands, *after)
    return results if isinstance(out_shape, list) else results[0]


def leaving_call(kernel, micros, operands, out_shape, parts, after, vmem):
    def run(*refs):
        ins, (out, token, buffer, sems) = refs[: len(operands)], refs[-4:]
        token[...] = jnp.zeros_like(token)
        copies = [pltpu.make_async_copy(buffer.at[part], out.at[part], sems.at[i]) for i, part in enumerate(parts)]
        kernel(lambda i: copies[i].start(), *ins, buffer)
        for copy in copies:
            copy.wait()

    near, anywhere = pl.BlockSpec(memory_space=pltpu.VMEM), pl.BlockSpec(memory_space=pl.ANY)
    return pl.pallas_call(
        run,
        in_specs=[near] * len(operands) + [anywhere] * len(after),
        out_specs=[pl.BlockSpec(memory_space=pltpu.HBM), near],
        out_shape=[pltpu.HBM(out_shape.shape, out_shape.dtype), TOKEN],
        scratch_shapes=[pltpu.VMEM(out_shape.shape, out_shape.dtype), pltpu.SemaphoreType.DMA((len(parts),))],
        compiler_params=pltpu.CompilerParams(vmem_limit_bytes=vmem * 2**20),
        cost_estimate=pl.CostEstimate(
            flops=int(micros * 1.0e9), bytes_accessed=1 << 20, transcendentals=0
        ),
    )(*operands, *after)


def shape_of(shape, dtype):
    return jax.ShapeDtypeStruct(shape, dtype)


def like(array):
    return shape_of(array.shape, array.dtype)


def flat_line(ref):
    return ref[...].reshape(1, -1)


def either(mask_ref, at, width):
    mask = jnp.concatenate([mask_ref[at : at + 1, :]] * (width // PAIR), 1) > 0.5

    def choose(one, zero):
        return jnp.where(jnp.broadcast_to(mask, one.shape), one, zero)

    return choose


def tile_rows(start, rows):
    return pl.ds(pl.multiple_of(start, 16), rows)


def tile_lanes(start, lanes):
    return pl.ds(pl.multiple_of(start, PAIR), lanes)


def key_bias(count, rows, padded):
    row = lax.broadcasted_iota(jnp.int32, (padded, PAIR), 0)
    valid = ((row < MEM + count) | (row >= rows - MEM)) & (row < rows)
    return jnp.where(valid, 0.0, NEG_BIG).astype(BF)


def attend_kernel(
    rows,
    slot,
    count_ref,
    x_ref,
    wq_ref,
    wk_ref,
    wv_ref,
    bq_ref,
    bv_ref,
    q_ref,
    aux_ref,
    k_ref,
    v_ref,
    ctx_ref,
    bias_ref,
):
    padded, width = x_ref.shape[1:]
    x = x_ref[slot]
    q_ref[...] = ((nn(x, wq_ref[...]) + flat_line(bq_ref)) * (1.0 / math.sqrt(HEAD))).astype(BF)
    k_ref[...] = nn(x, wk_ref[...]).astype(BF)
    v_ref[...] = (nn(x, wv_ref[...]) + flat_line(bv_ref)).astype(BF)
    lane = lax.broadcasted_iota(jnp.int32, (padded, PAIR), 1)
    bias_ref[...] = key_bias(count_ref[slot], rows, padded)
    bias = bias_ref[...]
    one = jnp.ones((), BF)
    zero = jnp.zeros((), BF)
    for pair in range(width // PAIR):
        lanes = slice(pair * PAIR, (pair + 1) * PAIR)
        q, k, v = q_ref[:, lanes], k_ref[:, lanes], v_ref[:, lanes]
        contexts, extras = [], []
        for head in range(2):
            own = (lane < HEAD) if head == 0 else (lane >= HEAD)
            aux = HEAD if head == 0 else 0
            at_aux = jnp.where(lane == aux, one, zero)
            scores = nt(
                jnp.where(own, q, at_aux),
                jnp.where(own, k, jnp.where(lane == aux, bias, zero)),
            )
            top = jnp.max(scores, -1, keepdims=True)
            exps = jnp.exp(scores - top).astype(BF)
            weighted = nn(exps, jnp.where(own, v, at_aux))
            total = weighted[:, aux : aux + 1]
            contexts.append(weighted * (1.0 / total))
            rest = -(top + jnp.log(total))
            high = rest.astype(BF)
            rest = rest - high.astype(F32)
            middle = rest.astype(BF)
            low = (rest - middle.astype(F32)).astype(BF)
            extras.append(
                jnp.where(
                    lane == aux + 1,
                    high,
                    jnp.where(lane == aux + 2, middle, jnp.where(lane == aux + 3, low, at_aux)),
                )
            )
        ctx_ref[:, lanes] = jnp.where(lane < HEAD, contexts[0], contexts[1]).astype(BF)
        aux_ref[:, lanes] = jnp.where(lane < HEAD, extras[1], extras[0])


def attend(rows, slot, count, x, weights, vectors, after):
    array = shape_of(x.shape[1:], BF)
    return kernel_call(
        functools.partial(attend_kernel, rows, slot),
        9,
        [count, x, *weights, *vectors],
        [array] * 5 + [shape_of((x.shape[1], PAIR), BF)],
        scalars=1,
        after=after,
        vmem=ATTEND_MIB,
    )


def first_norm_kernel(slots, x_ref, wp_ref, bp_ref, gain_ref, shift_ref, *refs):
    ctx_refs, normed_refs, xhat_refs, rstd_refs = (refs[i * slots : (i + 1) * slots] for i in range(4))
    for slot in range(slots):
        pre_norm = x_ref[slot].astype(F32) + nn(ctx_refs[slot][...], wp_ref[...]) + flat_line(bp_ref)
        center = pre_norm - rowmean(pre_norm)
        rstd = lax.rsqrt(rowmean(center * center) + EPSILON)
        xhat = center * rstd
        normed_refs[slot][...] = (xhat * flat_line(gain_ref) + flat_line(shift_ref)).astype(BF)
        xhat_refs[slot][...] = xhat.astype(BF)
        rstd_refs[slot][...] = rstd


def first_norm(x, wp, vectors, ctx, after):
    slots, padded, width = x.shape
    array, column = shape_of((padded, width), BF), shape_of((padded, 1), F32)
    out = kernel_call(
        functools.partial(first_norm_kernel, slots),
        3,
        [x, wp, *vectors, *ctx],
        [array] * (2 * slots) + [column] * slots,
        after=after,
        vmem=FFN_MIB,
    )
    return [out[i * slots : (i + 1) * slots] for i in range(3)]


def hidden_units(n_refs, up_ref, ub_ref, act_ref, slope_ref):
    size = up_ref.shape[1]
    bias = flat_line(ub_ref)
    cut = math.gcd(256, size)
    padded = n_refs[0].shape[0]
    for at in range(0, size, cut):
        part = slice(at, at + cut)
        for slot, n_ref in enumerate(n_refs):
            rows = slice(slot * padded, (slot + 1) * padded)
            pre = nn(n_ref[...], up_ref[:, part]) + bias[:, part]
            cdf = 0.5 + 0.5 * lax.erf(pre * math.sqrt(0.5))
            act_ref[rows, part] = (pre * cdf).astype(BF)
            slope = cdf + pre * (jnp.exp(-0.5 * (pre * pre)) * (1.0 / math.sqrt(2.0 * math.pi)))
            slope_ref[rows, part] = slope.astype(BF)


def ffn_first_kernel(slots, *refs):
    up_ref, ub_ref, down_ref, act_ref, slope_ref, sum_ref = refs[slots:]
    hidden_units(refs[:slots], up_ref, ub_ref, act_ref, slope_ref)
    sum_ref[...] = nn(act_ref[...], down_ref[...])


def ffn_last_kernel(rows, slots, count_ref, *refs):
    n_refs, refs = refs[:slots], refs[slots:]
    up_ref, ub_ref, down_ref, first_ref, cot_ref, bd_ref, gain_ref, shift_ref, *refs = refs
    act_ref, slope_ref, out_ref, gsum_ref, gbranch_ref, vec_ref = refs
    hidden_units(n_refs, up_ref, ub_ref, act_ref, slope_ref)
    padded, width = n_refs[0].shape
    row = lax.broadcasted_iota(jnp.int32, (padded, width), 0)
    gain = flat_line(gain_ref)
    sums = [jnp.zeros((1, width), F32)] * 3
    for slot, n_ref in enumerate(n_refs):
        part = slice(slot * padded, (slot + 1) * padded)
        count = count_ref[slot]
        keep = ((row < MEM + count) | (row >= rows - MEM)) & (row < rows) & (count > 0)
        branch = first_ref[part, :] + nn(act_ref[part, :], down_ref[...])
        summed = n_ref[...].astype(F32) + branch + flat_line(bd_ref)
        center = summed - rowmean(summed)
        rstd = lax.rsqrt(rowmean(center * center) + EPSILON)
        xhat = center * rstd
        out_ref[slot] = jnp.where(keep, xhat * gain + flat_line(shift_ref), 0.0).astype(BF)
        g_out = jnp.where(keep, cot_ref[slot].astype(F32), 0.0)
        g_xhat = g_out * gain
        g_sum = rstd * (g_xhat - rowmean(g_xhat) - xhat * rowmean(g_xhat * xhat))
        gsum_ref[part, :] = g_sum
        gbranch_ref[part, :] = g_sum.astype(BF)
        new = (colsum(g_out * xhat), colsum(g_out), colsum(g_sum))
        sums = [a + b for a, b in zip(sums, new)]
    vec_ref[...] = jnp.concatenate(sums + [jnp.zeros((5, width), F32)])


def ffn_first(normed, own, after):
    total, width = len(normed) * normed[0].shape[0], normed[0].shape[1]
    acts = shape_of((total, own[0].shape[1]), BF)
    return kernel_call(
        functools.partial(ffn_first_kernel, len(normed)),
        7.5,
        [*normed, *own],
        [acts, acts, shape_of((total, width), F32)],
        after=after,
        vmem=FFN_MIB,
    )


def ffn_last(rows, count, normed, others, first, cot, vectors):
    total, width = first.shape
    acts = shape_of((total, others[0].shape[1]), BF)
    return kernel_call(
        functools.partial(ffn_last_kernel, rows, len(normed)),
        10.5,
        [count, *normed, *others, first, cot, *vectors],
        [
            acts,
            acts,
            shape_of(cot.shape, BF),
            shape_of(first.shape, F32),
            shape_of(first.shape, BF),
            shape_of((8, width), F32),
        ],
        scalars=1,
        vmem=FFN_MIB,
    )


def slots_last(array, rows, after):
    slots, _, width = array.shape
    parts = row_parts(rows)

    def kernel(leave, in_ref, out_ref):
        for i, (part,) in enumerate(parts):
            for slot in range(slots):
                out_ref[part, slot, :] = in_ref[slot, part, :]
            leave(i)

    return leaving_call(kernel, 8, [array], shape_of((rows, slots, width), array.dtype), parts, after, 8)


def row_parts(rows):
    cut = rows // 32 * 16
    return [(slice(0, cut),), (slice(cut, rows),)]


def store_half(piece_ref, values, step, half, unit, shards):
    per = values.shape[0] // unit
    for i in range(per):
        block = step * per + i
        shard, y = block // 2, block % 2
        low, high = shard % 2, shard // 2
        place = jnp.where(half == 0, low * 2 + y, y * 2 + low) * (shards // 2) + high
        piece_ref[tile_rows(place * unit, unit), :] = values[i * unit : (i + 1) * unit].astype(BF)


def block_start(shards, j, half, size):
    return half * size if shards == 2 else (half * 2 + j) * size


def down_grad_kernel(unit, shards, other, at, table_ref, act0_ref, act1_ref, g_ref, piece_ref):
    half = table_ref[at] ^ other
    size = piece_ref.shape[0] // 2
    for j, act_ref in enumerate((act0_ref, act1_ref)):
        act = act_ref[:, tile_lanes(block_start(shards, j, half, size), size)]
        store_half(piece_ref, tn(act, g_ref[...]), j, half, unit, shards)


def down_grad(links, other, acts, g_branch, every, after):
    shards = links.shards
    return kernel_call(
        functools.partial(down_grad_kernel, every // shards // 4, shards, other, links.at("core")),
        4,
        [links.table, *acts, g_branch],
        shape_of((every // 2, g_branch.shape[1]), BF),
        scalars=1,
        after=after,
        vmem=DOWN_MIB,
    )


def up_grad_kernel(unit, shards, slots, other, at_core, table_ref, g_ref, *refs):
    n_refs, refs = refs[:slots], refs[slots:]
    slope0_ref, slope1_ref, down0_ref, up0_ref, down1_ref, up1_ref, *so_far, piece_ref, gb_ref, gn_ref, pre_ref = refs
    half = table_ref[at_core] ^ other
    size = piece_ref.shape[0] // 2
    cut = math.gcd(256, size)
    for j, (slope_ref, down_ref, up_ref) in enumerate(
        ((slope0_ref, down0_ref, up0_ref), (slope1_ref, down1_ref, up1_ref))
    ):
        start = block_start(shards, j, half, size)
        for at in range(0, size, cut):
            g_pre = nt(g_ref[...], down_ref[tile_rows(start + at, cut), :])
            g_pre = g_pre * slope_ref[:, tile_lanes(start + at, cut)].astype(F32)
            pre_ref[:, at : at + cut] = g_pre.astype(BF)
        normed = jnp.concatenate([ref[...] for ref in n_refs])
        store_half(piece_ref, tn(pre_ref[...], normed), j, half, unit, shards)
        gb_ref[:, j * size : (j + 1) * size] = colsum(pre_ref[...].astype(F32))
        share = nt(pre_ref[...], up_ref[:, tile_lanes(start, size)])
        if j:
            gn_ref[...] += share
        else:
            gn_ref[...] = so_far[0][...] + share if so_far else share


def up_grad(links, other, g_branch, normed, slopes, weights, every, so_far, after):
    total, width = g_branch.shape
    shards = links.shards
    return kernel_call(
        functools.partial(up_grad_kernel, every // shards // 4, shards, len(normed), other, links.at("core")),
        9.5,
        [links.table, g_branch, *normed, *slopes, *weights, *so_far],
        [
            shape_of((every // 2, width), BF),
            shape_of((1, every // 2), F32),
            shape_of((total, width), F32),
        ],
        scalars=1,
        after=after,
        scratch_shapes=[pltpu.VMEM((total, every // 4), BF)],
        vmem=UP_MIB,
    )


def proj_grad_kernel(slots, gsum_ref, gn_ref, wp_ref, gain_ref, *refs):
    xhat_refs, rstd_refs, ctx_refs = (refs[i * slots : (i + 1) * slots] for i in range(3))
    gpre_ref, gctx_ref, gw_ref, vec_ref, attn_ref = refs[3 * slots :]
    padded, width = xhat_refs[0].shape
    sums = [jnp.zeros((1, width), F32)] * 3
    for slot in range(slots):
        part = slice(slot * padded, (slot + 1) * padded)
        g_normed = gsum_ref[part, :] + gn_ref[part, :]
        xhat = xhat_refs[slot][...].astype(F32)
        g_xhat = g_normed * flat_line(gain_ref)
        g_pre = rstd_refs[slot][...] * (g_xhat - rowmean(g_xhat) - xhat * rowmean(g_xhat * xhat))
        gpre_ref[slot] = g_pre
        g_attn = g_pre.astype(BF)
        attn_ref[part, :] = g_attn
        gctx_ref[slot] = nt(g_attn, wp_ref[...]).astype(BF)
        new = (colsum(g_normed * xhat), colsum(g_normed), colsum(g_pre))
        sums = [a + b for a, b in zip(sums, new)]
    gw_ref[...] = tn(jnp.concatenate([ref[...] for ref in ctx_refs]), attn_ref[...]).astype(BF)
    vec_ref[...] = jnp.concatenate(sums + [jnp.zeros((5, width), F32)])


def proj_grad(g_sum, g_norm, wp, gain, xhat, rstd, ctx, after):
    slots, (padded, width) = len(xhat), xhat[0].shape
    return kernel_call(
        functools.partial(proj_grad_kernel, slots),
        4,
        [g_sum, g_norm, wp, gain, *xhat, *rstd, *ctx],
        [
            shape_of((slots, padded, width), F32),
            shape_of((slots, padded, width), BF),
            shape_of((width, width), BF),
            shape_of((8, width), F32),
        ],
        after=after,
        scratch_shapes=[pltpu.VMEM((slots * padded, width), BF)],
        vmem=UP_MIB,
    )


def attend_back_kernel(pair, slots, at_core, g_ref, *rest):
    arrays, bias_refs, rest = rest[: 5 * slots], rest[5 * slots : 6 * slots], rest[6 * slots :]
    x_ref = None
    if len(rest) > 1:
        x_ref, mask_ref, before_ref, *beside, d_ref, send_ref, keep_ref, vec_ref = rest
    else:
        (d_ref,) = rest
    padded = d_ref.shape[1]
    lanes = slice(pair * PAIR, (pair + 1) * PAIR)
    lane = lax.broadcasted_iota(jnp.int32, (padded, PAIR), 1)
    one = jnp.ones((), BF)
    zero = jnp.zeros((), BF)
    for slot in range(slots):
        bias = bias_refs[slot][...]
        g = g_ref[slot, :, lanes]
        q, extra, k, v, ctx = (ref[:, lanes] for ref in arrays[slot::slots])
        products = g.astype(F32) * ctx.astype(F32)
        parts = []
        for head in range(2):
            own = (lane < HEAD) if head == 0 else (lane >= HEAD)
            aux = HEAD if head == 0 else 0
            delta = -jnp.sum(jnp.where(own, products, 0.0), -1, keepdims=True)
            high = delta.astype(BF)
            low = (delta - high.astype(F32)).astype(BF)
            after = (lane > aux) & (lane < aux + 4)
            k_more = jnp.where(own, k, jnp.where(lane == aux, bias, jnp.where(after, one, zero)))
            v_more = jnp.where(own, v, jnp.where((lane >= aux) & (lane < aux + 2), one, zero))
            q_more = jnp.where(own, q, extra)
            g_more = jnp.where(own, g, jnp.where(lane == aux, high, jnp.where(lane == aux + 1, low, zero)))
            probs = jnp.exp(nt(k_more, q_more))
            g_scores = (probs * nt(v_more, g_more)).astype(BF)
            parts.append((tn(g_scores, k_more), nn(g_scores, q_more), nn(probs.astype(BF), g_more)))
        g_q, g_k, g_v = (jnp.where(lane < HEAD, a, b) for a, b in zip(*parts))
        g_q = (g_q.astype(BF).astype(F32) * (1.0 / math.sqrt(HEAD))).astype(BF)
        for i, part in enumerate((g_q, g_k.astype(BF), g_v.astype(BF))):
            d_ref[slot, :, i * PAIR : (i + 1) * PAIR] = part
    if x_ref is None:
        return
    both = slots * padded
    d = [ref[...].reshape(both, 3 * PAIR) for ref in (before_ref, d_ref)]
    d = jnp.concatenate(d, axis=1)
    g_weights = tn(x_ref[...].reshape(both, x_ref.shape[2]), d).astype(BF)
    vec_ref[...] = colsum(d.astype(F32))
    half = g_weights.shape[0] // 2
    first, second = (beside[0][...], g_weights) if beside else (g_weights[:half], g_weights[half:])
    choose = either(mask_ref, at_core, g_weights.shape[1])
    keep_ref[...] = choose(second, first)
    send_ref[...] = choose(first, second)


def attend_back(links, pair, g_ctx, arrays, bias, x, before, beside, after):
    slots, padded, width = g_ctx.shape
    operands = [g_ctx, *[t for of_slots in arrays for t in of_slots], *bias]
    outs = [shape_of((slots, padded, 3 * PAIR), BF)]
    if before is not None:
        operands += [x, links.masks, before, *beside]
        part = shape_of((width if beside else width // 2, 6 * PAIR), BF)
        outs += [part, part, shape_of((1, 6 * PAIR), F32)]
    return kernel_call(
        functools.partial(attend_back_kernel, pair, slots, links.at("core")),
        5 if before is None else 7,
        operands,
        outs,
        after=after,
        vmem=BACK_MIB,
    )


def in_lanes(pairs, i):
    return jnp.concatenate([p[..., i * PAIR : (i + 1) * PAIR] for p in pairs], axis=-1)


def input_grad(rows, g_pre, parts, weights, after):
    slots, _, width = g_pre.shape
    cuts = row_parts(rows)

    def kernel(leave, gpre_ref, *refs):
        d_refs, w_refs, out_ref = refs[: len(parts)], refs[len(parts) : len(parts) + 3], refs[-1]
        totals = []
        for slot in range(slots):
            total = gpre_ref[slot]
            for i, w_ref in enumerate(w_refs):
                total = total + nt(in_lanes([d[slot] for d in d_refs], i), w_ref[...])
            totals.append(total)
        for i, (cut,) in enumerate(cuts):
            for slot in range(slots):
                out_ref[cut, slot, :] = totals[slot][cut]
            leave(i)

    return leaving_call(
        kernel, 9, [g_pre, *parts, *weights], shape_of((rows, slots, width), F32), cuts, after, 14
    )


class Links:
    def __init__(self, items, shards):
        self.items, self.shards = items, shards
        self.joint = lax.axis_index("dp") * shards + lax.axis_index("seg")
        self.core = shards
        self.y = 2 * shards
        self.seg = [1 << i for i in range(shards.bit_length() - 1)]
        self.z = [shards << i for i in range(2, items.bit_length() - 1)]
        first = self.seg[0] if self.seg else self.y
        self.steps = (
            [(self.core, self.core), (first, self.y), (self.y, first)]
            + [(m, m) for m in reversed(self.seg[1:])]
            + [(m, m) for m in self.z]
        )
        self.numbers = {"core": self.bit(self.core, self.core), "seg": lax.axis_index("seg")}
        between = [(self.z[0], self.y), (self.y, self.z[0])] if self.z else []
        for masks in [*self.steps, *between, (self.y, self.y)]:
            self.numbers[masks] = self.bit(*masks)
        for masks in self.steps:
            self.numbers["own", masks] = self.keep_own(masks)
        self.names = list(self.numbers)
        self.table = jnp.stack(list(self.numbers.values())).astype(jnp.int32)
        self.masks = jnp.broadcast_to(self.table[:, None], (len(self.names), PAIR)).astype(F32)

    def at(self, name):
        return self.names.index(name)

    def swap(self, value, mask0, mask1):
        count = self.items * self.shards
        pairs = [(i, i ^ (mask1 if i & self.core else mask0)) for i in range(count)]
        return lax.ppermute(value, JOINT, pairs)

    def bit(self, mask0, mask1):
        on_core1 = (self.joint & self.core) != 0
        return jnp.where(on_core1, (self.joint & mask1) != 0, (self.joint & mask0) != 0).astype(jnp.int32)

    def keep_own(self, masks):
        own = [mask in self.seg for mask in masks]
        on_core1 = (self.joint & self.core) != 0
        return jnp.where(jnp.where(on_core1, own[1], own[0]), 0, self.bit(*masks))


def tiled(rows):
    return rows % 16 == 0


def ordered(late, a, b, axis=0):
    return jnp.concatenate([jnp.where(late, b, a), jnp.where(late, a, b)], axis=axis)


def add_halves(links, name, held, got, small, after):
    rows, width = held.shape
    half = rows // 2
    extra = 0 if small is None else small.shape[0]
    if not tiled(half):
        keep = links.numbers[name]
        total = held + got[:rows]
        send = lax.dynamic_slice_in_dim(total, (1 - keep) * half, half)
        held = lax.dynamic_slice_in_dim(total, keep * half, half)
        if extra:
            small = small + got[rows:]
            send = jnp.concatenate([send, small])
        return send, held, small
    at = links.at(name)

    def kernel(mask_ref, held_ref, got_ref, *rest):
        choose = either(mask_ref, at, width)
        if extra:
            small_in, send_ref, keep_out, small_ref = rest
            small_ref[...] = small_in[...] + got_ref[rows:, :]
            send_ref[half:, :] = small_ref[...]
        else:
            send_ref, keep_out = rest
        first = held_ref[:half, :] + got_ref[:half, :]
        second = held_ref[half:, :] + got_ref[half:rows, :]
        send_ref[:half, :] = choose(first, second)
        keep_out[...] = choose(second, first)

    outs = [shape_of((half + extra, width), BF), shape_of((half, width), BF)]
    smalls = [] if small is None else [small]
    out = kernel_call(
        kernel,
        1,
        [links.masks, held, got, *smalls],
        outs + [like(t) for t in smalls],
        after=after,
        vmem=PASS_MIB,
    )
    return (*out, None)[:3]


def add_whole(held, got, small, after):
    rows, width = held.shape
    extra = 0 if small is None else small.shape[0]
    if not tiled(rows):
        piece = held[:rows] + got[:rows]
        if small is None:
            return piece, None
        small = small + got[rows:]
        return jnp.concatenate([piece, small]), small

    def kernel(held_ref, got_ref, *rest):
        if extra:
            small_in, piece_ref, small_ref = rest
            small_ref[...] = small_in[...] + got_ref[rows:, :]
            piece_ref[rows:, :] = small_ref[...]
        else:
            (piece_ref,) = rest
        piece_ref[:rows, :] = held_ref[...] + got_ref[:rows, :]

    smalls = [] if small is None else [small]
    out = kernel_call(
        kernel,
        1,
        [held, got, *smalls],
        [shape_of((rows + extra, width), BF)] + [like(t) for t in smalls],
        after=after,
        vmem=PASS_MIB,
    )
    return (*out, None)[:2]


def add_apart(held, got, rows, after):
    if not tiled(rows):
        both = held + got
        return both[:rows], both[rows:]

    def kernel(held_ref, got_ref, piece_ref, small_ref):
        piece_ref[...] = held_ref[:rows, :] + got_ref[:rows, :]
        small_ref[...] = held_ref[rows:, :] + got_ref[rows:, :]

    outs = [shape_of((n, held.shape[1]), BF) for n in (rows, held.shape[0] - rows)]
    return kernel_call(kernel, 1, [held, got], outs, after=after, vmem=PASS_MIB)


def add_pairs(pieces, gots, after):
    if not tiled(pieces[0].shape[0]):
        return jnp.stack([a + b for a, b in zip(pieces, gots)])
    many = len(pieces)

    def kernel(*refs):
        for i in range(many):
            refs[-1][i] = refs[i][...] + refs[many + i][...]

    out = shape_of((many, *pieces[0].shape), BF)
    return kernel_call(kernel, 1, [*pieces, *gots], out, after=after, vmem=PASS_MIB)


def join(links, name, piece, got, after):
    rows, width = piece.shape[-2:]
    if not tiled(rows):
        return ordered(links.numbers[name] == 1, piece, got, axis=-2)
    at = links.at(name)

    def kernel(mask_ref, piece_ref, got_ref, out_ref):
        choose = either(mask_ref, at, width)
        for i in [()] if piece.ndim == 2 else [(i,) for i in range(piece.shape[0])]:
            mine, other = piece_ref[i], got_ref[i]
            out_ref[(*i, slice(0, rows), slice(None))] = choose(other, mine)
            out_ref[(*i, slice(rows, 2 * rows), slice(None))] = choose(mine, other)

    out = shape_of((*piece.shape[:-2], 2 * rows, width), BF)
    return kernel_call(kernel, 1, [links.masks, piece, got], out, after=after, vmem=PASS_MIB)


class Sum:
    def __init__(self, links, relative, halves, small=None, whole=1):
        self.links, self.relative, self.small = links, relative, small
        self.halves = halves
        self.adding = links.steps
        self.whole = whole
        self.passing = list(self.way_back(links.steps[:-whole]))
        self.held = self.piece = self.flying = None
        self.place = 0

    def way_back(self, steps):
        links = self.links
        for step in reversed(steps):
            crosses = [mask in links.seg for mask in step]
            if self.relative and crosses[0]:
                if not crosses[1]:
                    yield (links.y, links.y)
            elif not (self.relative and crosses[1]):
                yield step

    def advance(self, after=()):
        links, index = self.links, self.place
        self.place += 1
        last = len(self.adding) - 1
        if index == 0:
            send, self.held = self.halves
        elif index <= last - self.whole:
            name = self.adding[index]
            name = ("own", name) if self.relative else name
            send, self.held, self.small = add_halves(links, name, self.held, self.flying, self.small, after)
        elif index == last - self.whole + 1:
            send, self.small = add_whole(self.held, self.flying, self.small, after)
            self.held = send
        elif index <= last:
            send, _ = add_whole(self.held, self.flying, None, after)
            self.held = send
        elif index == last + 1:
            rows = self.held.shape[0] - (0 if self.small is None else self.small.shape[0])
            if self.small is None:
                self.piece, _ = add_whole(self.held, self.flying, None, after)
            else:
                self.piece, self.small = add_apart(self.held, self.flying, rows, after)
            send = self.piece
        else:
            send = self.piece = join(links, self.passing[index - last - 2], self.piece, self.flying, after)
        step = self.adding[index] if index <= last else self.passing[index - last - 1]
        self.flying = links.swap(send, *step)
        return [send]

    def left(self):
        return len(self.adding) + len(self.passing) - self.place

    def finish(self, after=()):
        while self.left():
            self.advance(after)
        return self.piece, self.flying


class Merged:
    def __init__(self, links, sums):
        self.links, self.sums = links, sums
        self.passing = sums[0].passing
        self.place = 0

    def advance(self, after=()):
        index = self.place
        self.place += 1
        if index == 0:
            for s in self.sums:
                while s.place < len(s.adding):
                    s.advance(after)
            self.piece = add_pairs([s.held for s in self.sums], [s.flying for s in self.sums], after)
            if len(self.sums) == 1:
                self.piece = self.piece.reshape(self.piece.shape[1:])
        else:
            self.piece = join(self.links, self.passing[index - 1], self.piece, self.flying, after)
        self.flying = self.links.swap(self.piece, *self.passing[index])
        return [self.piece]

    def left(self):
        return len(self.passing) - self.place

    def finish(self, after=()):
        while self.left():
            self.advance(after)
        return self.piece, self.flying


class Gather:
    def __init__(self, links, up, up_bias, down):
        self.links = links
        width, hidden = up.shape
        self.width, self.hidden = width, hidden
        self.wide = hidden // width
        cut, deep, wide = width // 8, hidden // 8, self.wide
        rows = wide * cut + deep + 16
        y, z = links.y, links.z[0]
        self.near = [(z, y), (y, z)]
        places = [links.at(name) for name in ("core", (y, z), (z, y))]
        self.sent = None

        def kernel(table_ref, bias_ref, up_ref, down_ref, *refs):
            outs, (up_cuts, down_cuts, sems) = refs[:2], refs[2:]
            place = sum(table_ref[at] * weight for at, weight in zip(places, (4, 2, 1)))
            copies = []
            for i, eighth in enumerate((place, place ^ 3)):
                for j, (ref, size, cuts) in enumerate(((up_ref, cut, up_cuts), (down_ref, deep, down_cuts))):
                    from_rows = ref.at[tile_rows(eighth * size, size), :]
                    copies.append(pltpu.make_async_copy(from_rows, cuts.at[i], sems.at[2 * i + j]))
            for copy in copies:
                copy.start()
            lines, rest = [], flat_line(bias_ref)
            for _ in range(3):
                term = rest.astype(BF).astype(F32)
                lines += [term[:, i * width : (i + 1) * width] for i in range(wide)]
                rest = rest - term
            lines.append(jnp.zeros((16 - len(lines), width), F32))
            for out_ref in outs:
                out_ref[rows - 16 :, :] = jnp.concatenate(lines).astype(BF)
            for copy in copies:
                copy.wait()
            for i, out_ref in enumerate(outs):
                for j in range(wide):
                    out_ref[j * cut : (j + 1) * cut, :] = up_cuts[i, :, j * width : (j + 1) * width]
                out_ref[wide * cut : wide * cut + deep, :] = down_cuts[i]

        near, anywhere = pl.BlockSpec(memory_space=pltpu.VMEM), pl.BlockSpec(memory_space=pl.ANY)
        self.mine = pl.pallas_call(
            kernel,
            in_specs=[pl.BlockSpec(memory_space=pltpu.SMEM), near, anywhere, anywhere],
            out_specs=[near, near],
            out_shape=[pltpu.VMEM((rows, width), BF)] * 2,
            scratch_shapes=[
                pltpu.VMEM((2, cut, hidden), BF),
                pltpu.VMEM((2, deep, width), BF),
                pltpu.SemaphoreType.DMA((4,)),
            ],
            compiler_params=pltpu.CompilerParams(vmem_limit_bytes=6 * 2**20),
        )(links.table, up_bias, *(pltpu.with_memory_space_constraint(t, pltpu.HBM) for t in (up, down)))

    def advance(self, after=()):
        links = self.links
        if self.sent is None:
            seg = links.seg[0]
            self.first, self.last = (links.swap(t, seg, seg) for t in self.mine)
            self.sent = list(self.mine)
        elif len(self.sent) == 2:
            self.between = [links.swap(self.first, *masks) for masks in self.near]
            self.sent = [self.first]
        else:
            eighths = [self.first, *self.between, self.last]
            rows, width = self.first.shape

            def kernel(*refs):
                for i, ref in enumerate(refs[:4]):
                    refs[4][i * rows : (i + 1) * rows, :] = ref[...]

            self.piece = kernel_call(
                kernel, 1, eighths, shape_of((4 * rows, width), BF), after=after, vmem=PASS_MIB
            )
            self.flying = links.swap(self.piece, links.core, links.core)
            self.sent = [self.piece]
        return self.sent

    def finish(self, after=()):
        links, width, hidden, wide = self.links, self.width, self.hidden, self.wide
        cut, deep = width // 8, hidden // 8
        rows = wide * cut + deep + 16
        y, z = links.y, links.z[0]
        at_core, at_first, at_second = (links.at(name) for name in ("core", (y, z), (z, y)))

        def kernel(table_ref, piece_ref, got_ref, up_ref, bias_ref, down_ref):
            core, first, second = table_ref[at_core], table_ref[at_first], table_ref[at_second]
            for ref, start in (
                (piece_ref, core * 4 + first * 2 + second),
                (got_ref, (1 - core) * 4 + second * 2 + first),
            ):
                for i in range(4):
                    place = start ^ i
                    at = tile_rows(place * cut, cut)
                    for j in range(wide):
                        from_row = i * rows + j * cut
                        up_ref[at, j * width : (j + 1) * width] = ref[from_row : from_row + cut, :]
                    from_row = i * rows + wide * cut
                    down_ref[tile_rows(place * deep, deep), :] = ref[from_row : from_row + deep, :]
            lines = piece_ref[rows - 16 : rows, :].astype(F32)
            parts = [sum(lines[i * wide + j : i * wide + j + 1] for i in range(3)) for j in range(wide)]
            bias_ref[...] = jnp.concatenate(parts, 1).reshape(hidden)

        return kernel_call(
            kernel,
            2,
            [links.table, self.piece, self.flying],
            [shape_of((width, hidden), BF), shape_of((hidden,), F32), shape_of((hidden, width), BF)],
            scalars=1,
            after=after,
            vmem=10,
        )


class GatherAny:
    def __init__(self, *args):
        self.args = args

    def advance(self, after=()):
        return []

    def finish(self, after=()):
        return other_shards(*self.args)


def other_shards(links, up, up_bias, down):
    shards = links.shards
    hidden = down.shape[0]
    ups = lax.all_gather(up, "seg", axis=0)
    downs = lax.all_gather(down, "seg", axis=0)
    biases = lax.all_gather(up_bias.reshape(1, -1), "seg", axis=0)
    order = lax.axis_index("seg") ^ jnp.arange(1, shards)
    ups = jnp.moveaxis(jnp.take(ups, order, axis=0), 0, 1).reshape(up.shape[0], -1)
    return ups, jnp.take(biases, order, axis=0).reshape(-1), jnp.take(downs, order, axis=0).reshape(-1, down.shape[1])


def pack_small(links, vec_ffn, vec_attn, g_lines, bias_send, bias_keep, send):
    width = vec_ffn.shape[1]
    shards = links.shards
    if shards != 2 or bias_send.shape[1] != 2 * width or not tiled(send.shape[0]):
        halves = ordered(links.numbers["core"] == 1, bias_keep, bias_send).reshape(2, shards, -1)
        by_shard = jnp.moveaxis(halves, 0, 1).reshape(shards, -1)
        by_shard = jnp.take(by_shard, jnp.arange(shards) ^ lax.axis_index("seg"), axis=0).reshape(-1, width)
        lines = [
            in_lanes([g[:, i * 3 * PAIR : (i + 1) * 3 * PAIR] for g in g_lines for i in range(2)], i) for i in (0, 2)
        ]
        small = jnp.concatenate([vec_ffn[:3], vec_attn[:3], *lines, by_shard])
        pad = -(-small.shape[0] // 16) * 16 - small.shape[0]
        small = jnp.pad(small, ((0, pad), (0, 0))).astype(BF)
        return jnp.concatenate([send, small]), small
    at_core, at_seg = links.at("core"), links.at("seg")
    rows = send.shape[0]

    def kernel(table_ref, send_ref, ffn_ref, attn_ref, *rest):
        line_refs, (bias_send_ref, bias_keep_ref, out_ref, small_ref, rows_ref) = rest[:-5], rest[-5:]
        rows_ref[...] = jnp.zeros_like(rows_ref)
        rows_ref[0:3, :] = ffn_ref[0:3, :]
        rows_ref[3:6, :] = attn_ref[0:3, :]
        for g, line_ref in enumerate(line_refs):
            for i in range(2):
                for row, part in ((6, 0), (7, 2)):
                    at = (3 * i + part) * PAIR
                    place = (2 * g + i) * PAIR
                    rows_ref[row : row + 1, place : place + PAIR] = line_ref[:, at : at + PAIR]
        for ref, half in ((bias_send_ref, 1 - table_ref[at_core]), (bias_keep_ref, table_ref[at_core])):
            for i in range(2):
                row = 8 + 2 * (table_ref[at_seg] ^ i) + half
                rows_ref[pl.ds(row, 1), :] = ref[:, i * width : (i + 1) * width]
        small_ref[...] = rows_ref[...].astype(BF)
        out_ref[:rows, :] = send_ref[...]
        out_ref[rows:, :] = small_ref[...]

    return kernel_call(
        kernel,
        1,
        [links.table, send, vec_ffn, vec_attn, *g_lines, bias_send, bias_keep],
        [shape_of((rows + 16, width), BF), shape_of((16, width), BF)],
        scalars=1,
        scratch_shapes=[pltpu.VMEM((16, width), F32)],
        vmem=PASS_MIB,
    )


def ffn_output(links, pair, turned, after):
    rows, width = pair[0].shape
    if rows % PAIR:
        array = ordered(links.numbers["core"] == 1, *pair).astype(F32)
        return [array.T if turned else array]
    at_core = links.at("core")
    halves = [slice(0, rows), slice(rows, 2 * rows)]
    parts = [(slice(None), h) if turned else (h,) for h in halves]

    def kernel(leave, mask_ref, mine_ref, other_ref, out_ref):
        choose = either(mask_ref, at_core, width)
        for i, order in enumerate(((other_ref, mine_ref), (mine_ref, other_ref))):
            values = choose(order[0][...], order[1][...]).astype(F32)
            out_ref[parts[i]] = values.T if turned else values
            leave(i)

    shape = (width, 2 * rows) if turned else (2 * rows, width)
    return leaving_call(kernel, 9, [links.masks, *pair], shape_of(shape, F32), parts, after, 10)


def square_outputs(links, first, groups, begin, before, small, hidden, after):
    given = [t for pair in [*first, *groups] for t in pair]
    width = given[0].shape[1]
    wide = 2 * PAIR
    at_core, at_seg = links.at("core"), links.at("seg")
    lines = hidden // width
    many = len(first) + len(groups)
    smalls = [] if small is None else [small]

    def kernel(mask_ref, *refs):
        refs = list(refs)
        pairs = [refs[2 * i : 2 * i + 2] for i in range(many)]
        small_refs = refs[2 * many : 2 * many + len(smalls)]
        refs = refs[2 * many + len(smalls) + len(before) + len(after) :]
        *outs, sems = refs
        token = outs.pop(len(outs) - 3 * many - len(first) - 1)
        token[...] = jnp.zeros_like(token)
        outs, scratch = outs[: len(outs) - 3 * many - len(first)], outs[len(outs) - 3 * many - len(first) :]
        choose = either(mask_ref, at_core, width)
        copies = []

        def leave(values, out, lanes):
            buffer = scratch[len(copies)]
            buffer[...] = values
            copy = pltpu.make_async_copy(buffer, out.at[:, lanes], sems.at[len(copies)])
            copy.start()
            copies.append(copy)

        for number, (mine, other) in enumerate(pairs):
            group = number + begin
            if first and number == 0:
                leave(choose(other[...], mine[...]).astype(F32), outs[3], slice(0, width))
                values = choose(mine[...], other[...])
            else:
                values = jnp.concatenate([choose(other[...], mine[...]), choose(mine[...], other[...])])
            for i in range(3):
                parts = [values[:, (3 * j + i) * PAIR : (3 * j + i + 1) * PAIR] for j in range(2)]
                leave(jnp.concatenate(parts, 1).astype(F32), outs[i], slice(group * wide, (group + 1) * wide))
        if small_refs:
            vector_outs, bias_out = outs[3:11], outs[11]
            rows = small_refs[0][...].astype(F32)
            for i, out_ref in enumerate(vector_outs):
                out_ref[...] = rows[i : i + 1].reshape(width)
            by_shard = [
                jnp.concatenate([rows[8 + n * lines + i : 9 + n * lines + i] for i in range(lines)], 1)
                for n in range(2)
            ]
            bias_out[...] = either(mask_ref, at_seg, hidden)(by_shard[1], by_shard[0]).reshape(hidden)
        for copy in copies:
            copy.wait()

    square, vector = pltpu.HBM((width, width), F32), shape_of((width,), F32)
    anywhere, near = pl.BlockSpec(memory_space=pl.ANY), pl.BlockSpec(memory_space=pltpu.VMEM)
    far = pl.BlockSpec(memory_space=pltpu.HBM)
    outs, out_specs = [square] * 3, [far] * 3
    if first:
        outs, out_specs = outs + [square], out_specs + [far]
    if smalls:
        outs, out_specs = outs + [vector] * 8 + [shape_of((hidden,), F32)], out_specs + [near] * 9
    outs, out_specs = outs + [TOKEN], out_specs + [near]
    scratch = []
    for number in range(many):
        if first and number == 0:
            scratch.append(pltpu.VMEM((width, width), F32))
        scratch += [pltpu.VMEM((width, wide), F32)] * 3
    operands = [links.masks, *given, *smalls]
    return pl.pallas_call(
        kernel,
        in_specs=[near] * len(operands) + [far] * len(before) + [anywhere] * len(after),
        out_specs=out_specs,
        out_shape=outs,
        scratch_shapes=scratch + [pltpu.SemaphoreType.DMA((len(scratch),))],
        input_output_aliases={len(operands) + i: i for i in range(len(before))},
        compiler_params=pltpu.CompilerParams(vmem_limit_bytes=16 * 2**20),
        cost_estimate=pl.CostEstimate(flops=9 * 10**9, bytes_accessed=1 << 20, transcendentals=0),
    )(*operands, *before, *after)


def attention_outputs_any(links, first, groups, small, hidden):
    on_core1 = links.numbers["core"] == 1
    whole = [ordered(on_core1, *pair) for pair in (first, *groups)]
    width = whole[0].shape[1]
    grads = [whole[0][width:], *whole[1:]]
    pairs = [g[:, i * 3 * PAIR : (i + 1) * 3 * PAIR] for g in grads for i in range(2)]
    small = small.astype(F32)
    biases = small[8 : 8 + hidden * links.shards // width].reshape(links.shards, -1)
    bias = lax.dynamic_index_in_dim(biases, lax.axis_index("seg"), keepdims=False)
    squares = [in_lanes(pairs, i).astype(F32) for i in range(3)]
    return [whole[0][:width].astype(F32), *squares, *[small[i] for i in range(8)], bias]


def in_halves(array, axis, shards):
    shape = list(array.shape)
    parts = array.reshape(shape[:axis] + [shards, 2, -1] + shape[axis + 1 :])
    return jnp.moveaxis(parts, axis + 1, axis).reshape(shape)


def body(
    activations,
    tok_count,
    w_query,
    w_key,
    w_value,
    w_proj,
    b_query,
    b_value,
    b_proj,
    gain_attn,
    shift_attn,
    w_up,
    b_up,
    w_down,
    b_down,
    gain_ffn,
    shift_ffn,
    cotangent,
    items,
    shards,
):
    slots, rows, width = activations.shape
    links = Links(items, shards)
    count = tok_count[:, 0]
    more = ((0, 0), (0, -rows % 16), (0, 0))
    x, cot = jnp.pad(activations, more), jnp.pad(cotangent, more)
    own = (w_up, b_up, w_down)
    hidden = w_up.shape[1]
    every = hidden * shards
    weights = (Gather if shards == 2 and links.z else GatherAny)(links, *own)

    state, done = [], [cot]
    for slot in range(slots):
        weights_in = [w_query, w_key, w_value]
        after = weights.advance(done) + done
        state.append(attend(rows, slot, count, x, weights_in, [b_query, b_value], after))
        done = [state[-1][-1]]
    q, extra, k, v, ctx, bias = zip(*state)
    normed, xhat, rstd = first_norm(x, w_proj, [b_proj, gain_attn, shift_attn], ctx, done)
    done = [rstd[-1]]
    act0, slope0, first = ffn_first(normed, own, weights.advance(done) + done)
    others = weights.finish([first])
    act1, slope1, layer_out, g_sum, g_branch, vec_ffn = ffn_last(
        rows, count, normed, others, first, cot, [b_down, gain_ffn, shift_ffn]
    )
    acts, slopes = [act0, act1], [slope0, slope1]
    if shards == 2:
        pieces = [own[2], own[0], others[2], others[0]]
    else:
        acts, slopes = ([in_halves(jnp.concatenate(t, 1), 1, shards)] * 2 for t in (acts, slopes))
        ups = in_halves(jnp.concatenate([own[0], others[0]], 1), 1, shards)
        downs = in_halves(jnp.concatenate([own[2], others[2]]), 0, shards)
        pieces = [downs, ups, downs, ups]

    done = [vec_ffn]
    made, sums = {}, {}
    d_parts, g_lines, small = [], [], None
    arrays = [q, extra, k, v, ctx]
    count_pairs = width // PAIR
    whole_tiles = shards == 2 and tiled(width >> (len(links.steps) - 1))

    def step(name):
        nonlocal done
        sent = sums[name].advance(done)
        done = sent if sums[name].place > 1 else done + sent

    def run(name):
        nonlocal done, small
        if name == "down send":
            made["down"] = [down_grad(links, 1, acts, g_branch, every, done)]
            done = made["down"]
        elif name == "down keep":
            made["down"].append(down_grad(links, 0, acts, g_branch, every, done))
            sums["down"] = Sum(links, True, made["down"])
            done = made["down"][1:]
        elif name == "up send":
            *made["up send"], made["g_norm"] = up_grad(links, 1, g_branch, normed, slopes, pieces, every, [], done)
            done = [made["g_norm"]]
        elif name == "up keep":
            *made["up keep"], made["g_norm"] = up_grad(
                links, 0, g_branch, normed, slopes, pieces, every, [made["g_norm"]], done
            )
            sums["up"] = Sum(links, True, (made["up send"][0], made["up keep"][0]))
            done = [made["g_norm"]]
        elif name == "proj":
            made["g_pre"], made["g_ctx"], made["g_proj"], made["vec"] = proj_grad(
                g_sum, made["g_norm"], w_proj, gain_attn, xhat, rstd, ctx, done
            )
            done = [made["vec"]]
        elif name == "pair":
            pair = len(d_parts)
            before = None if pair % 2 == 0 else d_parts[-1]
            beside = [made["g_proj"]] if pair == 1 else []
            d, *rest = attend_back(links, pair, made["g_ctx"], arrays, bias, x, before, beside, done)
            d_parts.append(d)
            done = [d]
            if rest:
                send, keep, lines = rest
                g_lines.append(lines)
                if pair == count_pairs - 1:
                    hidden_bias = [made[n][1] for n in ("up send", "up keep")]
                    send, small = pack_small(links, vec_ffn, made["vec"], g_lines, *hidden_bias, send)
                    done = [small]
                wide = 2 if pair // 2 in WIDE and len(links.z) > 1 else 1
                sums["heads %d" % (pair // 2)] = Sum(links, False, (send, keep), small, wide)
        elif name == "input":
            made["input"], *done = input_grad(
                rows, made["g_pre"], d_parts, [w_query, w_key, w_value], done
            )
        elif name == "layer":
            made["layer"], *done = slots_last(layer_out, rows, done)
        elif name in ("down out", "up out"):
            pair = sums[name[:-3] + "back"].finish()
            made[name], *done = ffn_output(links, pair, name == "up out", done)
        elif name == "squares":
            if whole_tiles:
                pairs = [sums["heads %d" % i].finish() for i in range(count_pairs // 2 - 1)]
                *made["squares"], token = square_outputs(links, pairs[:1], pairs[1:], 0, [], None, hidden, done)
                done = [token]
        elif name in ("down back", "up back") and name not in sums:
            sums[name] = Merged(links, [sums[name[:-5]]])
            step(name)
        elif sums[name].left():
            step(name)

    for name in PLAN:
        run(name)
    for name in ("down back", "up back"):
        if name not in sums:
            run(name)
    while any(s.left() for s in sums.values()):
        for s in sums.values():
            if s.left():
                s.advance([])
    for name in ("down out", "up out", "squares", "layer"):
        if name not in made:
            run(name)
    grad_w_down, grad_w_up = made["down out"], made["up out"]
    layer_out, grad_input = (jnp.transpose(t, (1, 0, 2)) for t in (made["layer"], made["input"]))
    last = sums["heads %d" % (count_pairs // 2 - 1)]
    if whole_tiles:
        *squares, g_proj = made["squares"]
        g_query, g_key, g_value, *vectors, grad_b_up, _ = square_outputs(
            links, [], [last.finish()], count_pairs // 2 - 1, squares, last.small, hidden, []
        )
    else:
        pairs = [sums["heads %d" % i].finish() for i in range(count_pairs // 2)]
        g_proj, g_query, g_key, g_value, *vectors, grad_b_up = attention_outputs_any(
            links, pairs[0], pairs[1:], last.small, hidden
        )
    g_gain_ffn, g_shift_ffn, g_b_down, g_gain_attn, g_shift_attn, g_b_proj, g_b_query, g_b_value = vectors
    return (
        layer_out,
        grad_input,
        g_query,
        g_key,
        g_value,
        g_proj,
        g_b_query,
        g_b_value,
        g_b_proj,
        g_gain_attn,
        g_shift_attn,
        grad_w_up,
        grad_b_up,
        grad_w_down,
        g_b_down,
        g_gain_ffn,
        g_shift_ffn,
    )


def solution(mesh):
    rows, everywhere = P("dp", "seg", None), P()
    return jax.shard_map(
        functools.partial(body, items=mesh.shape["dp"], shards=mesh.shape["seg"]),
        mesh=mesh,
        in_specs=(rows, P("dp", "seg"))
        + (everywhere,) * 9
        + (P(None, "seg"), P("seg"), P("seg", None))
        + (everywhere,) * 3
        + (rows,),
        out_specs=(rows, rows)
        + (everywhere,) * 9
        + (P(None, "seg"), P("seg"), P("seg", None))
        + (everywhere,) * 3,
        check_vma=False,
    )
```
